512 devices in a mesh: gx: 8 (over y_lo, x), gy: 16 (over z, core), col: 4 (over y_hi).
Axes of the slice: x: 4, y: 8 (y_hi: 4, y_lo: 2; y = y_hi * 2 + y_lo), z: 8, core: 2. Of those that a mesh axis runs over, the one named last changes fastest.
Arguments:
- permeability: float32 [64, 128, 512], P('gx', 'gy', 'col'), may hold values from 0.1 to 10
- source: float32 [64, 128, 512], P('gx', 'gy', 'col'), may hold values from -2400 to 2400
- ownership: int32 [64, 128, 512], P('gx', 'gy', 'col'), may hold values from 0 to 63, as said below
- assignment: int32 [8, 16, 4, 64], P('gx', 'gy', 'col'), may hold values from 0 to 1023, as said below
- layer_flags: int32 [512], replicated, may hold values 0 or 1
Outputs:
- pressure: float32 [64, 128, 512], P('gx', 'gy', 'col')
- coarse_pressure: float32 [8, 1024], P('gx', ('gy', 'col'))
The draws below stay inside these ranges and needn't reach their ends.
Inputs may be any that keep to these rules, and one draw needn't show every extreme that they name: `ownership`: every brick of 8 x 8 x 128 cells holds cells of every subdomain. `assignment`: in every slab every coarse cell is named by some subdomain; coarse cells hold unequal numbers of subdomains.
All inputs are finite; a program needn't handle non-finite values.
Results may differ from the reference program's by a relative error of at most 0.00013.
Values sent between devices are 32-bit elements; how exact they have to be, the bound alone decides.
No kernel may reach another device: no remote copies, remote signals or barrier semaphores. Data moves between devices by JAX's collectives and lax.ppermute only.
A program may use at most 64 MiB of HBM per device.

```python
import math
import jax
import jax.numpy as jnp

CX = 8
CY = 8
CZ = 128
NSUB = 64
SWEEPS = 4
NX = 64
NY = 128
NZ = 512
NCS = 1024
N_GX = 8
N_GY = 16
N_COL = 4


def draw_ownership(key, part):
    key = jax.random.fold_in(key, 11)
    key_move, key_other = jax.random.split(key)
    local_x = (jnp.arange(NX) % CX)[:, None, None]
    local_y = (jnp.arange(NY) % CY)[None, :, None]
    local_z = (jnp.arange(NZ) % CZ)[None, None, :]
    tile_index = local_x * 4 // CX * 16 + local_y * 4 // CY * 4 + local_z * 4 // CZ
    moved = (jax.random.randint(key_move, (NX, NY, NZ), 0, 4) == 0) & (local_z % 4 != 0)
    other = jax.random.randint(key_other, (NX, NY, NZ), 0, NSUB)
    return jnp.where(moved, other, tile_index).astype(jnp.int32)


def draw_assignment(key, part):
    key = jax.random.fold_in(key, 23)
    count = N_GY * N_COL * NSUB

    def slab_draw(slab_key):
        key_order, key_first, key_second = jax.random.split(slab_key, 3)
        order = jax.random.permutation(key_order, count)
        ranks = jnp.argsort(order)
        skewed = jnp.minimum(jax.random.randint(key_first, (count,), 0, NCS), jax.random.randint(key_second, (count,), 0, NCS))
        return jnp.where(ranks < NCS, ranks, skewed)
    labels = jax.vmap(slab_draw)(jax.random.split(key, N_GX))
    return labels.reshape(N_GX, N_GY, N_COL, NSUB).astype(jnp.int32)


def set_ends(result, own_key, least, top_value):
    longest = result.shape.index(max(result.shape))
    spots = []
    for shift in (0, 1):
        where = [jax.random.randint(jax.random.fold_in(own_key, axis), (), 0, length) for axis, length in enumerate(result.shape)]
        where[longest] = (where[longest] + shift) % result.shape[longest]
        spots.append(tuple(where))
    return result.at[spots[0]].set(least).at[spots[1]].set(top_value)


def level_of(key, extent, pieces, smallest, largest):
    factor_of, own = 1.0, jax.random.fold_in(key, 6)
    for dim, shards_of in pieces:
        draws = jnp.exp(jax.random.uniform(jax.random.fold_in(own, dim), (shards_of,), jnp.float32, smallest / len(pieces), largest / len(pieces)))
        factor_of = factor_of * jnp.repeat(draws, extent[dim] // shards_of).reshape([-1 if axis == dim else 1 for axis in range(len(extent))])
    return factor_of


def noise(own_key, dims, spread, reach, cuts=(), dtype=jnp.bfloat16):
    array = jax.random.normal(own_key, dims, jnp.float32) * spread
    if len(cuts) > 0:
        array = level_of(own_key, dims, cuts, -0.22, 0.18) * array
    return jnp.clip(array, min=-reach, max=reach).astype(dtype)


def setup_inputs(seed: int = 0) -> dict:
    splits = jax.random.split(jax.random.key(seed), 6)
    permeability = jnp.clip(jnp.exp(math.log(10.0) - 4.6051702 * jax.random.uniform(splits[0], (NX, NY, NZ), jnp.float32) ** level_of(splits[0], (NX, NY, NZ), ((0, 8), (1, 16), (2, 4)), -0.2, 0.2)), 0.1, 10.0)
    source = noise(splits[1], (NX, NY, NZ), 300.0, 2400.0, ((0, 8), (1, 16), (2, 4)), jnp.float32)
    ownership = draw_ownership(jax.random.fold_in(splits[5], 71), 0)
    assignment = draw_assignment(jax.random.fold_in(splits[5], 71), 0)
    layer_flags = set_ends((jax.random.randint(splits[4], (NZ,), 0, 2) < 1).astype(jnp.int32), jax.random.fold_in(splits[4], 1), 0, 1)
    return dict(permeability=permeability, source=source, ownership=ownership, assignment=assignment, layer_flags=layer_flags)


fine_relax = 0.6666667
coarse_relax = 0.7


def harmonic(lower_value, upper_value):
    return 2.0 * lower_value * upper_value / (lower_value + upper_value)


def face_terms(permeability, layer_flags):
    inner_x = harmonic(permeability[:-1], permeability[1:])
    plus_x = jnp.concatenate([inner_x, permeability[-1:]], axis=0)
    minus_x = jnp.concatenate([permeability[:1], inner_x], axis=0)
    plus_y = harmonic(permeability, jnp.roll(permeability, -1, axis=1))
    edge_rows = (jnp.arange(NY) == NY - 1)[None, :, None]
    flag_values = layer_flags.astype(jnp.float32)[None, None, :]
    plus_y = jnp.where(edge_rows, plus_y * flag_values, plus_y)
    minus_y = jnp.roll(plus_y, 1, axis=1)
    inner_z = harmonic(permeability[:, :, :-1], permeability[:, :, 1:])
    closed = jnp.zeros((NX, NY, 1), jnp.float32)
    plus_z = jnp.concatenate([inner_z, closed], axis=2)
    minus_z = jnp.concatenate([closed, inner_z], axis=2)
    diagonal = plus_x + minus_x + plus_y + minus_y + plus_z + minus_z
    return plus_x, minus_x, plus_y, minus_y, plus_z, minus_z, diagonal


def operator_apply(values, terms):
    plus_x, minus_x, plus_y, minus_y, plus_z, minus_z, diagonal = terms
    padded = jnp.pad(values, ((1, 1), (0, 0), (1, 1)))
    return diagonal * values - (plus_x * padded[2:, :, 1:-1] + minus_x * padded[:-2, :, 1:-1]
                                + plus_y * jnp.roll(values, -1, axis=1) + minus_y * jnp.roll(values, 1, axis=1)
                                + plus_z * padded[1:-1, :, 2:] + minus_z * padded[1:-1, :, :-2])


def coarse_labels(ownership, assignment):
    slab = (jnp.arange(NX) // CX).astype(jnp.int32)[:, None, None]
    row_block = (jnp.arange(NY) // CY).astype(jnp.int32)[None, :, None]
    layer_block = (jnp.arange(NZ) // CZ).astype(jnp.int32)[None, None, :]
    labels = assignment[slab, row_block, layer_block, ownership].astype(jnp.int32)
    return (slab * NCS + labels).astype(jnp.int32)


def aggregate(field, labels):
    sums = jax.ops.segment_sum(field.reshape(-1), labels.reshape(-1), num_segments=N_GX * NCS)
    return sums.reshape(N_GX, NCS)


def expand(coarse, labels):
    return coarse.reshape(-1)[labels]


def reference(permeability, source, ownership, assignment, layer_flags):
    terms = face_terms(permeability, layer_flags)
    diagonal = terms[6]
    labels = coarse_labels(ownership, assignment)

    def restrict_sweeps(field):
        for sweep_turn in range(SWEEPS):
            field = field - fine_relax * operator_apply(field / diagonal, terms)
        return field

    def prolong_sweeps(field):
        for sweep_turn in range(SWEEPS):
            field = field - fine_relax * operator_apply(field, terms) / diagonal
        return field

    coarse_rhs = aggregate(restrict_sweeps(source), labels)
    coarse_diag = aggregate(diagonal, labels)
    first_guess = coarse_relax * coarse_rhs / coarse_diag
    image_field = restrict_sweeps(operator_apply(prolong_sweeps(expand(first_guess, labels)), terms))
    second_guess = first_guess + coarse_relax * (coarse_rhs - aggregate(image_field, labels)) / coarse_diag
    pressure = prolong_sweeps(expand(second_guess, labels))
    return pressure, second_guess
```

```python
import functools

import jax
import jax.numpy as jnp
from jax import lax
from jax.experimental import pallas as pl
from jax.experimental.pallas import tpu as pltpu
from jax.sharding import PartitionSpec as P

f32 = jnp.float32
i32 = jnp.int32
bf16 = jnp.bfloat16
NSUB = 64
B = 8
LZ = 128
NP = 3 * B
W = 9
fine_relax = 0.6666667
coarse_relax = 0.7
VMEM_LIMIT = 48 * 1024 * 1024

PERM, OWN, HZ, ASG, SRC = 0, 8, 16, 24, 25
STACK = 33
BASE = (0, 29, 62)
LINE = 91


def lanes(shape):
    return lax.broadcasted_iota(i32, shape, len(shape) - 1)


def rows(shape):
    return lax.broadcasted_iota(i32, shape, len(shape) - 2)


def call(kernel, outs, scratch=(), n_vmem=0, smem_first=False):
    specs = [pl.BlockSpec(memory_space=pltpu.VMEM)] * n_vmem
    if smem_first:
        specs = [pl.BlockSpec(memory_space=pltpu.SMEM)] + specs
    single = not isinstance(outs, (list, tuple))
    vm = pl.BlockSpec(memory_space=pltpu.VMEM)
    return pl.pallas_call(
        kernel,
        out_shape=outs,
        in_specs=specs,
        out_specs=vm if single else [vm] * len(outs),
        scratch_shapes=list(scratch),
        compiler_params=pltpu.CompilerParams(vmem_limit_bytes=VMEM_LIMIT),
    )


def sds(*shape, dtype=f32):
    return jax.ShapeDtypeStruct(shape, dtype)


def z_messages(perm, src, own, asg, mr, ml, xa, xb, ya, yb):
    lane = lanes((B, LZ))
    tile = jnp.concatenate([asg[...].astype(f32), jnp.zeros((1, LZ - NSUB), f32)], axis=1)
    tile = jnp.where(rows((B, LZ)) == 0, jnp.broadcast_to(tile, (B, LZ)), 0.0)
    for p in range(B):
        k, s, o = perm[p], src[p], own[p].astype(f32)
        mr[p] = jnp.where(
            lane < 16, k, jnp.where(lane < 32, pltpu.roll(o, 16, 1), pltpu.roll(s, 32, 1))
        )
        ml[p] = jnp.where(
            lane >= 112, k, jnp.where(lane >= 96, pltpu.roll(o, 112, 1), pltpu.roll(s, 96, 1))
        )
    for out in (mr, ml):
        out[B] = tile
    for out, at in ((xa, B - 1), (xb, 0)):
        out[0] = perm[at]
        out[1] = own[at].astype(f32)
        out[2] = tile
    for out, at in ((ya, B - 1), (yb, 0)):
        out[0] = perm[:, at, :]
        out[1] = own[:, at, :].astype(f32)
        out[2] = tile


def stack_up(perm, src, own, mr, ml, asg, stack):
    lane = lanes((B, LZ))
    for p in range(B):
        stack[PERM + p] = perm[p]
        stack[OWN + p] = own[p].astype(f32)
        stack[HZ + p] = jnp.where(lane < 64, mr[p], ml[p])
        stack[SRC + p] = src[p]
    tile = jnp.concatenate([asg[...].astype(f32), jnp.zeros((1, LZ - NSUB), f32)], axis=1)
    row = rows((B, LZ))
    stack[ASG] = jnp.where(
        row == 0,
        jnp.broadcast_to(tile, (B, LZ)),
        jnp.where(
            row == 1,
            jnp.broadcast_to(mr[B, 0:1, :], (B, LZ)),
            jnp.where(row == 2, jnp.broadcast_to(ml[B, 0:1, :], (B, LZ)), 0.0),
        ),
    )


def shifted(u):
    return (
        pltpu.roll(u, NP - 1, 0),
        pltpu.roll(u, 1, 0),
        pltpu.roll(u, 2 * LZ - 1, 1),
        pltpu.roll(u, 1, 1),
    )


def around(u_ref, w_ref, p, edge=None):
    u = u_ref[p + 1]
    up, down, right, left = shifted(u)
    if edge is not None:
        up, down = edge(up, down)
    return u, (
        (w_ref[0, p] * u_ref[p + 2] + w_ref[1, p] * u_ref[p])
        + (w_ref[2, p] * up + w_ref[3, p] * down)
        + (w_ref[4, p] * right + w_ref[5, p] * left)
    )


def sweep(src, dst, w_ref, first, last):
    def one(p, carry):
        u, near = around(src, w_ref, p)
        dst[p + 1] = (1.0 - fine_relax) * u + near
        return carry

    lax.fori_loop(first, last + 1, one, 0)


def label_sums(label_tiles, field_sets, sums):
    def one(s, carry):
        hits = [tile == s for tile in label_tiles]
        for k, tiles in enumerate(field_sets):
            parts = [jnp.where(hit, tile, 0.0) for hit, tile in zip(hits, tiles)]
            while len(parts) > 1:
                parts = [a + b for a, b in zip(parts[::2], parts[1::2])]
            sums[pl.ds(k * NSUB + s, 1), :] = jnp.sum(parts[0], axis=0, keepdims=True)
        return carry

    lax.fori_loop(0, NSUB, one, 0, unroll=4)


def lane_sums(sums):
    ones = jnp.ones((B, LZ), f32)
    return lax.dot_general(
        ones, sums, (((1,), (1,)), ((), ())),
        precision=lax.Precision.HIGHEST, preferred_element_type=f32,
    )


def harmonic(a, b):
    return 2.0 * a * b / (a + b)


def first_sums(n_gx, n_gy, n_col, idx, y_lo, y_mid, y_hi, xl, xr, yl, yr, flags,
               weights, labels, chunk, kext, fx, va, vb, fmul, zmul, dvals, sums):
    gx, gy, col = idx[0], idx[1], idx[2]
    lines = (y_lo, y_mid, y_hi)
    lane = lanes((B, LZ))
    halo = (lane < W) | (lane >= LZ - W)
    near_side = lane < 64

    def positive(t):
        return jnp.where(t > 0.0, t, 1.0)

    ones = jnp.ones((NP, 2 * LZ), f32)
    for at, plane in ((0, xl), (NP + 1, xr)):
        kext[at] = ones
        kext[at, B : 2 * B, 0:LZ] = positive(plane[0])

    for b in range(3):

        def fill(q, carry, b=b):
            p = b * B + q
            for ty in range(3):
                line = lines[ty]
                r = slice(ty * B, (ty + 1) * B)
                packed = line[BASE[b] + HZ + q]
                kext[p + 1, r, 0:LZ] = positive(line[BASE[b] + PERM + q])
                kext[p + 1, r, LZ:] = positive(jnp.where(halo, packed, 1.0))
                own = line[BASE[b] + OWN + q]
                labels[p, r, 0:LZ] = own.astype(i32)
                own_z = jnp.where(near_side, pltpu.roll(packed, LZ - 16, 1), pltpu.roll(packed, 16, 1))
                labels[p, r, LZ:] = jnp.where(halo, own_z, 0.0).astype(i32)
            return carry

        lax.fori_loop(0, B, fill, 0)

    flag_row = jnp.concatenate(
        [flags[1:2, :], jnp.where(lane[0:1] < 64, flags[2:3, :], flags[0:1, :])], axis=1
    )
    row_all, lane_all = rows((NP, 2 * LZ)), lanes((NP, 2 * LZ))
    wrap_row = jnp.where(
        gy == 0, B - 1, jnp.where(gy == n_gy - 1, 2 * B - 1, jnp.where(gy == n_gy - 2, NP - 1, -1))
    )
    fmul[...] = jnp.where(row_all == wrap_row, jnp.broadcast_to(flag_row, (NP, 2 * LZ)), 1.0)
    low_flag = jnp.where(gy == 1, flag_row, 1.0)
    closed = ((lane_all == LZ - 1) & (col == n_col - 1)) | ((lane_all == 2 * LZ - 1) & (col == 0))
    zmul[...] = jnp.where(closed, 0.0, 1.0)

    def x_face(p, carry):
        fx[p] = harmonic(kext[p], kext[p + 1])
        return carry

    lax.fori_loop(0, NP + 1, x_face, 0)

    @pl.when(gx == 0)
    def _():
        fx[B] = kext[B + 1]

    @pl.when(gx == n_gx - 1)
    def _():
        fx[2 * B] = kext[2 * B]

    for b in range(3):
        if b == 0:
            inside = jnp.where(gx > 0, 1.0, 0.0)
        elif b == 2:
            inside = jnp.where(gx < n_gx - 1, 1.0, 0.0)
        else:
            inside = 1.0

        def terms(q, carry, b=b, inside=inside):
            p = b * B + q
            k = kext[p + 1]
            k_up = pltpu.roll(k, NP - 1, 0)
            if b == 1:
                one = jnp.ones((1, LZ), f32)
                high = jnp.concatenate([positive(yr[0, pl.ds(q, 1), :]), one], axis=1)
                k_up = jnp.where(row_all == NP - 1, jnp.broadcast_to(high, k.shape), k_up)
            fy_up = harmonic(k, k_up) * fmul[...]
            fy_down = pltpu.roll(fy_up, 1, 0)
            if b == 1:
                low = jnp.concatenate([positive(yl[0, pl.ds(q, 1), :]), one], axis=1)
                edge = harmonic(low, k[0:1]) * low_flag
                fy_down = jnp.where(row_all == 0, jnp.broadcast_to(edge, k.shape), fy_down)
            fz_right = harmonic(k, pltpu.roll(k, 2 * LZ - 1, 1)) * zmul[...]
            fz_left = pltpu.roll(fz_right, 1, 1)
            fx_up, fx_down = fx[p + 1], fx[p]
            diag = fx_up + fx_down + fy_up + fy_down + fz_right + fz_left
            scale = (fine_relax * inside) / diag
            for i, face in enumerate((fx_up, fx_down, fy_up, fy_down, fz_right, fz_left)):
                weights[i, p] = face * scale
            if b == 1:
                dvals[q] = diag[B : 2 * B, 0:LZ]
            if b == 1:
                source_field(p, BASE[1] + SRC + q, diag)
            else:

                @pl.when((q >= 4) if b == 0 else (q < 4))
                def _():
                    source_field(p, (BASE[0] + SRC - 4 if b == 0 else BASE[2] + SRC) + q, diag)

            return carry

        def source_field(p, at, diag, b=b):
            hz = BASE[b] + HZ + (p - b * B)
            for ty in range(3):
                line = lines[ty]
                r = slice(ty * B, (ty + 1) * B)
                packed = line[hz]
                src_z = jnp.where(near_side, pltpu.roll(packed, LZ - 32, 1), pltpu.roll(packed, 32, 1))
                va[p + 1, r, 0:LZ] = line[at] / diag[r, 0:LZ]
                va[p + 1, r, LZ:] = jnp.where(halo, src_z, 0.0) / diag[r, LZ:]

        lax.fori_loop(0, B, terms, 0)

    sweep(va, vb, weights, 5, 18)
    sweep(vb, va, weights, 6, 17)
    sweep(va, vb, weights, 7, 16)
    sweep(vb, va, weights, 8, 15)
    tiles = [va[B + 1 + q, B : 2 * B, 0:LZ] * dvals[q] for q in range(B)]
    diag_tiles = [dvals[q] for q in range(B)]
    label_tiles = [labels[B + q, B : 2 * B, 0:LZ] for q in range(B)]
    label_sums(label_tiles, (tiles, diag_tiles), sums)
    totals = lane_sums(sums[...])
    asg = y_mid[BASE[1] + ASG]
    twice = jnp.where(lane < NSUB, asg, pltpu.roll(asg, NSUB, 1))
    row = rows((B, LZ))
    tile = jnp.where(
        row == 0, totals, jnp.where(row == 1, jnp.broadcast_to(twice[0:1], (B, LZ)), 0.0)
    )
    for d in range(n_gy):
        chunk[d] = tile


def coarse_partial(n_gy, n_out, sets, values, assigned, out):
    sub = rows((B, LZ))
    lane = lanes((B, LZ))
    wide = rows((LZ, LZ))
    total = None
    for g in range(n_gy):
        value = jnp.broadcast_to(values[g, 0:1, :], (B, LZ))
        a = jnp.broadcast_to(assigned[g, 1:2, :], (B, LZ)).astype(i32)
        high = (a >> 7) == sub
        parts = [
            jnp.where(high & ((lane >= NSUB * i) & (lane < NSUB * (i + 1))), value, 0.0)
            for i in range(sets)
        ]
        left = jnp.concatenate(parts, axis=0)
        l1 = left.astype(bf16)
        rest = left - l1.astype(f32)
        l2 = rest.astype(bf16)
        l3 = (rest - l2.astype(f32)).astype(bf16)
        low = jnp.broadcast_to((a & 127)[0:1], (LZ, LZ)) == wide
        right = jnp.where(low, 1.0, 0.0).astype(bf16)
        for part in (l1, l2, l3):
            more = lax.dot_general(
                part, right, (((1,), (1,)), ((), ())), preferred_element_type=f32
            )
            total = more if total is None else total + more
    for d in range(n_out):
        out[d] = total


def lookup(table, index):
    low, high = index & 127, index >> 7
    result = jnp.zeros((B, LZ), f32)
    for h in range(B):
        got = jnp.take_along_axis(jnp.broadcast_to(table[h : h + 1], (B, LZ)), low, axis=1)
        result = jnp.where(high == h, got, result)
    return result


def pick(row, index):
    return jnp.take_along_axis(jnp.broadcast_to(row, (B, LZ)), index, axis=1)


def slab_totals(parts, g, n_gx, n_col):
    exists = (g >= 0) & (g < n_gx)
    at = jnp.clip(g, 0, n_gx - 1) * n_col
    total = parts[at]
    for c in range(1, n_col):
        total = total + parts[at + c]
    return total, exists


def guess(parts, g, n_gx, n_col):
    total, exists = slab_totals(parts, g, n_gx, n_col)
    rhs, diag = total[0:B], total[B : 2 * B]
    return rhs, diag, jnp.where(exists, coarse_relax * rhs / diag, 0.0)


def expand(coarse, lines, labels, u, first, last):
    near_side = lanes((B, LZ)) < 64
    for b in range(3):
        tables = [
            lookup(coarse[b], lines[ty][BASE[b] + ASG].astype(i32)) for ty in range(3)
        ]

        def one(p, carry, tables=tables):
            for ty in range(3):
                r = slice(ty * B, (ty + 1) * B)
                t = tables[ty]
                u[p + 1, r, 0:LZ] = pick(t[0:1], labels[p, r, 0:LZ])
                lab = labels[p, r, LZ:]
                u[p + 1, r, LZ:] = jnp.where(near_side, pick(t[1:2], lab), pick(t[2:3], lab))
            return carry

        lax.fori_loop(max(first, b * B), min(last + 1, (b + 1) * B), one, 0)


def second_sums(n_gx, n_gy, n_col, idx, parts, weights, labels, y_lo, y_mid, y_hi,
                xl, xr, yl, yr, dvals, chunk, ua, ub, ends, sums):
    gx = idx[0]
    lines = (y_lo, y_mid, y_hi)
    coarse = [guess(parts, gx + s, n_gx, n_col)[2] for s in (-2, -1, 0, 1, 2)]
    expand(coarse[1:4], lines, labels, ua, 0, NP - 1)
    zero = jnp.zeros((NP, 2 * LZ), f32)
    for at, plane, c in ((0, xl, coarse[0]), (NP + 1, xr, coarse[4])):
        ua[at] = zero
        table = lookup(c, plane[2].astype(i32))
        ua[at, B : 2 * B, 0:LZ] = pick(table[0:1], plane[1].astype(i32))
    for at, line in ((0, yl), (1, yr)):
        table = lookup(coarse[2], line[2].astype(i32))
        ends[at] = pick(table[0:1], line[1].astype(i32))
    row_all = rows((NP, 2 * LZ))
    blank = jnp.zeros((1, LZ), f32)
    for b in range(3):

        def one(q, carry, b=b):
            p = b * B + q

            def edge(up, down):
                high = jnp.concatenate([ends[1, pl.ds(q, 1), :], blank], axis=1)
                low = jnp.concatenate([ends[0, pl.ds(q, 1), :], blank], axis=1)
                return (
                    jnp.where(row_all == NP - 1, jnp.broadcast_to(high, up.shape), up),
                    jnp.where(row_all == 0, jnp.broadcast_to(low, down.shape), down),
                )

            u, near = around(ua, weights, p, edge if b == 1 else None)
            ub[p + 1] = (1.0 - fine_relax) * u + near
            return carry

        lax.fori_loop(0, B, one, 0)
    sweep(ub, ua, weights, 1, 22)
    sweep(ua, ub, weights, 2, 21)
    sweep(ub, ua, weights, 3, 20)

    def operator(p, carry):
        u, near = around(ua, weights, p)
        ub[p + 1] = u - near * (1.0 / fine_relax)
        return carry

    lax.fori_loop(4, 20, operator, 0)
    sweep(ub, ua, weights, 5, 18)
    sweep(ua, ub, weights, 6, 17)
    sweep(ub, ua, weights, 7, 16)
    sweep(ua, ub, weights, 8, 15)
    tiles = [ub[B + 1 + q, B : 2 * B, 0:LZ] * dvals[q] for q in range(B)]
    label_tiles = [labels[B + q, B : 2 * B, 0:LZ] for q in range(B)]
    label_sums(label_tiles, (tiles,), sums)
    totals = lane_sums(sums[...])
    tile = jnp.concatenate([totals, jnp.zeros((B, LZ - NSUB), f32)], axis=1)
    for d in range(n_gy):
        chunk[d] = tile


def last_sweeps(n_gx, n_gy, n_col, idx, parts, images, weights, labels, y_lo, y_mid, y_hi,
                pressure, coarse_out, ua, ub, held):
    gx, gy, col = idx[0], idx[1], idx[2]
    lines = (y_lo, y_mid, y_hi)
    coarse = []
    for s in (-1, 0, 1):
        rhs, diag, start = guess(parts, gx + s, n_gx, n_col)
        image, exists = slab_totals(images, gx + s, n_gx, n_col)
        coarse.append(
            jnp.where(exists, start + coarse_relax * (rhs - image) / diag, 0.0)
        )
    held[...] = coarse[1]
    share = B * LZ // (n_gy * n_col)
    per_row = LZ // share
    mine = gy * n_col + col
    row = held[pl.ds(mine // per_row, 1), :]
    turned = pltpu.roll(
        jnp.broadcast_to(row, (B, LZ)), lax.rem(LZ - lax.rem(mine, per_row) * share, LZ), 1
    )
    coarse_out[...] = turned[0:1, 0:share]
    expand(coarse, lines, labels, ua, 4, 19)
    sweep(ua, ub, weights, 5, 18)
    sweep(ub, ua, weights, 6, 17)
    sweep(ua, ub, weights, 7, 16)

    def one(q, carry):
        u, near = around(ub, weights, B + q)
        moved = (1.0 - fine_relax) * u + near
        pressure[q] = moved[B : 2 * B, 0:LZ]
        return carry

    lax.fori_loop(0, B, one, 0)


def steps(count, by, wrap):
    return [
        (i, (i + by) % count) for i in range(count) if wrap or 0 <= i + by < count
    ]


def on_device(n_gx, n_gy, n_col, permeability, source, ownership, assignment, layer_flags):
    idx = jnp.stack([lax.axis_index(a) for a in ("gx", "gy", "col")]).astype(i32)
    asg = assignment.reshape(1, NSUB)
    flags = layer_flags.astype(f32)
    flags = lax.dynamic_slice_in_dim(
        jnp.pad(flags, (LZ, LZ)), lax.axis_index("col") * LZ, 3 * LZ
    ).reshape(3, LZ)
    n_out = n_gx * n_col

    def send(x, axis, by, wrap=False):
        return lax.ppermute(x, axis, steps({"gx": n_gx, "gy": n_gy, "col": n_col}[axis], by, wrap))

    mr, ml, xa, xb, ya, yb = call(
        z_messages, [sds(B + 1, B, LZ)] * 2 + [sds(3, B, LZ)] * 4, n_vmem=4
    )(permeability, source, ownership, asg)
    mr, ml = send(mr, "col", -1), send(ml, "col", 1)
    stack = call(stack_up, sds(STACK, B, LZ), n_vmem=6)(
        permeability, source, ownership, mr, ml, asg
    )
    low, high = send(stack, "gx", 1), send(stack, "gx", -1)
    xl, xr = send(xa, "gx", 2), send(xb, "gx", -2)
    line = jnp.concatenate([low[:SRC], low[SRC + 4 :], stack, high[: SRC + 4]], axis=0)
    y_lo, y_hi = send(line, "gy", 1, True), send(line, "gy", -1, True)
    yl, yr = send(ya, "gy", 2, True), send(yb, "gy", -2, True)

    full = (NP, 2 * LZ)
    weights, labels, chunk, dvals = call(
        functools.partial(drop_dvals, functools.partial(first_sums, n_gx, n_gy, n_col)),
        [sds(6, NP, *full), sds(NP, *full, dtype=i32), sds(n_gy, B, LZ), sds(B, B, LZ)],
        scratch=[
            pltpu.VMEM((NP + 2, *full), f32),
            pltpu.VMEM((NP + 1, *full), f32),
            pltpu.VMEM((NP + 2, *full), f32),
            pltpu.VMEM((NP + 2, *full), f32),
            pltpu.VMEM(full, f32),
            pltpu.VMEM(full, f32),
            pltpu.VMEM((2 * NSUB, LZ), f32),
        ],
        n_vmem=8,
        smem_first=True,
    )(idx, y_lo, line, y_hi, xl, xr, yl, yr, flags)
    bricks = lax.all_to_all(chunk, "gy", 0, 0, tiled=True)
    parts = call(
        functools.partial(coarse_partial, n_gy, n_out, 2), sds(n_out, 2 * B, LZ), n_vmem=2
    )(bricks, bricks)
    parts = lax.all_to_all(parts, ("gx", "col"), 0, 0, tiled=True)
    chunk = call(
        functools.partial(second_sums, n_gx, n_gy, n_col),
        sds(n_gy, B, LZ),
        scratch=[
            pltpu.VMEM((NP + 2, *full), f32),
            pltpu.VMEM((NP + 2, *full), f32),
            pltpu.VMEM((2, B, LZ), f32),
            pltpu.VMEM((NSUB, LZ), f32),
        ],
        n_vmem=11,
        smem_first=True,
    )(idx, parts, weights, labels, y_lo, line, y_hi, xl, xr, yl, yr, dvals)
    images = lax.all_to_all(chunk, "gy", 0, 0, tiled=True)
    images = call(
        functools.partial(coarse_partial, n_gy, n_out, 1), sds(n_out, B, LZ), n_vmem=2
    )(images, bricks)
    images = lax.all_to_all(images, ("gx", "col"), 0, 0, tiled=True)
    share = B * LZ // (n_gy * n_col)
    pressure, coarse = call(
        functools.partial(last_sweeps, n_gx, n_gy, n_col),
        [sds(B, B, LZ), sds(1, share)],
        scratch=[
            pltpu.VMEM((NP + 2, *full), f32),
            pltpu.VMEM((NP + 2, *full), f32),
            pltpu.VMEM((B, LZ), f32),
        ],
        n_vmem=7,
        smem_first=True,
    )(idx, parts, images, weights, labels, y_lo, line, y_hi)
    return pressure, coarse


def drop_dvals(kernel, idx, y_lo, y_mid, y_hi, xl, xr, yl, yr, flags,
               weights, labels, chunk, dvals, kext, fx, va, vb, fmul, zmul, sums):
    kernel(idx, y_lo, y_mid, y_hi, xl, xr, yl, yr, flags,
           weights, labels, chunk, kext, fx, va, vb, fmul, zmul, dvals, sums)


def solution(mesh):
    placed = (
        P("gx", "gy", "col"),
        P("gx", "gy", "col"),
        P("gx", "gy", "col"),
        P("gx", "gy", "col", None),
        P(),
    )
    sizes = mesh.shape
    return jax.shard_map(
        functools.partial(on_device, sizes["gx"], sizes["gy"], sizes["col"]),
        mesh=mesh,
        in_specs=placed,
        out_specs=(P("gx", "gy", "col"), P("gx", ("gy", "col"))),
        check_vma=False,
    )
```

```python
import functools

import jax
import jax.numpy as jnp
from jax import lax
from jax.experimental import pallas as pl
from jax.experimental.pallas import tpu as pltpu
from jax.sharding import PartitionSpec as P

f32 = jnp.float32
i32 = jnp.int32
bf16 = jnp.bfloat16
NSUB = 64
B = 8
LZ = 128
NP = 3 * B
W = 9
FULL = (NP, 2 * LZ)
CHUNK = 8
fine_relax = 0.6666667
coarse_relax = 0.7
VMEM_LIMIT = 48 * 1024 * 1024

PERM, OWN, HZ, ASG, SRC = 0, 8, 16, 24, 25
STACK = 33
HEAD = 25
LINE = 3 * HEAD + 2 * B


def lanes(shape):
    return lax.broadcasted_iota(i32, shape, len(shape) - 1)


def rows(shape):
    return lax.broadcasted_iota(i32, shape, len(shape) - 2)


def sds(*shape, dtype=f32):
    return jax.ShapeDtypeStruct(shape, dtype)


def call(kernel, outs, n_in, scratch=(), space=pltpu.VMEM):
    single = not isinstance(outs, (list, tuple))
    vm = pl.BlockSpec(memory_space=pltpu.VMEM)
    return pl.pallas_call(
        kernel,
        out_shape=outs,
        in_specs=[pl.BlockSpec(memory_space=space)] * n_in,
        out_specs=vm if single else [vm] * len(outs),
        scratch_shapes=list(scratch),
        compiler_params=pltpu.CompilerParams(vmem_limit_bytes=VMEM_LIMIT),
    )


def spread(row):
    return jnp.broadcast_to(row, (B, LZ))


def z_messages(perm_in, src_in, own_in, asg_in, flags_in, mr, ml, base, flags_out,
               perm, src, own, asg, flags, sem):
    copies = [
        pltpu.make_async_copy(a, b, sem.at[i])
        for i, (a, b) in enumerate(
            ((perm_in, perm), (src_in, src), (own_in, own), (asg_in, asg), (flags_in, flags))
        )
    ]
    for copy in copies:
        copy.start()
    for copy in copies:
        copy.wait()
    lane = lanes((B, LZ))
    tile = jnp.concatenate([asg[...].astype(f32), jnp.zeros((1, LZ - NSUB), f32)], axis=1)
    tile = jnp.where(rows((B, LZ)) == 0, spread(tile), 0.0)
    for p in range(B):
        k, s, o = perm[p], src[p], own[p].astype(f32)
        base[p], base[B + p], base[2 * B + p] = k, o, s
        mr[p] = jnp.where(
            lane < 16, k, jnp.where(lane < 32, pltpu.roll(o, 16, 1), pltpu.roll(s, 32, 1))
        )
        ml[p] = jnp.where(
            lane >= 112, k, jnp.where(lane >= 96, pltpu.roll(o, 112, 1), pltpu.roll(s, 96, 1))
        )
    base[3 * B] = tile
    mr[B] = tile
    ml[B] = tile
    col, n_col = lax.axis_index("col"), flags_in.shape[0]
    for i, at in enumerate((col - 1, col, col + 1)):
        at = jnp.clip(at, 0, n_col - 1)
        flags_out[pl.ds(i, 1), :] = flags[pl.ds(at, 1), :].astype(f32)


def stack_up(base, mr, ml, stack):
    lane = lanes((B, LZ))
    row = rows((B, LZ))
    for p in range(B):
        stack[PERM + p] = base[p]
        stack[OWN + p] = base[B + p]
        stack[SRC + p] = base[2 * B + p]
        stack[HZ + p] = jnp.where(lane < 64, mr[p], ml[p])
    stack[ASG] = jnp.where(
        row == 1, spread(mr[B, 0:1, :]), jnp.where(row == 2, spread(ml[B, 0:1, :]), base[3 * B])
    )


def around(u_ref, w_ref, p):
    u = u_ref[p + 1]
    return u, (
        (w_ref[0, p] * u_ref[p + 2] + w_ref[1, p] * u_ref[p])
        + (w_ref[2, p] * pltpu.roll(u, NP - 1, 0) + w_ref[3, p] * pltpu.roll(u, 1, 0))
        + (w_ref[4, p] * pltpu.roll(u, 2 * LZ - 1, 1) + w_ref[5, p] * pltpu.roll(u, 1, 1))
    )


def sweeps(both, w_ref, first, last, after=None, operator_at=-1):
    def one_sweep(k, carry):
        now = lax.rem(k, 2)
        src, dst = both.at[now], both.at[1 - now]
        count = NP - 2 * k
        keep = jnp.where(k == operator_at, 1.0, 1.0 - fine_relax)
        give = jnp.where(k == operator_at, -1.0 / fine_relax, 1.0)

        def chunk(i, carry):
            start = jnp.minimum(k + CHUNK * i, k + count - CHUNK)
            moved = []
            for j in range(CHUNK):
                u, near = around(src, w_ref, start + j)
                moved.append(keep * u + give * near)
            for j in range(CHUNK):
                dst[start + j + 1] = moved[j]
            return carry

        lax.fori_loop(0, (count + CHUNK - 1) // CHUNK, chunk, 0)
        if after is not None:
            after(k)
        return carry

    lax.fori_loop(first, last + 1, one_sweep, 0)


def label_sums(groups, sums):
    def one(s, carry):
        for first, labels, fields in groups:
            hits = [tile == s for tile in labels]
            for i, tiles in enumerate(fields):
                parts = [jnp.where(hit, tile, 0.0) for hit, tile in zip(hits, tiles)]
                while len(parts) > 1:
                    parts = [a + b for a, b in zip(parts[::2], parts[1::2])]
                sums[pl.ds(first + i * NSUB + s, 1), :] = jnp.sum(parts[0], axis=0, keepdims=True)
        return carry

    lax.fori_loop(0, NSUB, one, 0, unroll=4)


def lane_sums(sums):
    return lax.dot_general(
        jnp.ones((B, LZ), f32), sums, (((1,), (1,)), ((), ())),
        precision=lax.Precision.HIGHEST, preferred_element_type=f32,
    )


def harmonic(a, b):
    return 2.0 * a * b / (a + b)


def row_product(tile):
    for by in (4, 2, 1):
        tile = tile * pltpu.roll(tile, by, 0)
    return tile


def first_sums(n_gx, n_gy, n_col, y_lo, y_mid, y_hi, flags,
               weights, labels, chunk, dvals, paths, kext, fx, both, masks, sums):
    gx, gy, col = (lax.axis_index(a) for a in ("gx", "gy", "col"))
    lines = (y_lo, y_mid, y_hi)
    lane = lanes((B, LZ))
    row = rows((B, LZ))
    halo = (lane < W) | (lane >= LZ - W)
    near_side = lane < 64

    def positive(t):
        return jnp.where(t > 0.0, t, 1.0)

    def fill(p, carry):
        at = HEAD * (p // B) + lax.rem(p, B)
        for ty in range(3):
            line = lines[ty]
            r = slice(ty * B, (ty + 1) * B)
            packed = line[at + HZ]
            kext[p + 1, r, 0:LZ] = positive(line[at + PERM])
            kext[p + 1, r, LZ:] = positive(jnp.where(halo, packed, 1.0))
            labels[p, r, 0:LZ] = line[at + OWN].astype(i32)
            own_z = jnp.where(near_side, pltpu.roll(packed, LZ - 16, 1), pltpu.roll(packed, 16, 1))
            labels[p, r, LZ:] = jnp.where(halo, own_z, 0.0).astype(i32)
        return carry

    lax.fori_loop(0, NP, fill, 0, unroll=4)
    kext[0] = jnp.ones(FULL, f32)
    kext[NP + 1] = jnp.ones(FULL, f32)

    flag_row = jnp.concatenate(
        [flags[1:2, :], jnp.where(lane[0:1] < 64, flags[2:3, :], flags[0:1, :])], axis=1
    )
    row_all, lane_all = rows(FULL), lanes(FULL)
    wrap_row = jnp.where(gy == 0, B - 1, jnp.where(gy == n_gy - 1, 2 * B - 1, -1))
    masks[0] = jnp.where(row_all == wrap_row, jnp.broadcast_to(flag_row, FULL), 1.0)
    closed = ((lane_all == LZ - 1) & (col == n_col - 1)) | ((lane_all == 2 * LZ - 1) & (col == 0))
    masks[1] = jnp.where(closed, 0.0, 1.0)

    def x_face(p, carry):
        fx[p] = harmonic(kext[p], kext[p + 1])
        return carry

    lax.fori_loop(0, NP + 1, x_face, 0, unroll=5)

    @pl.when(gx == 0)
    def _():
        fx[B] = kext[B + 1]

    @pl.when(gx == n_gx - 1)
    def _():
        fx[2 * B] = kext[2 * B]

    def terms(p, carry):
        b = p // B
        out = ((b == 0) & (gx == 0)) | ((b == 2) & (gx == n_gx - 1))
        k = kext[p + 1]
        fy_up = harmonic(k, pltpu.roll(k, NP - 1, 0)) * masks[0]
        fy_down = pltpu.roll(fy_up, 1, 0)
        fz_right = harmonic(k, pltpu.roll(k, 2 * LZ - 1, 1)) * masks[1]
        fz_left = pltpu.roll(fz_right, 1, 1)
        fx_up, fx_down = fx[p + 1], fx[p]
        diag = fx_up + fx_down + fy_up + fy_down + fz_right + fz_left
        inverse = 1.0 / diag
        scale = jnp.where(out, 0.0, fine_relax) * inverse
        for i, face in enumerate((fx_up, fx_down, fy_up, fy_down, fz_right, fz_left)):
            weights[i, p] = face * scale
        at = 3 * HEAD + jnp.clip(p - 4, 0, 2 * B - 1)
        hz = HEAD * b + HZ + lax.rem(p, B)
        for ty in range(3):
            line = lines[ty]
            r = slice(ty * B, (ty + 1) * B)
            packed = line[hz]
            src_z = jnp.where(near_side, pltpu.roll(packed, LZ - 32, 1), pltpu.roll(packed, 32, 1))
            both[1, p + 1, r, 0:LZ] = line[at] * inverse[r, 0:LZ]
            both[1, p + 1, r, LZ:] = jnp.where(halo, src_z, 0.0) * inverse[r, LZ:]

        @pl.when(b == 1)
        def _():
            q = p - B
            r = slice(B, 2 * B)
            dvals[q] = diag[r, 0:LZ]
            up, down = (face[r, 0:LZ] for face in (fy_up, fy_down))
            s = scale[r, 0:LZ]
            rise = row_product(jnp.where(row == 0, 1.0, down * s))
            fall = row_product(jnp.where(row == B - 1, 1.0, up * s))
            paths[2, pl.ds(q, 1), :] = rise[0:1] * up[B - 1 : B]
            paths[3, pl.ds(q, 1), :] = fall[0:1] * down[0:1]

        return carry

    lax.fori_loop(0, NP, terms, 0, unroll=2)
    rise, fall = fx[2 * B, B : 2 * B, 0:LZ], fx[B, B : 2 * B, 0:LZ]
    for p in range(B + 1, 2 * B):
        rise = rise * weights[1, p, B : 2 * B, 0:LZ]
        fall = fall * weights[0, p - 1, B : 2 * B, 0:LZ]
    paths[0] = rise
    paths[1] = fall

    sweeps(both, weights, 5, 8)
    tiles = [both[1, B + 1 + q, B : 2 * B, 0:LZ] * dvals[q] for q in range(B)]
    diag_tiles = [dvals[q] for q in range(B)]
    label_tiles = [labels[B + q, B : 2 * B, 0:LZ] for q in range(B)]
    label_sums([(0, label_tiles, (tiles, diag_tiles))], sums)
    totals = lane_sums(sums[...])

    def twice(low, high):
        return jnp.where(lane < NSUB, low, pltpu.roll(high, NSUB, 1))

    own, left, right = (spread(y_mid[HEAD * b + ASG, 0:1, :]) for b in (1, 0, 2))
    tile = jnp.where(
        row == 0, totals, jnp.where(row == 1, twice(own, own), twice(right, left))
    )
    for d in range(n_gy):
        chunk[d] = tile


def one_hot_product(lefts, lows, out, n_out):
    left = jnp.concatenate(lefts, axis=1)
    l1 = left.astype(bf16)
    rest = left - l1.astype(f32)
    l2 = rest.astype(bf16)
    l3 = (rest - l2.astype(f32)).astype(bf16)
    wide = rows((LZ, LZ))
    right = jnp.concatenate(
        [
            jnp.where(jnp.broadcast_to(low, (LZ, LZ)) == wide, 1.0, 0.0).astype(bf16)
            for low in lows
        ],
        axis=1,
    )
    total = sum(
        lax.dot_general(part, right, (((1,), (1,)), ((), ())), preferred_element_type=f32)
        for part in (l3, l2, l1)
    )
    for d in range(n_out):
        out[d] = total


def halves(value, high):
    lane = lanes((B, LZ))
    scaled = jnp.where(high == rows((B, LZ)), value, 0.0)
    return jnp.where(lane < NSUB, scaled, 0.0), jnp.where(lane < NSUB, 0.0, scaled)


def first_partial(n_gy, n_out, values, out):
    lefts, lows = [], []
    for g in range(n_gy):
        a = values[g, 1:2, :].astype(i32)
        lefts.append(jnp.concatenate(halves(spread(values[g, 0:1, :]), spread(a >> 7)), axis=0))
        lows.append(a & 127)
    one_hot_product(lefts, lows, out, n_out)


def second_partial(n_gy, n_out, values, first, out):
    lane = lanes((B, LZ))
    lefts, lows = [], []
    for g in range(n_gy):
        before, after = (g - 1) % n_gy, (g + 1) % n_gy
        own = spread(values[g, 0:1, :] + values[before, 2:3, :])
        own = own + pltpu.roll(spread(values[after, 2:3, :]), NSUB, 1)
        a = first[g, 1:2, :].astype(i32)
        mine, _ = halves(own, spread(a >> 7))
        lows.append(a & 127)
        a = first[g, 2:3, :].astype(i32)
        above, below = halves(spread(values[g, 1:2, :]), spread(a >> 7))
        lows.append(a & 127)
        zero = jnp.zeros((B, LZ), f32)
        lefts.append(jnp.concatenate([mine, zero, zero], axis=0))
        lefts.append(jnp.concatenate([zero, above, below], axis=0))
    one_hot_product(lefts, lows, out, n_out)


def lookup(table, index):
    low, high = index & 127, index >> 7
    result = jnp.zeros((B, LZ), f32)
    for h in range(B):
        got = jnp.take_along_axis(spread(table[h : h + 1]), low, axis=1)
        result = jnp.where(high == h, got, result)
    return result


def pick(row, index):
    return jnp.take_along_axis(spread(row), index, axis=1)


def slab_total(parts, g, n_gx, n_col, part, size):
    at = jnp.clip(g, 0, n_gx - 1) * n_col
    total = parts[at, part : part + size]
    for c in range(1, n_col):
        total = total + parts[at + c, part : part + size]
    return jnp.where((g >= 0) & (g < n_gx), total, 0.0)


def guess(parts, g, n_gx, n_col):
    total = slab_total(parts, g, n_gx, n_col, 0, 2 * B)
    exists = (g >= 0) & (g < n_gx)
    rhs, diag = total[0:B], jnp.where(exists, total[B : 2 * B], 1.0)
    return rhs, diag, coarse_relax * rhs / diag


def expand(coarse, lines, labels, u, tables, first, last):
    near_side = lanes((B, LZ)) < 64

    def table(b, carry):
        for ty in range(3):
            tables[b, ty] = lookup(coarse[b], lines[ty][HEAD * b + ASG].astype(i32))
        return carry

    lax.fori_loop(0, 3, table, 0)

    def one(p, carry):
        b = p // B
        for ty in range(3):
            r = slice(ty * B, (ty + 1) * B)
            t = tables[b, ty]
            u[p + 1, r, 0:LZ] = pick(t[0:1], labels[p, r, 0:LZ])
            lab = labels[p, r, LZ:]
            u[p + 1, r, LZ:] = jnp.where(near_side, pick(t[1:2], lab), pick(t[2:3], lab))
        return carry

    lax.fori_loop(first, last + 1, one, 0, unroll=4)


def second_sums(n_gx, n_gy, n_col, parts, weights, labels, y_lo, y_mid, y_hi, dvals, paths,
                chunk, both, coarse, tables, ends, sums):
    gx = lax.axis_index("gx")
    row = rows((B, LZ))
    r = slice(B, 2 * B)
    for i in range(3):
        coarse[i] = guess(parts, gx + i - 1, n_gx, n_col)[2]
    expand(coarse, (y_lo, y_mid, y_hi), labels, both.at[0], tables, 0, NP - 1)

    def after(k):
        @pl.when(k == 0)
        def _():
            first = both.at[1]
            zero = jnp.zeros(FULL, f32)
            first[1] = zero
            first[NP] = zero
            first[:, 0:1, :] = jnp.zeros((NP + 2, 1, 2 * LZ), f32)
            first[:, NP - 1 :, :] = jnp.zeros((NP + 2, 1, 2 * LZ), f32)
            ends[0] = first[B + 1, r, 0:LZ] * -paths[0]
            ends[1] = first[2 * B, r, 0:LZ] * -paths[1]
            for q in range(B):
                plane = first[B + 1 + q, r, 0:LZ]
                ends[2, q : q + 1, :] = plane[0:1] * -paths[2, q : q + 1, :]
                ends[3, q : q + 1, :] = plane[B - 1 : B] * -paths[3, q : q + 1, :]

    sweeps(both, weights, 0, 8, after=after, operator_at=4)
    tiles = [both[1, B + 1 + q, r, 0:LZ] * dvals[q] for q in range(B)]
    label_tiles = [labels[B + q, r, 0:LZ] for q in range(B)]
    beyond = [labels[2 * B, r, 0:LZ], labels[B - 1, r, 0:LZ]]
    for at in (2 * B, B - 1):
        edge = labels[B, at : at + 1, 0:LZ]
        edge = spread(edge)
        for q in range(1, B):
            edge = jnp.where(row == q, spread(labels[B + q, at : at + 1, 0:LZ]), edge)
        beyond.append(edge)
    groups = [(0, label_tiles, (tiles,))]
    groups += [((2 + i) * NSUB, [beyond[i]], ([ends[i]],)) for i in range(4)]
    sums[NSUB : 2 * NSUB, :] = jnp.zeros((NSUB, LZ), f32)
    label_sums(groups, sums)
    totals = lane_sums(sums[...])
    tile = jnp.where(
        row == 0,
        totals[:, 0:LZ],
        jnp.where(row == 1, totals[:, LZ : 2 * LZ], totals[:, 2 * LZ :]),
    )
    for d in range(n_gy):
        chunk[d] = tile


def last_sweeps(n_gx, n_gy, n_col, parts, images, weights, labels, y_lo, y_mid, y_hi,
                pressure, coarse_out, both, coarse, tables):
    gx, gy, col = (lax.axis_index(a) for a in ("gx", "gy", "col"))
    for i in range(3):
        g = gx + i - 1
        rhs, diag, start = guess(parts, g, n_gx, n_col)
        image = (
            slab_total(images, g, n_gx, n_col, 0, B)
            + slab_total(images, g - 1, n_gx, n_col, B, B)
            + slab_total(images, g + 1, n_gx, n_col, 2 * B, B)
        )
        second = start + coarse_relax * (rhs - image) / diag
        coarse[i] = jnp.where((g >= 0) & (g < n_gx), second, 0.0)
    share = B * LZ // (n_gy * n_col)
    per_row = LZ // share
    mine = gy * n_col + col
    row = coarse[1, pl.ds(mine // per_row, 1), :]
    turned = pltpu.roll(spread(row), lax.rem(LZ - lax.rem(mine, per_row) * share, LZ), 1)
    coarse_out[...] = turned[0:1, 0:share]
    expand(coarse, (y_lo, y_mid, y_hi), labels, both.at[1], tables, 4, 19)
    sweeps(both, weights, 5, 8)
    for q in range(B):
        pressure[q] = both[1, B + 1 + q, B : 2 * B, 0:LZ]


def steps(count, by, wrap):
    return [
        (i, (i + by) % count) for i in range(count) if wrap or 0 <= i + by < count
    ]


def on_device(n_gx, n_gy, n_col, permeability, source, ownership, assignment, layer_flags):
    n_out = n_gx * n_col
    sizes = (n_gx, n_gy, n_col)
    vm = pltpu.VMEM
    fields = vm((2, NP + 2, *FULL), f32)
    plane = (B, B, LZ)

    def send(x, axis, by, wrap=False):
        return lax.ppermute(x, axis, steps(lax.axis_size(axis), by, wrap))

    mr, ml, base, flags = call(
        z_messages,
        [sds(B + 1, B, LZ)] * 2 + [sds(3 * B + 1, B, LZ), sds(3, LZ)],
        5,
        scratch=[
            vm(plane, f32), vm(plane, f32), vm(plane, i32), vm((1, NSUB), i32),
            vm((n_col, LZ), i32), pltpu.SemaphoreType.DMA((5,)),
        ],
        space=pl.ANY,
    )(permeability, source, ownership, assignment.reshape(1, NSUB), layer_flags.reshape(n_col, LZ))
    mr, ml = send(mr, "col", -1), send(ml, "col", 1)
    stack = call(stack_up, sds(STACK, B, LZ), 3)(base, mr, ml)
    low, high = send(stack, "gx", 1), send(stack, "gx", -1)
    line = jnp.concatenate(
        [low[:HEAD], stack[:HEAD], high[:HEAD], low[SRC + 4 :], stack[SRC:], high[SRC : SRC + 4]],
        axis=0,
    )
    y_lo, y_hi = send(line, "gy", 1, True), send(line, "gy", -1, True)

    weights, labels, chunk, dvals, paths = call(
        functools.partial(first_sums, *sizes),
        [
            sds(6, NP, *FULL), sds(NP, *FULL, dtype=i32), sds(n_gy, B, LZ), sds(*plane),
            sds(4, B, LZ),
        ],
        4,
        scratch=[
            vm((NP + 2, *FULL), f32), vm((NP + 1, *FULL), f32), fields, vm((2, *FULL), f32),
            vm((2 * NSUB, LZ), f32),
        ],
    )(y_lo, line, y_hi, flags)
    bricks = lax.all_to_all(chunk, "gy", 0, 0, tiled=True)
    parts = call(
        functools.partial(first_partial, n_gy, n_out), sds(n_out, 2 * B, LZ), 1
    )(bricks)
    parts = lax.all_to_all(parts, ("gx", "col"), 0, 0, tiled=True)
    tables = [vm((3, B, LZ), f32), vm((3, 3, B, LZ), f32)]
    chunk = call(
        functools.partial(second_sums, *sizes),
        sds(n_gy, B, LZ),
        8,
        scratch=[fields, *tables, vm((4, B, LZ), f32), vm((6 * NSUB, LZ), f32)],
    )(parts, weights, labels, y_lo, line, y_hi, dvals, paths)
    images = lax.all_to_all(chunk, "gy", 0, 0, tiled=True)
    images = call(
        functools.partial(second_partial, n_gy, n_out), sds(n_out, 3 * B, LZ), 2
    )(images, bricks)
    images = lax.all_to_all(images, ("gx", "col"), 0, 0, tiled=True)
    return call(
        functools.partial(last_sweeps, *sizes),
        [sds(*plane), sds(1, B * LZ // (n_gy * n_col))],
        7,
        scratch=[fields, *tables],
    )(parts, images, weights, labels, y_lo, line, y_hi)


def solution(mesh):
    placed = (
        P("gx", "gy", "col"),
        P("gx", "gy", "col"),
        P("gx", "gy", "col"),
        P("gx", "gy", "col", None),
        P(),
    )
    sizes = mesh.shape
    return jax.shard_map(
        functools.partial(on_device, sizes["gx"], sizes["gy"], sizes["col"]),
        mesh=mesh,
        in_specs=placed,
        out_specs=(P("gx", "gy", "col"), P("gx", ("gy", "col"))),
        check_vma=False,
    )
```

```python
import functools

import jax
import jax.numpy as jnp
from jax import lax
from jax.experimental import pallas as pl
from jax.experimental.pallas import tpu as pltpu
from jax.sharding import PartitionSpec as P

f32 = jnp.float32
i32 = jnp.int32
bf16 = jnp.bfloat16
NSUB = 64
B = 8
LZ = 128
NP = 3 * B
W = 9
FULL = (NP, 2 * LZ)
CHUNK = 8
fine_relax = 0.6666667
coarse_relax = 0.7
VMEM_LIMIT = 48 * 1024 * 1024
WHOLE_VMEM = 63 * 1024 * 1024

PERM, OWN, HZ, ASG, SRC = 0, 8, 16, 24, 25
STACK = 33
HEAD = 25
LINE = 3 * HEAD + 2 * B


def lanes(shape):
    return lax.broadcasted_iota(i32, shape, len(shape) - 1)


def rows(shape):
    return lax.broadcasted_iota(i32, shape, len(shape) - 2)


def sds(*shape, dtype=f32):
    return jax.ShapeDtypeStruct(shape, dtype)


def call(kernel, outs, n_in, scratch=(), space=pltpu.VMEM, limit=VMEM_LIMIT):
    single = not isinstance(outs, (list, tuple))
    vm = pl.BlockSpec(memory_space=pltpu.VMEM)
    return pl.pallas_call(
        kernel,
        out_shape=outs,
        in_specs=[pl.BlockSpec(memory_space=space)] * n_in,
        out_specs=vm if single else [vm] * len(outs),
        scratch_shapes=list(scratch),
        compiler_params=pltpu.CompilerParams(vmem_limit_bytes=limit),
    )


def spread(row):
    return jnp.broadcast_to(row, (B, LZ))


def z_messages(perm_in, src_in, own_in, asg_in, flags_in, mr, ml, base, flags_out,
               perm, src, own, asg, flags, sem):
    copies = [
        pltpu.make_async_copy(a, b, sem.at[i])
        for i, (a, b) in enumerate(
            ((perm_in, perm), (src_in, src), (own_in, own), (asg_in, asg), (flags_in, flags))
        )
    ]
    for copy in copies:
        copy.start()
    for copy in copies:
        copy.wait()
    lane = lanes((B, LZ))
    tile = jnp.concatenate([asg[...].astype(f32), jnp.zeros((1, LZ - NSUB), f32)], axis=1)
    tile = jnp.where(rows((B, LZ)) == 0, spread(tile), 0.0)
    for p in range(B):
        k, s, o = perm[p], src[p], own[p].astype(f32)
        base[p], base[B + p], base[2 * B + p] = k, o, s
        mr[p] = jnp.where(
            lane < 16, k, jnp.where(lane < 32, pltpu.roll(o, 16, 1), pltpu.roll(s, 32, 1))
        )
        ml[p] = jnp.where(
            lane >= 112, k, jnp.where(lane >= 96, pltpu.roll(o, 112, 1), pltpu.roll(s, 96, 1))
        )
    base[3 * B] = tile
    mr[B] = tile
    ml[B] = tile
    col, n_col = lax.axis_index("col"), flags_in.shape[0]
    for i, at in enumerate((col - 1, col, col + 1)):
        at = jnp.clip(at, 0, n_col - 1)
        flags_out[pl.ds(i, 1), :] = flags[pl.ds(at, 1), :].astype(f32)


def stack_up(base, mr, ml, stack):
    lane = lanes((B, LZ))
    row = rows((B, LZ))
    for p in range(B):
        stack[PERM + p] = base[p]
        stack[OWN + p] = base[B + p]
        stack[SRC + p] = base[2 * B + p]
        stack[HZ + p] = jnp.where(lane < 64, mr[p], ml[p])
    stack[ASG] = jnp.where(
        row == 1, spread(mr[B, 0:1, :]), jnp.where(row == 2, spread(ml[B, 0:1, :]), base[3 * B])
    )


def around(u_ref, w_ref, p):
    u = u_ref[p + 1]
    return u, (
        (w_ref[0, p] * u_ref[p + 2] + w_ref[1, p] * u_ref[p])
        + (w_ref[2, p] * pltpu.roll(u, NP - 1, 0) + w_ref[3, p] * pltpu.roll(u, 1, 0))
        + (w_ref[4, p] * pltpu.roll(u, 2 * LZ - 1, 1) + w_ref[5, p] * pltpu.roll(u, 1, 1))
    )


def sweeps(both, w_ref, first, last, after=None, operator_at=-1):
    def one_sweep(k, carry):
        now = lax.rem(k, 2)
        src, dst = both.at[now], both.at[1 - now]
        count = NP - 2 * k
        keep = jnp.where(k == operator_at, 1.0, 1.0 - fine_relax)
        give = jnp.where(k == operator_at, -1.0 / fine_relax, 1.0)

        def chunk(i, carry):
            start = jnp.minimum(k + CHUNK * i, k + count - CHUNK)
            moved = []
            for j in range(CHUNK):
                u, near = around(src, w_ref, start + j)
                moved.append(keep * u + give * near)
            for j in range(CHUNK):
                dst[start + j + 1] = moved[j]
            return carry

        lax.fori_loop(0, (count + CHUNK - 1) // CHUNK, chunk, 0)
        if after is not None:
            after(k)
        return carry

    lax.fori_loop(first, last + 1, one_sweep, 0)


def label_sums(groups, sums):
    def one(s, carry):
        for first, labels, fields in groups:
            hits = [tile == s for tile in labels]
            for i, tiles in enumerate(fields):
                parts = [jnp.where(hit, tile, 0.0) for hit, tile in zip(hits, tiles)]
                while len(parts) > 1:
                    parts = [a + b for a, b in zip(parts[::2], parts[1::2])]
                sums[pl.ds(first + i * NSUB + s, 1), :] = jnp.sum(parts[0], axis=0, keepdims=True)
        return carry

    lax.fori_loop(0, NSUB, one, 0, unroll=4)


def lane_sums(sums):
    return lax.dot_general(
        jnp.ones((B, LZ), f32), sums, (((1,), (1,)), ((), ())),
        precision=lax.Precision.HIGHEST, preferred_element_type=f32,
    )


def harmonic(a, b):
    return 2.0 * a * b / (a + b)


def row_product(tile):
    for by in (4, 2, 1):
        tile = tile * pltpu.roll(tile, by, 0)
    return tile


def first_sums(n_gx, n_gy, n_col, y_lo, y_mid, y_hi, flags,
               weights, labels, chunk, dvals, paths, kext, fx, both, masks, sums):
    gx, gy, col = (lax.axis_index(a) for a in ("gx", "gy", "col"))
    lines = (y_lo, y_mid, y_hi)
    lane = lanes((B, LZ))
    row = rows((B, LZ))
    halo = (lane < W) | (lane >= LZ - W)
    near_side = lane < 64

    def positive(t):
        return jnp.where(t > 0.0, t, 1.0)

    def fill(p, carry):
        at = HEAD * (p // B) + lax.rem(p, B)
        for ty in range(3):
            line = lines[ty]
            r = slice(ty * B, (ty + 1) * B)
            packed = line[at + HZ]
            kext[p + 1, r, 0:LZ] = positive(line[at + PERM])
            kext[p + 1, r, LZ:] = positive(jnp.where(halo, packed, 1.0))
            labels[p, r, 0:LZ] = line[at + OWN].astype(i32)
            own_z = jnp.where(near_side, pltpu.roll(packed, LZ - 16, 1), pltpu.roll(packed, 16, 1))
            labels[p, r, LZ:] = jnp.where(halo, own_z, 0.0).astype(i32)
        return carry

    lax.fori_loop(0, NP, fill, 0, unroll=4)
    kext[0] = jnp.ones(FULL, f32)
    kext[NP + 1] = jnp.ones(FULL, f32)

    flag_row = jnp.concatenate(
        [flags[1:2, :], jnp.where(lane[0:1] < 64, flags[2:3, :], flags[0:1, :])], axis=1
    )
    row_all, lane_all = rows(FULL), lanes(FULL)
    wrap_row = jnp.where(gy == 0, B - 1, jnp.where(gy == n_gy - 1, 2 * B - 1, -1))
    masks[0] = jnp.where(row_all == wrap_row, jnp.broadcast_to(flag_row, FULL), 1.0)
    closed = ((lane_all == LZ - 1) & (col == n_col - 1)) | ((lane_all == 2 * LZ - 1) & (col == 0))
    masks[1] = jnp.where(closed, 0.0, 1.0)

    def x_face(p, carry):
        fx[p] = harmonic(kext[p], kext[p + 1])
        return carry

    lax.fori_loop(0, NP + 1, x_face, 0, unroll=5)

    @pl.when(gx == 0)
    def _():
        fx[B] = kext[B + 1]

    @pl.when(gx == n_gx - 1)
    def _():
        fx[2 * B] = kext[2 * B]

    def terms(p, carry):
        b = p // B
        out = ((b == 0) & (gx == 0)) | ((b == 2) & (gx == n_gx - 1))
        k = kext[p + 1]
        fy_up = harmonic(k, pltpu.roll(k, NP - 1, 0)) * masks[0]
        fy_down = pltpu.roll(fy_up, 1, 0)
        fz_right = harmonic(k, pltpu.roll(k, 2 * LZ - 1, 1)) * masks[1]
        fz_left = pltpu.roll(fz_right, 1, 1)
        fx_up, fx_down = fx[p + 1], fx[p]
        diag = fx_up + fx_down + fy_up + fy_down + fz_right + fz_left
        inverse = 1.0 / diag
        scale = jnp.where(out, 0.0, fine_relax) * inverse
        for i, face in enumerate((fx_up, fx_down, fy_up, fy_down, fz_right, fz_left)):
            weights[i, p] = face * scale
        at = 3 * HEAD + jnp.clip(p - 4, 0, 2 * B - 1)
        hz = HEAD * b + HZ + lax.rem(p, B)
        for ty in range(3):
            line = lines[ty]
            r = slice(ty * B, (ty + 1) * B)
            packed = line[hz]
            src_z = jnp.where(near_side, pltpu.roll(packed, LZ - 32, 1), pltpu.roll(packed, 32, 1))
            both[1, p + 1, r, 0:LZ] = line[at] * inverse[r, 0:LZ]
            both[1, p + 1, r, LZ:] = jnp.where(halo, src_z, 0.0) * inverse[r, LZ:]

        @pl.when(b == 1)
        def _():
            q = p - B
            r = slice(B, 2 * B)
            dvals[q] = diag[r, 0:LZ]
            up, down = (face[r, 0:LZ] for face in (fy_up, fy_down))
            s = scale[r, 0:LZ]
            rise = row_product(jnp.where(row == 0, 1.0, down * s))
            fall = row_product(jnp.where(row == B - 1, 1.0, up * s))
            paths[2, pl.ds(q, 1), :] = rise[0:1] * up[B - 1 : B]
            paths[3, pl.ds(q, 1), :] = fall[0:1] * down[0:1]

        return carry

    lax.fori_loop(0, NP, terms, 0, unroll=2)
    rise, fall = fx[2 * B, B : 2 * B, 0:LZ], fx[B, B : 2 * B, 0:LZ]
    for p in range(B + 1, 2 * B):
        rise = rise * weights[1, p, B : 2 * B, 0:LZ]
        fall = fall * weights[0, p - 1, B : 2 * B, 0:LZ]
    paths[0] = rise
    paths[1] = fall

    sweeps(both, weights, 5, 8)
    tiles = [both[1, B + 1 + q, B : 2 * B, 0:LZ] * dvals[q] for q in range(B)]
    diag_tiles = [dvals[q] for q in range(B)]
    label_tiles = [labels[B + q, B : 2 * B, 0:LZ] for q in range(B)]
    label_sums([(0, label_tiles, (tiles, diag_tiles))], sums)
    totals = lane_sums(sums[...])

    own = spread(y_mid[HEAD + ASG, 0:1, :])
    own = jnp.where(lane < NSUB, own, pltpu.roll(own, NSUB, 1))
    tile = jnp.where(row == 0, totals, own)[0:2]
    for d in range(n_gy * n_col):
        chunk[d] = tile


def one_hot_product(lefts, lows):
    left = jnp.concatenate(lefts, axis=1)
    l1 = left.astype(bf16)
    rest = left - l1.astype(f32)
    l2 = rest.astype(bf16)
    l3 = (rest - l2.astype(f32)).astype(bf16)
    wide = rows((LZ, LZ))
    right = jnp.concatenate(
        [
            jnp.where(jnp.broadcast_to(low, (LZ, LZ)) == wide, 1.0, 0.0).astype(bf16)
            for low in lows
        ],
        axis=1,
    )
    return sum(
        lax.dot_general(part, right, (((1,), (1,)), ((), ())), preferred_element_type=f32)
        for part in (l3, l2, l1)
    )


def halves(value, high):
    lane = lanes((B, LZ))
    scaled = jnp.where(high == rows((B, LZ)), value, 0.0)
    return jnp.concatenate(
        [jnp.where(lane < NSUB, scaled, 0.0), jnp.where(lane < NSUB, 0.0, scaled)], axis=0
    )


GROUP = 8


def first_coarse(n_bricks, n_out, values, out):
    def one(i, total):
        lefts, lows = [], []
        for j in range(GROUP):
            value = values[i * GROUP + j]
            a = value[1:2].astype(i32)
            lefts.append(halves(spread(value[0:1]), spread(a >> 7)))
            lows.append(a & 127)
        return total + one_hot_product(lefts, lows)

    total = lax.fori_loop(0, n_bricks // GROUP, one, jnp.zeros((2 * B, LZ), f32))
    for d in range(n_out):
        out[d] = total


def second_coarse(n_gy, n_col, n_out, values, first, out):
    n_bricks = n_gy * n_col
    lane = lanes((B, LZ))
    near = lanes((1, LZ)) < NSUB

    def own(j):
        before = lax.rem(j + n_bricks - n_col, n_bricks)
        after = lax.rem(j + n_col, n_bricks)
        mine = spread(values[j, 0:1] + values[before, 2:3])
        return mine + pltpu.roll(spread(values[after, 2:3]), NSUB, 1)

    def one(i, totals):
        lefts, lows, edge_lefts, edge_lows = [], [], [], []
        for j in range(GROUP // 2):
            at = i * GROUP + 2 * j
            pair = jnp.where(lane < NSUB, own(at), pltpu.roll(own(at + 1), NSUB, 1))
            a = jnp.where(near, first[at, 1:2], first[at + 1, 1:2]).astype(i32)
            lefts.append(jnp.where(spread(a >> 7) == rows((B, LZ)), pair, 0.0))
            lows.append(a & 127)
        for j in range(GROUP):
            a = values[i * GROUP + j, 3:4].astype(i32)
            edge_lefts.append(halves(spread(values[i * GROUP + j, 1:2]), spread(a >> 7)))
            edge_lows.append(a & 127)
        return (
            totals[0] + one_hot_product(lefts, lows),
            totals[1] + one_hot_product(edge_lefts, edge_lows),
        )

    mine, edges = lax.fori_loop(
        0, n_bricks // GROUP, one, (jnp.zeros((B, LZ), f32), jnp.zeros((2 * B, LZ), f32))
    )
    total = jnp.concatenate([mine, edges], axis=0)
    for d in range(n_out):
        out[d] = total


def lookup(table, index):
    low, high = index & 127, index >> 7
    result = jnp.zeros((B, LZ), f32)
    for h in range(B):
        got = jnp.take_along_axis(spread(table[h : h + 1]), low, axis=1)
        result = jnp.where(high == h, got, result)
    return result


def pick(row, index):
    return jnp.take_along_axis(spread(row), index, axis=1)


def slab_total(parts, g, n_gx, part, size):
    total = parts[jnp.clip(g, 0, n_gx - 1), part : part + size]
    return jnp.where((g >= 0) & (g < n_gx), total, 0.0)


def guess(parts, g, n_gx):
    total = slab_total(parts, g, n_gx, 0, 2 * B)
    exists = (g >= 0) & (g < n_gx)
    rhs, diag = total[0:B], jnp.where(exists, total[B : 2 * B], 1.0)
    return rhs, diag, coarse_relax * rhs / diag


def expand(coarse, lines, labels, u, tables, first, last):
    near_side = lanes((B, LZ)) < 64

    def table(b, carry):
        for ty in range(3):
            tables[b, ty] = lookup(coarse[b], lines[ty][HEAD * b + ASG].astype(i32))
        return carry

    lax.fori_loop(0, 3, table, 0)

    def one(p, carry):
        b = p // B
        for ty in range(3):
            r = slice(ty * B, (ty + 1) * B)
            t = tables[b, ty]
            u[p + 1, r, 0:LZ] = pick(t[0:1], labels[p, r, 0:LZ])
            lab = labels[p, r, LZ:]
            u[p + 1, r, LZ:] = jnp.where(near_side, pick(t[1:2], lab), pick(t[2:3], lab))
        return carry

    lax.fori_loop(first, last + 1, one, 0, unroll=4)


def second_sums(n_gx, n_gy, n_col, parts, weights, labels, y_lo, y_mid, y_hi, dvals, paths,
                chunk, both, coarse, tables, ends, sums):
    gx = lax.axis_index("gx")
    row = rows((B, LZ))
    r = slice(B, 2 * B)
    for i in range(3):
        coarse[i] = guess(parts, gx + i - 1, n_gx)[2]
    expand(coarse, (y_lo, y_mid, y_hi), labels, both.at[0], tables, 0, NP - 1)

    def after(k):
        @pl.when(k == 0)
        def _():
            first = both.at[1]
            zero = jnp.zeros(FULL, f32)
            first[1] = zero
            first[NP] = zero
            first[:, 0:1, :] = jnp.zeros((NP + 2, 1, 2 * LZ), f32)
            first[:, NP - 1 :, :] = jnp.zeros((NP + 2, 1, 2 * LZ), f32)
            ends[0] = first[B + 1, r, 0:LZ] * -paths[0]
            ends[1] = first[2 * B, r, 0:LZ] * -paths[1]
            for q in range(B):
                plane = first[B + 1 + q, r, 0:LZ]
                ends[2, q : q + 1, :] = plane[0:1] * -paths[2, q : q + 1, :]
                ends[3, q : q + 1, :] = plane[B - 1 : B] * -paths[3, q : q + 1, :]

    sweeps(both, weights, 0, 8, after=after, operator_at=4)
    tiles = [both[1, B + 1 + q, r, 0:LZ] * dvals[q] for q in range(B)]
    label_tiles = [labels[B + q, r, 0:LZ] for q in range(B)]
    beyond = [labels[2 * B, r, 0:LZ], labels[B - 1, r, 0:LZ]]
    for at in (2 * B, B - 1):
        edge = labels[B, at : at + 1, 0:LZ]
        edge = spread(edge)
        for q in range(1, B):
            edge = jnp.where(row == q, spread(labels[B + q, at : at + 1, 0:LZ]), edge)
        beyond.append(edge)
    groups = [(0, label_tiles, (tiles,))]
    groups += [((2 + i) * NSUB, [beyond[i]], ([ends[i]],)) for i in range(4)]
    sums[NSUB : 2 * NSUB, :] = jnp.zeros((NSUB, LZ), f32)
    label_sums(groups, sums)
    totals = lane_sums(sums[...])
    right, left = (spread(y_mid[HEAD * b + ASG, 0:1, :]) for b in (2, 0))
    asg = jnp.where(lanes((B, LZ)) < NSUB, right, pltpu.roll(left, NSUB, 1))
    tile = jnp.where(
        row < 2,
        jnp.where(row == 0, totals[:, 0:LZ], totals[:, LZ : 2 * LZ]),
        jnp.where(row == 2, totals[:, 2 * LZ :], asg),
    )[0:4]
    for d in range(n_gy * n_col):
        chunk[d] = tile


def last_sweeps(n_gx, n_gy, n_col, parts, images, weights, labels, y_lo, y_mid, y_hi,
                pressure, coarse_out, both, coarse, tables):
    gx, gy, col = (lax.axis_index(a) for a in ("gx", "gy", "col"))
    for i in range(3):
        g = gx + i - 1
        rhs, diag, start = guess(parts, g, n_gx)
        image = (
            slab_total(images, g, n_gx, 0, B)
            + slab_total(images, g - 1, n_gx, B, B)
            + slab_total(images, g + 1, n_gx, 2 * B, B)
        )
        second = start + coarse_relax * (rhs - image) / diag
        coarse[i] = jnp.where((g >= 0) & (g < n_gx), second, 0.0)
    share = B * LZ // (n_gy * n_col)
    per_row = LZ // share
    mine = gy * n_col + col
    row = coarse[1, pl.ds(mine // per_row, 1), :]
    turned = pltpu.roll(spread(row), lax.rem(LZ - lax.rem(mine, per_row) * share, LZ), 1)
    coarse_out[...] = turned[0:1, 0:share]
    expand(coarse, (y_lo, y_mid, y_hi), labels, both.at[1], tables, 4, 19)
    sweeps(both, weights, 5, 8)
    for q in range(B):
        pressure[q] = both[1, B + 1 + q, B : 2 * B, 0:LZ]


def steps(count, by, wrap):
    return [
        (i, (i + by) % count) for i in range(count) if wrap or 0 <= i + by < count
    ]


def on_device(n_gx, n_gy, n_col, permeability, source, ownership, assignment, layer_flags):
    n_bricks = n_gy * n_col
    sizes = (n_gx, n_gy, n_col)
    vm = pltpu.VMEM
    fields = vm((2, NP + 2, *FULL), f32)
    plane = (B, B, LZ)

    def send(x, axis, by, wrap=False):
        return lax.ppermute(x, axis, steps(lax.axis_size(axis), by, wrap))

    mr, ml, base, flags = call(
        z_messages,
        [sds(B + 1, B, LZ)] * 2 + [sds(3 * B + 1, B, LZ), sds(3, LZ)],
        5,
        scratch=[
            vm(plane, f32), vm(plane, f32), vm(plane, i32), vm((1, NSUB), i32),
            vm((n_col, LZ), i32), pltpu.SemaphoreType.DMA((5,)),
        ],
        space=pl.ANY,
        limit=WHOLE_VMEM,
    )(permeability, source, ownership, assignment.reshape(1, NSUB), layer_flags.reshape(n_col, LZ))
    mr, ml = send(mr, "col", -1), send(ml, "col", 1)
    stack = call(stack_up, sds(STACK, B, LZ), 3)(base, mr, ml)
    low, high = send(stack, "gx", 1), send(stack, "gx", -1)
    line = jnp.concatenate(
        [low[:HEAD], stack[:HEAD], high[:HEAD], low[SRC + 4 :], stack[SRC:], high[SRC : SRC + 4]],
        axis=0,
    )
    y_lo, y_hi = send(line, "gy", 1, True), send(line, "gy", -1, True)

    weights, labels, chunk, dvals, paths = call(
        functools.partial(first_sums, *sizes),
        [
            sds(6, NP, *FULL), sds(NP, *FULL, dtype=i32), sds(n_bricks, 2, LZ), sds(*plane),
            sds(4, B, LZ),
        ],
        4,
        scratch=[
            vm((NP + 2, *FULL), f32), vm((NP + 1, *FULL), f32), fields, vm((2, *FULL), f32),
            vm((2 * NSUB, LZ), f32),
        ],
    )(y_lo, line, y_hi, flags)
    bricks = lax.all_to_all(chunk, ("gy", "col"), 0, 0, tiled=True)
    parts = call(
        functools.partial(first_coarse, n_bricks, n_gx), sds(n_gx, 2 * B, LZ), 1
    )(bricks)
    parts = lax.all_to_all(parts, "gx", 0, 0, tiled=True)
    tables = [vm((3, B, LZ), f32), vm((3, 3, B, LZ), f32)]
    chunk = call(
        functools.partial(second_sums, *sizes),
        sds(n_bricks, 4, LZ),
        8,
        scratch=[fields, *tables, vm((4, B, LZ), f32), vm((6 * NSUB, LZ), f32)],
    )(parts, weights, labels, y_lo, line, y_hi, dvals, paths)
    images = lax.all_to_all(chunk, ("gy", "col"), 0, 0, tiled=True)
    images = call(
        functools.partial(second_coarse, n_gy, n_col, n_gx), sds(n_gx, 3 * B, LZ), 2
    )(images, bricks)
    images = lax.all_to_all(images, "gx", 0, 0, tiled=True)
    return call(
        functools.partial(last_sweeps, *sizes),
        [sds(*plane), sds(1, B * LZ // (n_gy * n_col))],
        7,
        scratch=[fields, *tables],
    )(parts, images, weights, labels, y_lo, line, y_hi)


def solution(mesh):
    placed = (
        P("gx", "gy", "col"),
        P("gx", "gy", "col"),
        P("gx", "gy", "col"),
        P("gx", "gy", "col", None),
        P(),
    )
    sizes = mesh.shape
    return jax.shard_map(
        functools.partial(on_device, sizes["gx"], sizes["gy"], sizes["col"]),
        mesh=mesh,
        in_specs=placed,
        out_specs=(P("gx", "gy", "col"), P("gx", ("gy", "col"))),
        check_vma=False,
    )
```

```python
import functools

import jax
import jax.numpy as jnp
from jax import lax
from jax.experimental import pallas as pl
from jax.experimental.pallas import tpu as pltpu
from jax.sharding import PartitionSpec as P

f32 = jnp.float32
i32 = jnp.int32
bf16 = jnp.bfloat16
NSUB = 64
B = 8
LZ = 128
NP = 3 * B
W = 9
FULL = (NP, 2 * LZ)
CHUNK = 12
fine_relax = 0.6666667
coarse_relax = 0.7
VMEM_LIMIT = 48 * 1024 * 1024
WHOLE_VMEM = 63 * 1024 * 1024

PERM, OWN, HZ, ASG, SRC = 0, 8, 16, 24, 25
STACK = 33
HEAD = 25
LINE = 3 * HEAD + 2 * B


def lanes(shape):
    return lax.broadcasted_iota(i32, shape, len(shape) - 1)


def rows(shape):
    return lax.broadcasted_iota(i32, shape, len(shape) - 2)


def sds(*shape, dtype=f32):
    return jax.ShapeDtypeStruct(shape, dtype)


def call(kernel, outs, n_in, scratch=(), space=pltpu.VMEM, limit=VMEM_LIMIT):
    single = not isinstance(outs, (list, tuple))
    vm = pl.BlockSpec(memory_space=pltpu.VMEM)
    return pl.pallas_call(
        kernel,
        out_shape=outs,
        in_specs=[pl.BlockSpec(memory_space=space)] * n_in,
        out_specs=vm if single else [vm] * len(outs),
        scratch_shapes=list(scratch),
        compiler_params=pltpu.CompilerParams(vmem_limit_bytes=limit),
    )


def spread(row):
    return jnp.broadcast_to(row, (B, LZ))


def z_messages(perm_in, src_in, own_in, asg_in, flags_in, mr, ml, base, flags_out,
               perm, src, own, asg, flags, sem):
    copies = [
        pltpu.make_async_copy(a, b, sem.at[i])
        for i, (a, b) in enumerate(
            ((perm_in, perm), (src_in, src), (own_in, own), (asg_in, asg), (flags_in, flags))
        )
    ]
    for copy in copies:
        copy.start()
    for copy in copies:
        copy.wait()
    lane = lanes((B, LZ))
    tile = jnp.concatenate([asg[...].astype(f32), jnp.zeros((1, LZ - NSUB), f32)], axis=1)
    tile = jnp.where(rows((B, LZ)) == 0, spread(tile), 0.0)
    for p in range(B):
        k, s, o = perm[p], src[p], own[p].astype(f32)
        base[p], base[B + p], base[2 * B + p] = k, o, s
        mr[p] = jnp.where(
            lane < 16, k, jnp.where(lane < 32, pltpu.roll(o, 16, 1), pltpu.roll(s, 32, 1))
        )
        ml[p] = jnp.where(
            lane >= 112, k, jnp.where(lane >= 96, pltpu.roll(o, 112, 1), pltpu.roll(s, 96, 1))
        )
    base[3 * B] = tile
    mr[B] = tile
    ml[B] = tile
    col, n_col = lax.axis_index("col"), flags_in.shape[0]
    for i, at in enumerate((col - 1, col, col + 1)):
        at = jnp.clip(at, 0, n_col - 1)
        flags_out[pl.ds(i, 1), :] = flags[pl.ds(at, 1), :].astype(f32)


def stack_up(base, mr, ml, stack):
    lane = lanes((B, LZ))
    row = rows((B, LZ))
    for p in range(B):
        stack[PERM + p] = base[p]
        stack[OWN + p] = base[B + p]
        stack[SRC + p] = base[2 * B + p]
        stack[HZ + p] = jnp.where(lane < 64, mr[p], ml[p])
    stack[ASG] = jnp.where(
        row == 1, spread(mr[B, 0:1, :]), jnp.where(row == 2, spread(ml[B, 0:1, :]), base[3 * B])
    )


def around(u_ref, w_ref, p):
    u = u_ref[p + 1]
    return u, (
        (w_ref[0, p] * u_ref[p + 2] + w_ref[1, p] * u_ref[p])
        + (w_ref[2, p] * pltpu.roll(u, NP - 1, 0) + w_ref[3, p] * pltpu.roll(u, 1, 0))
        + (w_ref[4, p] * pltpu.roll(u, 2 * LZ - 1, 1) + w_ref[5, p] * pltpu.roll(u, 1, 1))
    )


def sweeps(both, w_ref, first, last, after=None, operator_at=-1):
    def one_sweep(k, carry):
        now = lax.rem(k, 2)
        src, dst = both.at[now], both.at[1 - now]
        count = NP - 2 * k
        keep = jnp.where(k == operator_at, 1.0, 1.0 - fine_relax)
        give = jnp.where(k == operator_at, -1.0 / fine_relax, 1.0)

        def chunk(i, carry):
            start = jnp.minimum(k + CHUNK * i, k + count - CHUNK)
            moved = []
            for j in range(CHUNK):
                u, near = around(src, w_ref, start + j)
                moved.append(keep * u + give * near)
            for j in range(CHUNK):
                dst[start + j + 1] = moved[j]
            return carry

        lax.fori_loop(0, (count + CHUNK - 1) // CHUNK, chunk, 0)
        if after is not None:
            after(k)
        return carry

    lax.fori_loop(first, last + 1, one_sweep, 0)


def label_sums(groups, sums):
    def one(s, carry):
        for first, labels, fields in groups:
            hits = [tile == s for tile in labels]
            for i, tiles in enumerate(fields):
                parts = [jnp.where(hit, tile, 0.0) for hit, tile in zip(hits, tiles)]
                while len(parts) > 1:
                    parts = [a + b for a, b in zip(parts[::2], parts[1::2])]
                sums[pl.ds(first + i * NSUB + s, 1), :] = jnp.sum(parts[0], axis=0, keepdims=True)
        return carry

    lax.fori_loop(0, NSUB, one, 0, unroll=4)


def lane_sums(sums):
    return lax.dot_general(
        jnp.ones((B, LZ), f32), sums, (((1,), (1,)), ((), ())),
        precision=lax.Precision.HIGHEST, preferred_element_type=f32,
    )


def harmonic(a, b):
    return 2.0 * a * b / (a + b)


def row_product(tile):
    for by in (4, 2, 1):
        tile = tile * pltpu.roll(tile, by, 0)
    return tile


def first_sums(n_gx, n_gy, n_col, y_lo, y_mid, y_hi, flags,
               weights, labels, chunk, dvals, paths, kext, fx, both, masks, sums):
    gx, gy, col = (lax.axis_index(a) for a in ("gx", "gy", "col"))
    lines = (y_lo, y_mid, y_hi)
    lane = lanes((B, LZ))
    row = rows((B, LZ))
    halo = (lane < W) | (lane >= LZ - W)
    near_side = lane < 64

    def positive(t):
        return jnp.where(t > 0.0, t, 1.0)

    def fill(p, carry):
        at = HEAD * (p // B) + lax.rem(p, B)
        for ty in range(3):
            line = lines[ty]
            r = slice(ty * B, (ty + 1) * B)
            packed = line[at + HZ]
            kext[p + 1, r, 0:LZ] = positive(line[at + PERM])
            kext[p + 1, r, LZ:] = positive(jnp.where(halo, packed, 1.0))
            labels[p, r, 0:LZ] = line[at + OWN].astype(i32)
            own_z = jnp.where(near_side, pltpu.roll(packed, LZ - 16, 1), pltpu.roll(packed, 16, 1))
            labels[p, r, LZ:] = jnp.where(halo, own_z, 0.0).astype(i32)
        return carry

    lax.fori_loop(0, NP, fill, 0, unroll=8)
    kext[0] = jnp.ones(FULL, f32)
    kext[NP + 1] = jnp.ones(FULL, f32)

    flag_row = jnp.concatenate(
        [flags[1:2, :], jnp.where(lane[0:1] < 64, flags[2:3, :], flags[0:1, :])], axis=1
    )
    row_all, lane_all = rows(FULL), lanes(FULL)
    wrap_row = jnp.where(gy == 0, B - 1, jnp.where(gy == n_gy - 1, 2 * B - 1, -1))
    masks[0] = jnp.where(row_all == wrap_row, jnp.broadcast_to(flag_row, FULL), 1.0)
    closed = ((lane_all == LZ - 1) & (col == n_col - 1)) | ((lane_all == 2 * LZ - 1) & (col == 0))
    masks[1] = jnp.where(closed, 0.0, 1.0)

    def x_face(p, carry):
        fx[p] = harmonic(kext[p], kext[p + 1])
        return carry

    lax.fori_loop(0, NP + 1, x_face, 0, unroll=5)

    @pl.when(gx == 0)
    def _():
        fx[B] = kext[B + 1]

    @pl.when(gx == n_gx - 1)
    def _():
        fx[2 * B] = kext[2 * B]

    def terms(p, carry):
        b = p // B
        out = ((b == 0) & (gx == 0)) | ((b == 2) & (gx == n_gx - 1))
        k = kext[p + 1]
        fy_up = harmonic(k, pltpu.roll(k, NP - 1, 0)) * masks[0]
        fy_down = pltpu.roll(fy_up, 1, 0)
        fz_right = harmonic(k, pltpu.roll(k, 2 * LZ - 1, 1)) * masks[1]
        fz_left = pltpu.roll(fz_right, 1, 1)
        fx_up, fx_down = fx[p + 1], fx[p]
        diag = fx_up + fx_down + fy_up + fy_down + fz_right + fz_left
        scale = jnp.where(out, 0.0, fine_relax) / diag
        for i, face in enumerate((fx_up, fx_down, fy_up, fy_down, fz_right, fz_left)):
            weights[i, p] = face * scale
        both[0, p + 1] = scale
        dvals[p] = diag[B : 2 * B, 0:LZ]
        return carry

    lax.fori_loop(0, NP, terms, 0, unroll=8)

    def start(i, carry):
        p = i + B // 2
        packed_at = HEAD * (p // B) + HZ + lax.rem(p, B)
        for ty in range(3):
            line = lines[ty]
            r = slice(ty * B, (ty + 1) * B)
            packed = line[packed_at]
            src_z = jnp.where(near_side, pltpu.roll(packed, LZ - 32, 1), pltpu.roll(packed, 32, 1))
            over = both[0, p + 1, r, :] * (1.0 / fine_relax)
            both[1, p + 1, r, 0:LZ] = line[3 * HEAD + i] * over[:, 0:LZ]
            both[1, p + 1, r, LZ:] = jnp.where(halo, src_z, 0.0) * over[:, LZ:]
        return carry

    lax.fori_loop(0, 2 * B, start, 0, unroll=8)
    r = slice(B, 2 * B)
    for q in range(B):
        p = B + q
        up, down = weights[2, p, r, 0:LZ], weights[3, p, r, 0:LZ]
        rise = row_product(jnp.where(row == 0, 1.0, down)) * up
        fall = row_product(jnp.where(row == B - 1, 1.0, up)) * down
        per = dvals[p] * (1.0 / fine_relax)
        paths[2, q : q + 1, :] = (rise * per)[B - 1 : B]
        paths[3, q : q + 1, :] = (fall * per)[0:1]
    rise, fall = fx[2 * B, B : 2 * B, 0:LZ], fx[B, B : 2 * B, 0:LZ]
    for p in range(B + 1, 2 * B):
        rise = rise * weights[1, p, B : 2 * B, 0:LZ]
        fall = fall * weights[0, p - 1, B : 2 * B, 0:LZ]
    paths[0] = rise
    paths[1] = fall

    sweeps(both, weights, 5, 8)
    tiles = [both[1, B + 1 + q, B : 2 * B, 0:LZ] * dvals[B + q] for q in range(B)]
    diag_tiles = [dvals[B + q] for q in range(B)]
    label_tiles = [labels[B + q, B : 2 * B, 0:LZ] for q in range(B)]
    label_sums([(0, label_tiles, (tiles, diag_tiles))], sums)
    totals = lane_sums(sums[...])

    own = spread(y_mid[HEAD + ASG, 0:1, :])
    own = jnp.where(lane < NSUB, own, pltpu.roll(own, NSUB, 1))
    tile = jnp.where(row == 0, totals, own)[0:2]
    for d in range(n_gy * n_col):
        chunk[d] = tile


def one_hot_product(lefts, lows):
    left = jnp.concatenate(lefts, axis=1)
    l1 = left.astype(bf16)
    rest = left - l1.astype(f32)
    l2 = rest.astype(bf16)
    l3 = (rest - l2.astype(f32)).astype(bf16)
    wide = rows((LZ, LZ))
    right = jnp.concatenate(
        [
            jnp.where(jnp.broadcast_to(low, (LZ, LZ)) == wide, 1.0, 0.0).astype(bf16)
            for low in lows
        ],
        axis=1,
    )
    return lax.dot_general(
        jnp.concatenate([l1, l2, l3], axis=0), right, (((1,), (1,)), ((), ())),
        preferred_element_type=f32,
    )


def joined(total):
    n = total.shape[0] // 3
    return (total[2 * n :] + total[n : 2 * n]) + total[:n]


def halves(value, high):
    lane = lanes((B, LZ))
    scaled = jnp.where(high == rows((B, LZ)), value, 0.0)
    return jnp.concatenate(
        [jnp.where(lane < NSUB, scaled, 0.0), jnp.where(lane < NSUB, 0.0, scaled)], axis=0
    )


GROUP = 64


def first_coarse(n_bricks, n_out, values, out):
    def one(i, total):
        lefts, lows = [], []
        for j in range(min(GROUP, n_bricks)):
            value = values[i * min(GROUP, n_bricks) + j]
            a = value[1:2].astype(i32)
            lefts.append(halves(spread(value[0:1]), spread(a >> 7)))
            lows.append(a & 127)
        return total + one_hot_product(lefts, lows)

    total = lax.fori_loop(0, n_bricks // min(GROUP, n_bricks), one, jnp.zeros((6 * B, LZ), f32))
    total = joined(total)
    for d in range(n_out):
        out[d] = total


def second_coarse(n_gy, n_col, n_out, values, first, out):
    n_bricks = n_gy * n_col
    lane = lanes((B, LZ))
    near = lanes((1, LZ)) < NSUB

    def own(j):
        before = lax.rem(j + n_bricks - n_col, n_bricks)
        after = lax.rem(j + n_col, n_bricks)
        mine = spread(values[j, 0:1] + values[before, 2:3])
        return mine + pltpu.roll(spread(values[after, 2:3]), NSUB, 1)

    def one(i, totals):
        lefts, lows, edge_lefts, edge_lows = [], [], [], []
        for j in range(min(GROUP, n_bricks) // 2):
            at = i * min(GROUP, n_bricks) + 2 * j
            pair = jnp.where(lane < NSUB, own(at), pltpu.roll(own(at + 1), NSUB, 1))
            a = jnp.where(near, first[at, 1:2], first[at + 1, 1:2]).astype(i32)
            lefts.append(jnp.where(spread(a >> 7) == rows((B, LZ)), pair, 0.0))
            lows.append(a & 127)
        for j in range(min(GROUP, n_bricks)):
            a = values[i * min(GROUP, n_bricks) + j, 3:4].astype(i32)
            edge_lefts.append(halves(spread(values[i * min(GROUP, n_bricks) + j, 1:2]), spread(a >> 7)))
            edge_lows.append(a & 127)
        return (
            totals[0] + one_hot_product(lefts, lows),
            totals[1] + one_hot_product(edge_lefts, edge_lows),
        )

    mine, edges = lax.fori_loop(
        0, n_bricks // min(GROUP, n_bricks), one, (jnp.zeros((3 * B, LZ), f32), jnp.zeros((6 * B, LZ), f32))
    )
    total = jnp.concatenate([joined(mine), joined(edges)], axis=0)
    for d in range(n_out):
        out[d] = total


def lookup(table, index):
    low, high = index & 127, index >> 7
    result = jnp.zeros((B, LZ), f32)
    for h in range(B):
        got = jnp.take_along_axis(spread(table[h : h + 1]), low, axis=1)
        result = jnp.where(high == h, got, result)
    return result


def pick(row, index):
    return jnp.take_along_axis(spread(row), index, axis=1)


def slab_total(parts, g, n_gx, part, size):
    total = parts[jnp.clip(g, 0, n_gx - 1), part : part + size]
    return jnp.where((g >= 0) & (g < n_gx), total, 0.0)


def guess(parts, g, n_gx):
    total = slab_total(parts, g, n_gx, 0, 2 * B)
    exists = (g >= 0) & (g < n_gx)
    rhs, diag = total[0:B], jnp.where(exists, total[B : 2 * B], 1.0)
    return rhs, diag, coarse_relax * rhs / diag


def expand(coarse, lines, labels, u, tables, first, last):
    near_side = lanes((B, LZ)) < 64

    def table(b, carry):
        for ty in range(3):
            tables[b, ty] = lookup(coarse[b], lines[ty][HEAD * b + ASG].astype(i32))
        return carry

    lax.fori_loop(0, 3, table, 0)

    def one(p, carry):
        b = p // B
        for ty in range(3):
            r = slice(ty * B, (ty + 1) * B)
            t = tables[b, ty]
            u[p + 1, r, 0:LZ] = pick(t[0:1], labels[p, r, 0:LZ])
            lab = labels[p, r, LZ:]
            u[p + 1, r, LZ:] = jnp.where(near_side, pick(t[1:2], lab), pick(t[2:3], lab))
        return carry

    lax.fori_loop(first, last + 1, one, 0, unroll=8)


def second_sums(n_gx, n_gy, n_col, parts, weights, labels, y_lo, y_mid, y_hi, dvals, paths,
                chunk, both, coarse, tables, ends, sums):
    gx = lax.axis_index("gx")
    row = rows((B, LZ))
    r = slice(B, 2 * B)
    for i in range(3):
        coarse[i] = guess(parts, gx + i - 1, n_gx)[2]
    expand(coarse, (y_lo, y_mid, y_hi), labels, both.at[0], tables, 0, NP - 1)

    def after(k):
        @pl.when(k == 0)
        def _():
            first = both.at[1]
            zero = jnp.zeros(FULL, f32)
            first[1] = zero
            first[NP] = zero
            first[:, 0:1, :] = jnp.zeros((NP + 2, 1, 2 * LZ), f32)
            first[:, NP - 1 :, :] = jnp.zeros((NP + 2, 1, 2 * LZ), f32)
            ends[0] = first[B + 1, r, 0:LZ] * -paths[0]
            ends[1] = first[2 * B, r, 0:LZ] * -paths[1]
            for q in range(B):
                plane = first[B + 1 + q, r, 0:LZ]
                ends[2, q : q + 1, :] = plane[0:1] * -paths[2, q : q + 1, :]
                ends[3, q : q + 1, :] = plane[B - 1 : B] * -paths[3, q : q + 1, :]

    sweeps(both, weights, 0, 8, after=after, operator_at=4)
    tiles = [both[1, B + 1 + q, r, 0:LZ] * dvals[B + q] for q in range(B)]
    label_tiles = [labels[B + q, r, 0:LZ] for q in range(B)]
    beyond = [labels[2 * B, r, 0:LZ], labels[B - 1, r, 0:LZ]]
    for at in (2 * B, B - 1):
        edge = labels[B, at : at + 1, 0:LZ]
        edge = spread(edge)
        for q in range(1, B):
            edge = jnp.where(row == q, spread(labels[B + q, at : at + 1, 0:LZ]), edge)
        beyond.append(edge)
    groups = [(0, label_tiles, (tiles,))]
    groups += [((2 + i) * NSUB, [beyond[i]], ([ends[i]],)) for i in range(4)]
    sums[NSUB : 2 * NSUB, :] = jnp.zeros((NSUB, LZ), f32)
    label_sums(groups, sums)
    totals = lane_sums(sums[...])
    right, left = (spread(y_mid[HEAD * b + ASG, 0:1, :]) for b in (2, 0))
    asg = jnp.where(lanes((B, LZ)) < NSUB, right, pltpu.roll(left, NSUB, 1))
    tile = jnp.where(
        row < 2,
        jnp.where(row == 0, totals[:, 0:LZ], totals[:, LZ : 2 * LZ]),
        jnp.where(row == 2, totals[:, 2 * LZ :], asg),
    )[0:4]
    for d in range(n_gy * n_col):
        chunk[d] = tile


def last_sweeps(n_gx, n_gy, n_col, parts, images, weights, labels, y_lo, y_mid, y_hi,
                pressure, coarse_out, both, coarse, tables):
    gx, gy, col = (lax.axis_index(a) for a in ("gx", "gy", "col"))
    for i in range(3):
        g = gx + i - 1
        rhs, diag, start = guess(parts, g, n_gx)
        image = (
            slab_total(images, g, n_gx, 0, B)
            + slab_total(images, g - 1, n_gx, B, B)
            + slab_total(images, g + 1, n_gx, 2 * B, B)
        )
        second = start + coarse_relax * (rhs - image) / diag
        coarse[i] = jnp.where((g >= 0) & (g < n_gx), second, 0.0)
    share = B * LZ // (n_gy * n_col)
    per_row = LZ // share
    mine = gy * n_col + col
    row = coarse[1, pl.ds(mine // per_row, 1), :]
    turned = pltpu.roll(spread(row), lax.rem(LZ - lax.rem(mine, per_row) * share, LZ), 1)
    coarse_out[...] = turned[0:1, 0:share]
    expand(coarse, (y_lo, y_mid, y_hi), labels, both.at[1], tables, 4, 19)
    sweeps(both, weights, 5, 8)
    for q in range(B):
        pressure[q] = both[1, B + 1 + q, B : 2 * B, 0:LZ]


def steps(count, by, wrap):
    return [
        (i, (i + by) % count) for i in range(count) if wrap or 0 <= i + by < count
    ]


def on_device(n_gx, n_gy, n_col, permeability, source, ownership, assignment, layer_flags):
    n_bricks = n_gy * n_col
    sizes = (n_gx, n_gy, n_col)
    vm = pltpu.VMEM
    fields = vm((2, NP + 2, *FULL), f32)
    plane = (B, B, LZ)

    def send(x, axis, by, wrap=False):
        return lax.ppermute(x, axis, steps(lax.axis_size(axis), by, wrap))

    mr, ml, base, flags = call(
        z_messages,
        [sds(B + 1, B, LZ)] * 2 + [sds(3 * B + 1, B, LZ), sds(3, LZ)],
        5,
        scratch=[
            vm(plane, f32), vm(plane, f32), vm(plane, i32), vm((1, NSUB), i32),
            vm((n_col, LZ), i32), pltpu.SemaphoreType.DMA((5,)),
        ],
        space=pl.ANY,
        limit=WHOLE_VMEM,
    )(permeability, source, ownership, assignment.reshape(1, NSUB), layer_flags.reshape(n_col, LZ))
    mr, ml = send(mr, "col", -1), send(ml, "col", 1)
    stack = call(stack_up, sds(STACK, B, LZ), 3)(base, mr, ml)
    low, high = send(stack, "gx", 1), send(stack, "gx", -1)
    line = jnp.concatenate(
        [low[:HEAD], stack[:HEAD], high[:HEAD], low[SRC + 4 :], stack[SRC:], high[SRC : SRC + 4]],
        axis=0,
    )
    y_lo, y_hi = send(line, "gy", 1, True), send(line, "gy", -1, True)

    weights, labels, chunk, dvals, paths = call(
        functools.partial(first_sums, *sizes),
        [
            sds(6, NP, *FULL), sds(NP, *FULL, dtype=i32), sds(n_bricks, 2, LZ), sds(NP, B, LZ),
            sds(4, B, LZ),
        ],
        4,
        scratch=[
            vm((NP + 2, *FULL), f32), vm((NP + 1, *FULL), f32), fields, vm((2, *FULL), f32),
            vm((2 * NSUB, LZ), f32),
        ],
    )(y_lo, line, y_hi, flags)
    bricks = lax.all_to_all(chunk, ("gy", "col"), 0, 0, tiled=True)
    parts = call(
        functools.partial(first_coarse, n_bricks, n_gx), sds(n_gx, 2 * B, LZ), 1
    )(bricks)
    parts = lax.all_to_all(parts, "gx", 0, 0, tiled=True)
    tables = [vm((3, B, LZ), f32), vm((3, 3, B, LZ), f32)]
    chunk = call(
        functools.partial(second_sums, *sizes),
        sds(n_bricks, 4, LZ),
        8,
        scratch=[fields, *tables, vm((4, B, LZ), f32), vm((6 * NSUB, LZ), f32)],
    )(parts, weights, labels, y_lo, line, y_hi, dvals, paths)
    images = lax.all_to_all(chunk, ("gy", "col"), 0, 0, tiled=True)
    images = call(
        functools.partial(second_coarse, n_gy, n_col, n_gx), sds(n_gx, 3 * B, LZ), 2
    )(images, bricks)
    images = lax.all_to_all(images, "gx", 0, 0, tiled=True)
    return call(
        functools.partial(last_sweeps, *sizes),
        [sds(*plane), sds(1, B * LZ // (n_gy * n_col))],
        7,
        scratch=[fields, *tables],
    )(parts, images, weights, labels, y_lo, line, y_hi)


def solution(mesh):
    placed = (
        P("gx", "gy", "col"),
        P("gx", "gy", "col"),
        P("gx", "gy", "col"),
        P("gx", "gy", "col", None),
        P(),
    )
    sizes = mesh.shape
    return jax.shard_map(
        functools.partial(on_device, sizes["gx"], sizes["gy"], sizes["col"]),
        mesh=mesh,
        in_specs=placed,
        out_specs=(P("gx", "gy", "col"), P("gx", ("gy", "col"))),
        check_vma=False,
    )
```

```python
import functools

import jax
import jax.numpy as jnp
from jax import lax
from jax.experimental import pallas as pl
from jax.experimental.pallas import tpu as pltpu
from jax.sharding import PartitionSpec as P

f32 = jnp.float32
i32 = jnp.int32
bf16 = jnp.bfloat16
NSUB = 64
B = 8
LZ = 128
NP = 3 * B
W = 9
FULL = (NP, 2 * LZ)
FILL_UNROLL = 8
CHUNK = 12
fine_relax = 0.6666667
coarse_relax = 0.7
VMEM_LIMIT = 48 * 1024 * 1024
WHOLE_VMEM = 63 * 1024 * 1024

PERM, OWN, HZ, ASG, SRC = 0, 8, 16, 20, 21
STACK = 29

FOLDS = [(p, None, 0) for p in range(7, 17)]
FOLDS += [(6, 0, 1), (5, 1, 2), (4, 2, 3), (17, 23, 1), (18, 22, 2), (19, 21, 3), (3, 20, 4)]
FOLD_OF = {}
for _at, (_main, _other, _rows) in enumerate(FOLDS):
    FOLD_OF[_main] = (_at, 0)
    if _other is not None:
        FOLD_OF[_other] = (_at, _rows)
N_FOLD = len(FOLDS)
M_PERM, M_OWN, M_HZ, M_ASG, M_SRC = 0, N_FOLD, 2 * N_FOLD, 2 * N_FOLD + 12, 2 * N_FOLD + 13
SRC_FOLDS = [(8 + q, ((12 + q, 4, 4),)) for q in range(4)]
SRC_FOLDS += [(7, ((6, 2, 2), (5, 1, 3))), (16, ((17, 2, 2), (18, 1, 3)))]
SRC_OF = {}
for _at, (_main, _others) in enumerate(SRC_FOLDS):
    SRC_OF[_main] = (_at, 0)
    for _other, _rows, _top in _others:
        SRC_OF[_other] = (_at, _top)
MESSAGE = M_SRC + len(SRC_FOLDS)


def lanes(shape):
    return lax.broadcasted_iota(i32, shape, len(shape) - 1)


def rows(shape):
    return lax.broadcasted_iota(i32, shape, len(shape) - 2)


def sds(*shape, dtype=f32):
    return jax.ShapeDtypeStruct(shape, dtype)


def call(kernel, outs, n_in, scratch=(), space=pltpu.VMEM, limit=VMEM_LIMIT, cost=None):
    single = not isinstance(outs, (list, tuple))
    vm = pl.BlockSpec(memory_space=pltpu.VMEM)
    return pl.pallas_call(
        kernel,
        out_shape=outs,
        in_specs=[pl.BlockSpec(memory_space=space)] * n_in,
        out_specs=vm if single else [vm] * len(outs),
        scratch_shapes=list(scratch),
        compiler_params=pltpu.CompilerParams(vmem_limit_bytes=limit),
        cost_estimate=cost,
    )


def spread(row):
    return jnp.broadcast_to(row, (B, LZ))


def asg_tile(asg):
    tile = jnp.concatenate([asg[...].astype(f32), jnp.zeros((1, LZ - NSUB), f32)], axis=1)
    return jnp.where(rows((B, LZ)) == 0, spread(tile), 0.0)


def z_messages(perm_in, src_in, own_in, asg_in, mr, ml, perm, src, own, asg, sem):
    copies = [
        pltpu.make_async_copy(a, b, sem.at[i])
        for i, (a, b) in enumerate(
            ((perm_in, perm), (src_in, src), (own_in, own), (asg_in, asg))
        )
    ]
    for copy in copies:
        copy.start()
    for copy in copies:
        copy.wait()
    lane = lanes((B, LZ))

    def first_cells(q):
        k, s, o = perm[q], src[q], own[q].astype(f32)
        return jnp.where(
            lane < 9, k, jnp.where(lane < 18, pltpu.roll(o, 9, 1), pltpu.roll(s, 18, 1))
        )

    def last_cells(q):
        k, s, o = perm[q], src[q], own[q].astype(f32)
        return jnp.where(
            lane >= 55,
            pltpu.roll(k, 64, 1),
            jnp.where(lane >= 46, pltpu.roll(o, 55, 1), pltpu.roll(s, 46, 1)),
        )

    for out, cells in ((mr, first_cells), (ml, last_cells)):
        for q in range(B // 2):
            out[q] = jnp.where(lane < 64, cells(q), pltpu.roll(cells(q + B // 2), 64, 1))
        out[B // 2] = asg_tile(asg)


def own_stack(perm, src, own, asg, flags, base, flags_out):
    for q in range(B):
        base[q], base[B + q], base[2 * B + q] = perm[q], own[q].astype(f32), src[q]
    base[3 * B] = asg_tile(asg)
    col, n_col = lax.axis_index("col"), flags.shape[0]
    for i, at in enumerate((col - 1, col, col + 1)):
        at = jnp.clip(at, 0, n_col - 1)
        flags_out[pl.ds(i, 1), :] = flags[pl.ds(at, 1), :].astype(f32)


def stack_up(base, mr, ml, stack):
    lane = lanes((B, LZ))
    row = rows((B, LZ))
    for q in range(B):
        stack[PERM + q] = base[q]
        stack[OWN + q] = base[B + q]
        stack[SRC + q] = base[2 * B + q]
    for q in range(B // 2):
        stack[HZ + q] = jnp.where((lane & 63) < 32, mr[q], ml[q])
    at = B // 2
    stack[ASG] = jnp.where(
        row == 1, spread(mr[at, 0:1, :]), jnp.where(row == 2, spread(ml[at, 0:1, :]), base[3 * B])
    )


def y_messages(low, mid, high, up, down):
    stacks = (low, mid, high)
    row = rows((B, LZ))
    lane = lanes((B, LZ))

    def fold(main, other, n, top, upward):
        if upward:
            return jnp.where((row >= top - n) & (row < top), pltpu.roll(other, top, 0), main)
        return jnp.where(
            (row >= B - top) & (row < B - top + n), pltpu.roll(other, B - top, 0), main
        )

    for out, upward in ((up, True), (down, False)):
        for field, first in ((PERM, M_PERM), (OWN, M_OWN)):
            for at, (main, other, n) in enumerate(FOLDS):
                tile = stacks[main // B][field + main % B]
                if other is not None:
                    tile = fold(tile, stacks[other // B][field + other % B], n, n, upward)
                out[first + at] = tile
        for b in range(3):
            for q in range(B // 2):
                out[M_HZ + 4 * b + q] = stacks[b][HZ + q]
        for at, (main, others) in enumerate(SRC_FOLDS):
            tile = stacks[main // B][SRC + main % B]
            for other, n, top in others:
                tile = fold(tile, stacks[other // B][SRC + other % B], n, top, upward)
            out[M_SRC + at] = tile
        sides = jnp.where(lane < NSUB, low[ASG], pltpu.roll(high[ASG], NSUB, 1))
        out[M_ASG] = jnp.where(row < 3, sides, pltpu.roll(mid[ASG], 3, 0))


def line_asg(stacks, below, above, ty, b):
    if ty == 1:
        return stacks[b][ASG]
    tile = (below if ty == 0 else above)[M_ASG]
    return (tile, pltpu.roll(tile, 5, 0), pltpu.roll(tile, NSUB, 1))[b]


def around(u_ref, w_ref, p):
    u = u_ref[p + 1]
    return u, (
        (w_ref[0, p] * u_ref[p + 2] + w_ref[1, p] * u_ref[p])
        + (w_ref[2, p] * pltpu.roll(u, NP - 1, 0) + w_ref[3, p] * pltpu.roll(u, 1, 0))
        + (w_ref[4, p] * pltpu.roll(u, 2 * LZ - 1, 1) + w_ref[5, p] * pltpu.roll(u, 1, 1))
    )


def sweeps(both, w_ref, first, last, after=None, operator_at=-1):
    def one_sweep(k, carry):
        now = lax.rem(k, 2)
        src, dst = both.at[now], both.at[1 - now]
        count = NP - 2 * k
        keep = jnp.where(k == operator_at, 1.0, 1.0 - fine_relax)
        give = jnp.where(k == operator_at, -1.0 / fine_relax, 1.0)

        def chunk(i, carry):
            start = jnp.minimum(k + CHUNK * i, k + count - CHUNK)
            moved = []
            for j in range(CHUNK):
                u, near = around(src, w_ref, start + j)
                moved.append(keep * u + give * near)
            for j in range(CHUNK):
                dst[start + j + 1] = moved[j]
            return carry

        lax.fori_loop(0, (count + CHUNK - 1) // CHUNK, chunk, 0)
        if after is not None:
            after(k)
        return carry

    lax.fori_loop(first, last + 1, one_sweep, 0)


def label_sums(groups, sums):
    def one(s, carry):
        for first, labels, fields in groups:
            hits = [tile == s for tile in labels]
            for i, tiles in enumerate(fields):
                parts = [jnp.where(hit, tile, 0.0) for hit, tile in zip(hits, tiles)]
                while len(parts) > 1:
                    parts = [a + b for a, b in zip(parts[::2], parts[1::2])]
                sums[pl.ds(first + i * NSUB + s, 1), :] = jnp.sum(parts[0], axis=0, keepdims=True)
        return carry

    lax.fori_loop(0, NSUB, one, 0, unroll=4)


def lane_sums(sums):
    return lax.dot_general(
        jnp.ones((B, LZ), f32), sums, (((1,), (1,)), ((), ())),
        precision=lax.Precision.HIGHEST, preferred_element_type=f32,
    )


def harmonic(a, b):
    return 2.0 * a * b / (a + b)


def row_product(tile):
    for by in (4, 2, 1):
        tile = tile * pltpu.roll(tile, by, 0)
    return tile


def positive(t):
    return jnp.where(t > 0.0, t, 1.0)


def near_and_far(tile, q):
    turned = pltpu.roll(tile, 64, 1)
    return jnp.where(q < 4, tile, turned), jnp.where(q < 4, turned, tile)


def halo_values(near, far):
    lane = lanes((B, LZ))
    near_side = lane < 64
    halo = (lane < W) | (lane >= LZ - W)
    source_halo = (lane < 4) | (lane >= LZ - 4)
    k = positive(jnp.where(halo, jnp.where(near_side, near, far), 1.0))
    own = jnp.where(near_side, pltpu.roll(near, LZ - 9, 1), pltpu.roll(near, 73, 1))
    src = jnp.where(near_side, pltpu.roll(near, LZ - 18, 1), pltpu.roll(near, 82, 1))
    return k, jnp.where(halo, own, 0.0).astype(i32), jnp.where(source_halo, src, 0.0)


def own_rows(low, mid, high, kmid, lmid, smid):
    for p in range(NP):
        stack, q = (low, mid, high)[p // B], p % B
        k, label, src = halo_values(*near_and_far(stack[HZ + q % 4], q))
        kmid[p, :, 0:LZ] = positive(stack[PERM + q])
        kmid[p, :, LZ:] = k
        lmid[p, :, 0:LZ] = stack[OWN + q].astype(i32)
        lmid[p, :, LZ:] = label
        if 4 <= p < 20:
            smid[p - 4, :, 0:LZ] = stack[SRC + q]
            smid[p - 4, :, LZ:] = src


def first_sums(n_gx, n_gy, n_col, low, mid, high, below, above, flags, kmid, lmid, smid,
               weights, labels, chunk, dvals, paths, asg, kext, fx, both, masks, sums):
    gx, gy, col = (lax.axis_index(a) for a in ("gx", "gy", "col"))
    mids = (low, mid, high)
    lane = lanes((B, LZ))
    row = rows((B, LZ))
    def unfolded(ty, first, place):
        at, n = place
        tile = (below if ty == 0 else above)[first + at]
        return pltpu.roll(tile, (B - n if ty == 0 else n) % B, 0) if n else tile

    def beyond(ty, p):
        b, q = p // B, lax.rem(p, B)
        tile = (below if ty == 0 else above)[M_HZ + 4 * b + lax.rem(q, 4)]
        return halo_values(*near_and_far(tile, q))

    def fill(p, carry):
        kext[p + 1, B : 2 * B, :] = kmid[p]
        labels[p, B : 2 * B, :] = lmid[p]
        for ty in (0, 2):
            r = slice(ty * B, (ty + 1) * B)
            kext[p + 1, r, LZ:], labels[p, r, LZ:], _ = beyond(ty, p)
        return carry

    lax.fori_loop(0, NP, fill, 0, unroll=FILL_UNROLL)
    for p in range(NP):
        for ty in (0, 2):
            r = slice(ty * B, (ty + 1) * B)
            kext[p + 1, r, 0:LZ] = positive(unfolded(ty, M_PERM, FOLD_OF[p]))
            labels[p, r, 0:LZ] = unfolded(ty, M_OWN, FOLD_OF[p]).astype(i32)
    for b in range(3):
        for ty in range(3):
            asg[b, ty] = line_asg(mids, below, above, ty, b).astype(i32)
    kext[0] = jnp.ones(FULL, f32)
    kext[NP + 1] = jnp.ones(FULL, f32)

    flag_row = jnp.concatenate(
        [flags[1:2, :], jnp.where(lane[0:1] < 64, flags[2:3, :], flags[0:1, :])], axis=1
    )
    row_all, lane_all = rows(FULL), lanes(FULL)
    wrap_row = jnp.where(gy == 0, B - 1, jnp.where(gy == n_gy - 1, 2 * B - 1, -1))
    masks[0] = jnp.where(row_all == wrap_row, jnp.broadcast_to(flag_row, FULL), 1.0)
    closed = ((lane_all == LZ - 1) & (col == n_col - 1)) | ((lane_all == 2 * LZ - 1) & (col == 0))
    masks[1] = jnp.where(closed, 0.0, 1.0)

    def x_face(p, carry):
        fx[p] = harmonic(kext[p], kext[p + 1])
        return carry

    lax.fori_loop(0, NP + 1, x_face, 0, unroll=5)

    @pl.when(gx == 0)
    def _():
        fx[B] = kext[B + 1]

    @pl.when(gx == n_gx - 1)
    def _():
        fx[2 * B] = kext[2 * B]

    def terms(p, carry):
        b = p // B
        out = ((b == 0) & (gx == 0)) | ((b == 2) & (gx == n_gx - 1))
        k = kext[p + 1]
        fy_up = harmonic(k, pltpu.roll(k, NP - 1, 0)) * masks[0]
        fy_down = pltpu.roll(fy_up, 1, 0)
        fz_right = harmonic(k, pltpu.roll(k, 2 * LZ - 1, 1)) * masks[1]
        fz_left = pltpu.roll(fz_right, 1, 1)
        fx_up, fx_down = fx[p + 1], fx[p]
        diag = fx_up + fx_down + fy_up + fy_down + fz_right + fz_left
        scale = jnp.where(out, 0.0, fine_relax) / diag
        for i, face in enumerate((fx_up, fx_down, fy_up, fy_down, fz_right, fz_left)):
            weights[i, p] = face * scale
        both[0, p + 1] = scale
        dvals[p] = diag[B : 2 * B, 0:LZ]
        return carry

    lax.fori_loop(0, NP, terms, 0, unroll=8)


    def start(i, carry):
        p = i + B // 2
        over = both[0, p + 1] * (1.0 / fine_relax)
        both[1, p + 1, B : 2 * B, :] = smid[i] * over[B : 2 * B]
        for ty in (0, 2):
            r = slice(ty * B, (ty + 1) * B)
            both[1, p + 1, r, LZ:] = beyond(ty, p)[2] * over[r, LZ:]
        return carry

    lax.fori_loop(0, 2 * B, start, 0, unroll=8)
    for p in range(B // 2, NP - B // 2):
        for ty in (0, 2):
            r = slice(ty * B, (ty + 1) * B)
            if p in SRC_OF:
                over = both[0, p + 1, r, 0:LZ] * (1.0 / fine_relax)
                both[1, p + 1, r, 0:LZ] = unfolded(ty, M_SRC, SRC_OF[p]) * over
            else:
                both[1, p + 1, r, 0:LZ] = jnp.zeros((B, LZ), f32)

    r = slice(B, 2 * B)
    for q in range(B):
        p = B + q
        up, down = weights[2, p, r, 0:LZ], weights[3, p, r, 0:LZ]
        rise = row_product(jnp.where(row == 0, 1.0, down)) * up
        fall = row_product(jnp.where(row == B - 1, 1.0, up)) * down
        per = dvals[p] * (1.0 / fine_relax)
        paths[2, q : q + 1, :] = (rise * per)[B - 1 : B]
        paths[3, q : q + 1, :] = (fall * per)[0:1]
    rise, fall = fx[2 * B, B : 2 * B, 0:LZ], fx[B, B : 2 * B, 0:LZ]
    for p in range(B + 1, 2 * B):
        rise = rise * weights[1, p, B : 2 * B, 0:LZ]
        fall = fall * weights[0, p - 1, B : 2 * B, 0:LZ]
    paths[0] = rise
    paths[1] = fall

    sweeps(both, weights, 5, 8)
    tiles = [both[1, B + 1 + q, B : 2 * B, 0:LZ] * dvals[B + q] for q in range(B)]
    diag_tiles = [dvals[B + q] for q in range(B)]
    label_tiles = [labels[B + q, B : 2 * B, 0:LZ] for q in range(B)]
    label_sums([(0, label_tiles, (tiles, diag_tiles))], sums)
    totals = lane_sums(sums[...])

    own = spread(mid[ASG, 0:1, :])
    own = jnp.where(lane < NSUB, own, pltpu.roll(own, NSUB, 1))
    tile = jnp.where(row == 0, totals, own)[0:2]
    for d in range(n_gy * n_col):
        chunk[d] = tile


def one_hot_product(lefts, lows):
    left = jnp.concatenate(lefts, axis=1)
    l1 = left.astype(bf16)
    rest = left - l1.astype(f32)
    l2 = rest.astype(bf16)
    l3 = (rest - l2.astype(f32)).astype(bf16)
    wide = rows((LZ, LZ))
    right = jnp.concatenate(
        [
            jnp.where(jnp.broadcast_to(low, (LZ, LZ)) == wide, 1.0, 0.0).astype(bf16)
            for low in lows
        ],
        axis=1,
    )
    return lax.dot_general(
        jnp.concatenate([l1, l2, l3], axis=0), right, (((1,), (1,)), ((), ())),
        preferred_element_type=f32,
    )


def joined(total):
    n = total.shape[0] // 3
    return (total[2 * n :] + total[n : 2 * n]) + total[:n]


def halves(value, high):
    lane = lanes((B, LZ))
    scaled = jnp.where(high == rows((B, LZ)), value, 0.0)
    return jnp.concatenate(
        [jnp.where(lane < NSUB, scaled, 0.0), jnp.where(lane < NSUB, 0.0, scaled)], axis=0
    )


GROUP = 64


def first_coarse(n_bricks, n_out, values, out):
    def one(i, total):
        lefts, lows = [], []
        for j in range(min(GROUP, n_bricks)):
            value = values[i * min(GROUP, n_bricks) + j]
            a = value[1:2].astype(i32)
            lefts.append(halves(spread(value[0:1]), spread(a >> 7)))
            lows.append(a & 127)
        return total + one_hot_product(lefts, lows)

    total = lax.fori_loop(0, n_bricks // min(GROUP, n_bricks), one, jnp.zeros((6 * B, LZ), f32))
    total = joined(total)
    for d in range(n_out):
        out[d] = total


def second_coarse(n_gy, n_col, n_out, values, first, out):
    n_bricks = n_gy * n_col
    lane = lanes((B, LZ))
    near = lanes((1, LZ)) < NSUB

    def own(j):
        before = lax.rem(j + n_bricks - n_col, n_bricks)
        after = lax.rem(j + n_col, n_bricks)
        mine = spread(values[j, 0:1] + values[before, 2:3])
        return mine + pltpu.roll(spread(values[after, 2:3]), NSUB, 1)

    def one(i, totals):
        lefts, lows, edge_lefts, edge_lows = [], [], [], []
        for j in range(min(GROUP, n_bricks) // 2):
            at = i * min(GROUP, n_bricks) + 2 * j
            pair = jnp.where(lane < NSUB, own(at), pltpu.roll(own(at + 1), NSUB, 1))
            a = jnp.where(near, first[at, 1:2], first[at + 1, 1:2]).astype(i32)
            lefts.append(jnp.where(spread(a >> 7) == rows((B, LZ)), pair, 0.0))
            lows.append(a & 127)
        for j in range(min(GROUP, n_bricks)):
            a = values[i * min(GROUP, n_bricks) + j, 3:4].astype(i32)
            edge_lefts.append(halves(spread(values[i * min(GROUP, n_bricks) + j, 1:2]), spread(a >> 7)))
            edge_lows.append(a & 127)
        return (
            totals[0] + one_hot_product(lefts, lows),
            totals[1] + one_hot_product(edge_lefts, edge_lows),
        )

    mine, edges = lax.fori_loop(
        0, n_bricks // min(GROUP, n_bricks), one, (jnp.zeros((3 * B, LZ), f32), jnp.zeros((6 * B, LZ), f32))
    )
    total = jnp.concatenate([joined(mine), joined(edges)], axis=0)
    for d in range(n_out):
        out[d] = total


def lookup(table, index):
    low, high = index & 127, index >> 7
    result = jnp.zeros((B, LZ), f32)
    for h in range(B):
        got = jnp.take_along_axis(spread(table[h : h + 1]), low, axis=1)
        result = jnp.where(high == h, got, result)
    return result


def pick(row, index):
    return jnp.take_along_axis(spread(row), index, axis=1)


def slab_total(parts, g, n_gx, part, size):
    total = parts[jnp.clip(g, 0, n_gx - 1), part : part + size]
    return jnp.where((g >= 0) & (g < n_gx), total, 0.0)


def guess(parts, g, n_gx):
    total = slab_total(parts, g, n_gx, 0, 2 * B)
    exists = (g >= 0) & (g < n_gx)
    rhs, diag = total[0:B], jnp.where(exists, total[B : 2 * B], 1.0)
    return rhs, diag, coarse_relax * rhs / diag


def expand(coarse, asg, labels, u, tables, first, last):
    near_side = lanes((B, LZ)) < 64

    def table(i, carry):
        b, ty = i // 3, lax.rem(i, 3)
        tables[b, ty] = lookup(coarse[b], asg[b, ty])
        return carry

    lax.fori_loop(0, 9, table, 0, unroll=3)

    def one(p, carry):
        b = p // B
        for ty in range(3):
            r = slice(ty * B, (ty + 1) * B)
            t = tables[b, ty]
            u[p + 1, r, 0:LZ] = pick(t[0:1], labels[p, r, 0:LZ])
            lab = labels[p, r, LZ:]
            u[p + 1, r, LZ:] = jnp.where(near_side, pick(t[1:2], lab), pick(t[2:3], lab))
        return carry

    lax.fori_loop(first, last + 1, one, 0, unroll=8)


def second_sums(n_gx, n_gy, n_col, parts, weights, labels, asg, dvals, paths,
                chunk, both, coarse, tables, ends, sums):
    gx = lax.axis_index("gx")
    row = rows((B, LZ))
    r = slice(B, 2 * B)
    for i in range(3):
        coarse[i] = guess(parts, gx + i - 1, n_gx)[2]
    expand(coarse, asg, labels, both.at[0], tables, 0, NP - 1)

    def after(k):
        @pl.when(k == 0)
        def _():
            first = both.at[1]
            zero = jnp.zeros(FULL, f32)
            first[1] = zero
            first[NP] = zero
            first[:, 0:1, :] = jnp.zeros((NP + 2, 1, 2 * LZ), f32)
            first[:, NP - 1 :, :] = jnp.zeros((NP + 2, 1, 2 * LZ), f32)
            ends[0] = first[B + 1, r, 0:LZ] * -paths[0]
            ends[1] = first[2 * B, r, 0:LZ] * -paths[1]
            for q in range(B):
                plane = first[B + 1 + q, r, 0:LZ]
                ends[2, q : q + 1, :] = plane[0:1] * -paths[2, q : q + 1, :]
                ends[3, q : q + 1, :] = plane[B - 1 : B] * -paths[3, q : q + 1, :]

    sweeps(both, weights, 0, 8, after=after, operator_at=4)
    tiles = [both[1, B + 1 + q, r, 0:LZ] * dvals[B + q] for q in range(B)]
    label_tiles = [labels[B + q, r, 0:LZ] for q in range(B)]
    beyond = [labels[2 * B, r, 0:LZ], labels[B - 1, r, 0:LZ]]
    for at in (2 * B, B - 1):
        edge = labels[B, at : at + 1, 0:LZ]
        edge = spread(edge)
        for q in range(1, B):
            edge = jnp.where(row == q, spread(labels[B + q, at : at + 1, 0:LZ]), edge)
        beyond.append(edge)
    groups = [(0, label_tiles, (tiles,))]
    groups += [((2 + i) * NSUB, [beyond[i]], ([ends[i]],)) for i in range(4)]
    sums[NSUB : 2 * NSUB, :] = jnp.zeros((NSUB, LZ), f32)
    label_sums(groups, sums)
    totals = lane_sums(sums[...])
    right, left = (spread(asg[b, 1, 0:1, :].astype(f32)) for b in (2, 0))
    sides = jnp.where(lanes((B, LZ)) < NSUB, right, pltpu.roll(left, NSUB, 1))
    tile = jnp.where(
        row < 2,
        jnp.where(row == 0, totals[:, 0:LZ], totals[:, LZ : 2 * LZ]),
        jnp.where(row == 2, totals[:, 2 * LZ :], sides),
    )[0:4]
    for d in range(n_gy * n_col):
        chunk[d] = tile


def last_sweeps(n_gx, n_gy, n_col, parts, images, weights, labels, asg,
                pressure, coarse_out, both, coarse, tables):
    gx, gy, col = (lax.axis_index(a) for a in ("gx", "gy", "col"))
    for i in range(3):
        g = gx + i - 1
        rhs, diag, start = guess(parts, g, n_gx)
        image = (
            slab_total(images, g, n_gx, 0, B)
            + slab_total(images, g - 1, n_gx, B, B)
            + slab_total(images, g + 1, n_gx, 2 * B, B)
        )
        second = start + coarse_relax * (rhs - image) / diag
        coarse[i] = jnp.where((g >= 0) & (g < n_gx), second, 0.0)
    share = B * LZ // (n_gy * n_col)
    per_row = LZ // share
    mine = gy * n_col + col
    row = coarse[1, pl.ds(mine // per_row, 1), :]
    turned = pltpu.roll(spread(row), lax.rem(LZ - lax.rem(mine, per_row) * share, LZ), 1)
    coarse_out[...] = turned[0:1, 0:share]
    expand(coarse, asg, labels, both.at[1], tables, 4, 19)
    sweeps(both, weights, 5, 8)
    for q in range(B):
        pressure[q] = both[1, B + 1 + q, B : 2 * B, 0:LZ]


def steps(count, by, wrap):
    return [
        (i, (i + by) % count) for i in range(count) if wrap or 0 <= i + by < count
    ]


def on_device(n_gx, n_gy, n_col, permeability, source, ownership, assignment, layer_flags):
    n_bricks = n_gy * n_col
    sizes = (n_gx, n_gy, n_col)
    vm = pltpu.VMEM
    fields = vm((2, NP + 2, *FULL), f32)
    plane = (B, B, LZ)

    def send(x, axis, by, wrap=False):
        return lax.ppermute(x, axis, steps(lax.axis_size(axis), by, wrap))

    assigned, flags = assignment.reshape(1, NSUB), layer_flags.reshape(n_col, LZ)
    mr, ml = call(
        z_messages,
        [sds(B // 2 + 1, B, LZ)] * 2,
        4,
        scratch=[
            vm(plane, f32), vm(plane, f32), vm(plane, i32), vm((1, NSUB), i32),
            pltpu.SemaphoreType.DMA((4,)),
        ],
        space=pl.ANY,
        limit=WHOLE_VMEM,
    )(permeability, source, ownership, assigned)
    mr, ml = send(mr, "col", -1), send(ml, "col", 1)
    base, flags = call(
        own_stack,
        [sds(3 * B + 1, B, LZ), sds(3, LZ)],
        5,
        cost=pl.CostEstimate(flops=100000, bytes_accessed=300000, transcendentals=0),
    )(permeability, source, ownership, assigned, flags)
    mid = call(stack_up, sds(STACK, B, LZ), 3)(base, mr, ml)
    low, high = send(mid, "gx", 1), send(mid, "gx", -1)
    up, down = call(y_messages, [sds(MESSAGE, B, LZ)] * 2, 3)(low, mid, high)
    below, above = send(up, "gy", 1, True), send(down, "gy", -1, True)
    middle = call(
        own_rows,
        [sds(NP, B, 2 * LZ), sds(NP, B, 2 * LZ, dtype=i32), sds(2 * B, B, 2 * LZ)],
        3,
        cost=pl.CostEstimate(flops=1000000, bytes_accessed=1000000, transcendentals=0),
    )(low, mid, high)

    weights, labels, chunk, dvals, paths, asg = call(
        functools.partial(first_sums, *sizes),
        [
            sds(6, NP, *FULL), sds(NP, *FULL, dtype=i32), sds(n_bricks, 2, LZ), sds(NP, B, LZ),
            sds(4, B, LZ), sds(3, 3, B, LZ, dtype=i32),
        ],
        9,
        scratch=[
            vm((NP + 2, *FULL), f32), vm((NP + 1, *FULL), f32), fields, vm((2, *FULL), f32),
            vm((2 * NSUB, LZ), f32),
        ],
    )(low, mid, high, below, above, flags, *middle)
    bricks = lax.all_to_all(chunk, ("gy", "col"), 0, 0, tiled=True)
    parts = call(
        functools.partial(first_coarse, n_bricks, n_gx), sds(n_gx, 2 * B, LZ), 1
    )(bricks)
    parts = lax.all_to_all(parts, "gx", 0, 0, tiled=True)
    tables = [vm((3, B, LZ), f32), vm((3, 3, B, LZ), f32)]
    chunk = call(
        functools.partial(second_sums, *sizes),
        sds(n_bricks, 4, LZ),
        6,
        scratch=[fields, *tables, vm((4, B, LZ), f32), vm((6 * NSUB, LZ), f32)],
    )(parts, weights, labels, asg, dvals, paths)
    images = lax.all_to_all(chunk, ("gy", "col"), 0, 0, tiled=True)
    images = call(
        functools.partial(second_coarse, n_gy, n_col, n_gx), sds(n_gx, 3 * B, LZ), 2
    )(images, bricks)
    images = lax.all_to_all(images, "gx", 0, 0, tiled=True)
    return call(
        functools.partial(last_sweeps, *sizes),
        [sds(*plane), sds(1, B * LZ // (n_gy * n_col))],
        5,
        scratch=[fields, *tables],
    )(parts, images, weights, labels, asg)


def solution(mesh):
    placed = (
        P("gx", "gy", "col"),
        P("gx", "gy", "col"),
        P("gx", "gy", "col"),
        P("gx", "gy", "col", None),
        P(),
    )
    sizes = mesh.shape
    return jax.shard_map(
        functools.partial(on_device, sizes["gx"], sizes["gy"], sizes["col"]),
        mesh=mesh,
        in_specs=placed,
        out_specs=(P("gx", "gy", "col"), P("gx", ("gy", "col"))),
        check_vma=False,
    )
```

```python
import functools

import jax
import jax.numpy as jnp
from jax import lax
from jax.experimental import pallas as pl
from jax.experimental.pallas import tpu as pltpu
from jax.sharding import PartitionSpec as P

f32 = jnp.float32
i32 = jnp.int32
bf16 = jnp.bfloat16
NSUB = 64
B = 8
LZ = 128
NP = 3 * B
W = 9
FULL = (NP, 2 * LZ)
FILL_UNROLL = 8
CHUNK = 12
fine_relax = 0.6666667
coarse_relax = 0.7
VMEM_LIMIT = 48 * 1024 * 1024
WHOLE_VMEM = 63 * 1024 * 1024

PERM, OWN, HZ, ASG, SRC = 0, 8, 16, 20, 21
STACK = 29
X_MESSAGE = 25

FOLDS = [(p, None, 0) for p in range(7, 17)]
FOLDS += [(6, 0, 1), (5, 1, 2), (4, 2, 3), (17, 23, 1), (18, 22, 2), (19, 21, 3), (3, 20, 4)]
FOLD_OF = {}
for _at, (_main, _other, _rows) in enumerate(FOLDS):
    FOLD_OF[_main] = (_at, 0)
    if _other is not None:
        FOLD_OF[_other] = (_at, _rows)
N_FOLD = len(FOLDS)
M_PERM, M_OWN, M_HZ, M_ASG, M_SRC = 0, N_FOLD, 2 * N_FOLD, 2 * N_FOLD + 12, 2 * N_FOLD + 13
SRC_FOLDS = [(8 + q, ((12 + q, 4, 4),)) for q in range(4)]
SRC_FOLDS += [(7, ((6, 2, 2), (5, 1, 3))), (16, ((17, 2, 2), (18, 1, 3)))]
SRC_OF = {}
for _at, (_main, _others) in enumerate(SRC_FOLDS):
    SRC_OF[_main] = (_at, 0)
    for _other, _rows, _top in _others:
        SRC_OF[_other] = (_at, _top)
MESSAGE = M_SRC + len(SRC_FOLDS)


def lanes(shape):
    return lax.broadcasted_iota(i32, shape, len(shape) - 1)


def rows(shape):
    return lax.broadcasted_iota(i32, shape, len(shape) - 2)


def sds(*shape, dtype=f32):
    return jax.ShapeDtypeStruct(shape, dtype)


def pinned(*shape):
    return pltpu.VMEM(shape, f32)


def call(kernel, outs, n_in, scratch=(), space=pltpu.VMEM, limit=VMEM_LIMIT, cost=None):
    single = not isinstance(outs, (list, tuple))
    vm = pl.BlockSpec(memory_space=pltpu.VMEM)
    return pl.pallas_call(
        kernel,
        out_shape=outs,
        in_specs=[pl.BlockSpec(memory_space=space)] * n_in,
        out_specs=vm if single else [vm] * len(outs),
        scratch_shapes=list(scratch),
        compiler_params=pltpu.CompilerParams(vmem_limit_bytes=limit),
        cost_estimate=cost,
    )


def spread(row):
    return jnp.broadcast_to(row, (B, LZ))


def asg_tile(asg):
    tile = jnp.concatenate([asg[...].astype(f32), jnp.zeros((1, LZ - NSUB), f32)], axis=1)
    return jnp.where(rows((B, LZ)) == 0, spread(tile), 0.0)


def z_messages(perm_in, src_in, own_in, asg_in, flags_in, mr, ml, base, flags_out,
               perm, src, own, asg, flags, sem):
    copies = [
        pltpu.make_async_copy(a, b, sem.at[i])
        for i, (a, b) in enumerate(
            ((perm_in, perm), (src_in, src), (own_in, own), (asg_in, asg), (flags_in, flags))
        )
    ]
    for copy in copies:
        copy.start()
    for copy in copies:
        copy.wait()
    lane = lanes((B, LZ))

    def first_cells(q):
        k, s, o = perm[q], src[q], own[q].astype(f32)
        return jnp.where(
            lane < 9, k, jnp.where(lane < 18, pltpu.roll(o, 9, 1), pltpu.roll(s, 18, 1))
        )

    def last_cells(q):
        k, s, o = perm[q], src[q], own[q].astype(f32)
        return jnp.where(
            lane >= 55,
            pltpu.roll(k, 64, 1),
            jnp.where(lane >= 46, pltpu.roll(o, 55, 1), pltpu.roll(s, 46, 1)),
        )

    for out, cells in ((mr, first_cells), (ml, last_cells)):
        for q in range(B // 2):
            out[q] = jnp.where(lane < 64, cells(q), pltpu.roll(cells(q + B // 2), 64, 1))
        out[B // 2] = asg_tile(asg)
    for q in range(B):
        base[q], base[B + q], base[2 * B + q] = perm[q], own[q].astype(f32), src[q]
    base[3 * B] = asg_tile(asg)
    col, n_col = lax.axis_index("col"), flags.shape[0]
    for i, at in enumerate((col - 1, col, col + 1)):
        at = jnp.clip(at, 0, n_col - 1)
        flags_out[pl.ds(i, 1), :] = flags[pl.ds(at, 1), :].astype(f32)


def source_at(b, q):
    return SRC + (q - 4 if b == 0 else q)


def stack_up(base, mr, ml, stack, to_low, to_high):
    lane = lanes((B, LZ))
    row = rows((B, LZ))
    for q in range(B):
        stack[PERM + q] = base[q]
        stack[OWN + q] = base[B + q]
        stack[SRC + q] = base[2 * B + q]
    for q in range(B // 2):
        stack[HZ + q] = jnp.where((lane & 63) < 32, mr[q], ml[q])
    at = B // 2
    stack[ASG] = jnp.where(
        row == 1, spread(mr[at, 0:1, :]), jnp.where(row == 2, spread(ml[at, 0:1, :]), base[3 * B])
    )
    for out, first in ((to_low, 0), (to_high, 4)):
        out[0:SRC] = stack[0:SRC]
        for q in range(4):
            out[SRC + q] = base[2 * B + first + q]


def y_messages(low, mid, high, up, down):
    stacks = (low, mid, high)
    row = rows((B, LZ))
    lane = lanes((B, LZ))

    def fold(main, other, n, top, upward):
        if upward:
            return jnp.where((row >= top - n) & (row < top), pltpu.roll(other, top, 0), main)
        return jnp.where(
            (row >= B - top) & (row < B - top + n), pltpu.roll(other, B - top, 0), main
        )

    for out, upward in ((up, True), (down, False)):
        for field, first in ((PERM, M_PERM), (OWN, M_OWN)):
            for at, (main, other, n) in enumerate(FOLDS):
                tile = stacks[main // B][field + main % B]
                if other is not None:
                    tile = fold(tile, stacks[other // B][field + other % B], n, n, upward)
                out[first + at] = tile
        for b in range(3):
            for q in range(B // 2):
                out[M_HZ + 4 * b + q] = stacks[b][HZ + q]
        for at, (main, others) in enumerate(SRC_FOLDS):
            tile = stacks[main // B][source_at(main // B, main % B)]
            for other, n, top in others:
                tile = fold(tile, stacks[other // B][source_at(other // B, other % B)], n, top, upward)
            out[M_SRC + at] = tile
        sides = jnp.where(lane < NSUB, low[ASG], pltpu.roll(high[ASG], NSUB, 1))
        out[M_ASG] = jnp.where(row < 3, sides, pltpu.roll(mid[ASG], 3, 0))


def line_asg(stacks, below, above, ty, b):
    if ty == 1:
        return stacks[b][ASG]
    tile = (below if ty == 0 else above)[M_ASG]
    return (tile, pltpu.roll(tile, 5, 0), pltpu.roll(tile, NSUB, 1))[b]


def around(u_ref, w_ref, p):
    u = u_ref[p + 1]
    return u, (
        (w_ref[0, p] * u_ref[p + 2] + w_ref[1, p] * u_ref[p])
        + (w_ref[2, p] * pltpu.roll(u, NP - 1, 0) + w_ref[3, p] * pltpu.roll(u, 1, 0))
        + (w_ref[4, p] * pltpu.roll(u, 2 * LZ - 1, 1) + w_ref[5, p] * pltpu.roll(u, 1, 1))
    )


def sweeps(both, w_ref, first, last, after=None, operator_at=-1):
    def one_sweep(k, carry):
        now = lax.rem(k, 2)
        src, dst = both.at[now], both.at[1 - now]
        count = NP - 2 * k
        keep = jnp.where(k == operator_at, 1.0, 1.0 - fine_relax)
        give = jnp.where(k == operator_at, -1.0 / fine_relax, 1.0)

        def chunk(i, carry):
            start = jnp.minimum(k + CHUNK * i, k + count - CHUNK)
            moved = []
            for j in range(CHUNK):
                u, near = around(src, w_ref, start + j)
                moved.append(keep * u + give * near)
            for j in range(CHUNK):
                dst[start + j + 1] = moved[j]
            return carry

        lax.fori_loop(0, (count + CHUNK - 1) // CHUNK, chunk, 0)
        if after is not None:
            after(k)
        return carry

    lax.fori_loop(first, last + 1, one_sweep, 0)


def label_sums(groups, sums):
    def one(s, carry):
        for first, labels, fields in groups:
            hits = [tile == s for tile in labels]
            for i, tiles in enumerate(fields):
                parts = [jnp.where(hit, tile, 0.0) for hit, tile in zip(hits, tiles)]
                while len(parts) > 1:
                    parts = [a + b for a, b in zip(parts[::2], parts[1::2])]
                sums[pl.ds(first + i * NSUB + s, 1), :] = jnp.sum(parts[0], axis=0, keepdims=True)
        return carry

    lax.fori_loop(0, NSUB, one, 0, unroll=8)


def three_parts(x):
    l1 = x.astype(bf16)
    rest = x - l1.astype(f32)
    l2 = rest.astype(bf16)
    return l1, l2, (rest - l2.astype(f32)).astype(bf16)


def lane_sums(sums):
    return lax.dot_general(
        jnp.ones((B, 3 * LZ), bf16), jnp.concatenate(three_parts(sums), axis=1),
        (((1,), (1,)), ((), ())), preferred_element_type=f32,
    )


def harmonic(a, b):
    return 2.0 * a * b / (a + b)


def row_product(tile):
    for by in (4, 2, 1):
        tile = tile * pltpu.roll(tile, by, 0)
    return tile


def positive(t):
    return jnp.where(t > 0.0, t, 1.0)


def near_and_far(tile, q):
    turned = pltpu.roll(tile, 64, 1)
    return jnp.where(q < 4, tile, turned), jnp.where(q < 4, turned, tile)


def halo_values(near, far):
    lane = lanes((B, LZ))
    near_side = lane < 64
    halo = (lane < W) | (lane >= LZ - W)
    source_halo = (lane < 4) | (lane >= LZ - 4)
    k = positive(jnp.where(halo, jnp.where(near_side, near, far), 1.0))
    own = jnp.where(near_side, pltpu.roll(near, LZ - 9, 1), pltpu.roll(near, 73, 1))
    src = jnp.where(near_side, pltpu.roll(near, LZ - 18, 1), pltpu.roll(near, 82, 1))
    return k, jnp.where(halo, own, 0.0).astype(i32), jnp.where(source_halo, src, 0.0)


def own_rows(low, mid, high, kmid, lmid, smid):
    for p in range(NP):
        stack, q = (low, mid, high)[p // B], p % B
        k, label, src = halo_values(*near_and_far(stack[HZ + q % 4], q))
        kmid[p, :, 0:LZ] = positive(stack[PERM + q])
        kmid[p, :, LZ:] = k
        lmid[p, :, 0:LZ] = stack[OWN + q].astype(i32)
        lmid[p, :, LZ:] = label
        if 4 <= p < 20:
            smid[p - 4, :, 0:LZ] = stack[source_at(p // B, q)]
            smid[p - 4, :, LZ:] = src


def first_sums(n_gx, n_gy, n_col, low, mid, high, below, above, flags, kmid, lmid, smid,
               weights, labels, chunk, dvals, paths, asg, kext, fx, both, masks, sums):
    gx, gy, col = (lax.axis_index(a) for a in ("gx", "gy", "col"))
    mids = (low, mid, high)
    lane = lanes((B, LZ))
    row = rows((B, LZ))
    def unfolded(ty, first, place):
        at, n = place
        tile = (below if ty == 0 else above)[first + at]
        return pltpu.roll(tile, (B - n if ty == 0 else n) % B, 0) if n else tile

    def beyond(ty, p):
        b, q = p // B, lax.rem(p, B)
        tile = (below if ty == 0 else above)[M_HZ + 4 * b + lax.rem(q, 4)]
        return halo_values(*near_and_far(tile, q))

    def fill(p, carry):
        kext[p + 1, B : 2 * B, :] = kmid[p]
        labels[p, B : 2 * B, :] = lmid[p]
        for ty in (0, 2):
            r = slice(ty * B, (ty + 1) * B)
            kext[p + 1, r, LZ:], labels[p, r, LZ:], _ = beyond(ty, p)
        return carry

    lax.fori_loop(0, NP, fill, 0, unroll=FILL_UNROLL)
    for p in range(NP):
        for ty in (0, 2):
            r = slice(ty * B, (ty + 1) * B)
            kext[p + 1, r, 0:LZ] = positive(unfolded(ty, M_PERM, FOLD_OF[p]))
            labels[p, r, 0:LZ] = unfolded(ty, M_OWN, FOLD_OF[p]).astype(i32)
    for b in range(3):
        for ty in range(3):
            asg[b, ty] = line_asg(mids, below, above, ty, b).astype(i32)
    kext[0] = jnp.ones(FULL, f32)
    kext[NP + 1] = jnp.ones(FULL, f32)

    flag_row = jnp.concatenate(
        [flags[1:2, :], jnp.where(lane[0:1] < 64, flags[2:3, :], flags[0:1, :])], axis=1
    )
    row_all, lane_all = rows(FULL), lanes(FULL)
    wrap_row = jnp.where(gy == 0, B - 1, jnp.where(gy == n_gy - 1, 2 * B - 1, -1))
    masks[0] = jnp.where(row_all == wrap_row, jnp.broadcast_to(flag_row, FULL), 1.0)
    closed = ((lane_all == LZ - 1) & (col == n_col - 1)) | ((lane_all == 2 * LZ - 1) & (col == 0))
    masks[1] = jnp.where(closed, 0.0, 1.0)

    def x_face(p, carry):
        fx[p] = harmonic(kext[p], kext[p + 1])
        return carry

    lax.fori_loop(0, NP + 1, x_face, 0, unroll=5)

    @pl.when(gx == 0)
    def _():
        fx[B] = kext[B + 1]

    @pl.when(gx == n_gx - 1)
    def _():
        fx[2 * B] = kext[2 * B]

    def terms(p, carry):
        b = p // B
        out = ((b == 0) & (gx == 0)) | ((b == 2) & (gx == n_gx - 1))
        k = kext[p + 1]
        fy_up = harmonic(k, pltpu.roll(k, NP - 1, 0)) * masks[0]
        fy_down = pltpu.roll(fy_up, 1, 0)
        fz_right = harmonic(k, pltpu.roll(k, 2 * LZ - 1, 1)) * masks[1]
        fz_left = pltpu.roll(fz_right, 1, 1)
        fx_up, fx_down = fx[p + 1], fx[p]
        diag = fx_up + fx_down + fy_up + fy_down + fz_right + fz_left
        scale = jnp.where(out, 0.0, fine_relax) / diag
        for i, face in enumerate((fx_up, fx_down, fy_up, fy_down, fz_right, fz_left)):
            weights[i, p] = face * scale
        both[0, p + 1] = scale
        dvals[p] = diag[B : 2 * B, 0:LZ]
        return carry

    lax.fori_loop(0, NP, terms, 0, unroll=8)


    def start(i, carry):
        p = i + B // 2
        over = both[0, p + 1] * (1.0 / fine_relax)
        both[1, p + 1, B : 2 * B, :] = smid[i] * over[B : 2 * B]
        for ty in (0, 2):
            r = slice(ty * B, (ty + 1) * B)
            both[1, p + 1, r, LZ:] = beyond(ty, p)[2] * over[r, LZ:]
        return carry

    lax.fori_loop(0, 2 * B, start, 0, unroll=8)
    for p in range(B // 2, NP - B // 2):
        for ty in (0, 2):
            r = slice(ty * B, (ty + 1) * B)
            if p in SRC_OF:
                over = both[0, p + 1, r, 0:LZ] * (1.0 / fine_relax)
                both[1, p + 1, r, 0:LZ] = unfolded(ty, M_SRC, SRC_OF[p]) * over
            else:
                both[1, p + 1, r, 0:LZ] = jnp.zeros((B, LZ), f32)

    r = slice(B, 2 * B)
    for q in range(B):
        p = B + q
        up, down = weights[2, p, r, 0:LZ], weights[3, p, r, 0:LZ]
        rise = row_product(jnp.where(row == 0, 1.0, down)) * up
        fall = row_product(jnp.where(row == B - 1, 1.0, up)) * down
        per = dvals[p] * (1.0 / fine_relax)
        paths[2, q : q + 1, :] = (rise * per)[B - 1 : B]
        paths[3, q : q + 1, :] = (fall * per)[0:1]
    rise, fall = fx[2 * B, B : 2 * B, 0:LZ], fx[B, B : 2 * B, 0:LZ]
    for p in range(B + 1, 2 * B):
        rise = rise * weights[1, p, B : 2 * B, 0:LZ]
        fall = fall * weights[0, p - 1, B : 2 * B, 0:LZ]
    paths[0] = rise
    paths[1] = fall

    sweeps(both, weights, 5, 8)
    tiles = [both[1, B + 1 + q, B : 2 * B, 0:LZ] * dvals[B + q] for q in range(B)]
    diag_tiles = [dvals[B + q] for q in range(B)]
    label_tiles = [labels[B + q, B : 2 * B, 0:LZ] for q in range(B)]
    label_sums([(0, label_tiles, (tiles, diag_tiles))], sums)
    totals = lane_sums(sums[...])

    own = spread(mid[ASG, 0:1, :])
    own = jnp.where(lane < NSUB, own, pltpu.roll(own, NSUB, 1))
    tile = jnp.where(row == 0, totals, own)[0:2]
    for d in range(n_gy * n_col):
        chunk[d] = tile


def one_hot_product(lefts, lows):
    left = jnp.concatenate(lefts, axis=1)
    wide = rows((LZ, LZ))
    right = jnp.concatenate(
        [
            jnp.where(jnp.broadcast_to(low, (LZ, LZ)) == wide, 1.0, 0.0).astype(bf16)
            for low in lows
        ],
        axis=1,
    )
    return lax.dot_general(
        jnp.concatenate(three_parts(left), axis=0), right, (((1,), (1,)), ((), ())),
        preferred_element_type=f32,
    )


def joined(total):
    n = total.shape[0] // 3
    return (total[2 * n :] + total[n : 2 * n]) + total[:n]


def halves(value, high):
    lane = lanes((B, LZ))
    scaled = jnp.where(high == rows((B, LZ)), value, 0.0)
    return jnp.concatenate(
        [jnp.where(lane < NSUB, scaled, 0.0), jnp.where(lane < NSUB, 0.0, scaled)], axis=0
    )


GROUP = 64


def first_coarse(n_bricks, n_out, values, out):
    def one(i, total):
        lefts, lows = [], []
        for j in range(min(GROUP, n_bricks)):
            value = values[i * min(GROUP, n_bricks) + j]
            a = value[1:2].astype(i32)
            lefts.append(halves(spread(value[0:1]), spread(a >> 7)))
            lows.append(a & 127)
        return total + one_hot_product(lefts, lows)

    total = lax.fori_loop(0, n_bricks // min(GROUP, n_bricks), one, jnp.zeros((6 * B, LZ), f32))
    total = joined(total)
    for d in range(n_out):
        out[d] = total


def second_coarse(n_gy, n_col, n_out, values, first, out):
    n_bricks = n_gy * n_col
    lane = lanes((B, LZ))
    near = lanes((1, LZ)) < NSUB

    def own(j):
        before = lax.rem(j + n_bricks - n_col, n_bricks)
        after = lax.rem(j + n_col, n_bricks)
        mine = spread(values[j, 0:1] + values[before, 2:3])
        return mine + pltpu.roll(spread(values[after, 2:3]), NSUB, 1)

    def one(i, totals):
        lefts, lows, edge_lefts, edge_lows = [], [], [], []
        for j in range(min(GROUP, n_bricks) // 2):
            at = i * min(GROUP, n_bricks) + 2 * j
            pair = jnp.where(lane < NSUB, own(at), pltpu.roll(own(at + 1), NSUB, 1))
            a = jnp.where(near, first[at, 1:2], first[at + 1, 1:2]).astype(i32)
            lefts.append(jnp.where(spread(a >> 7) == rows((B, LZ)), pair, 0.0))
            lows.append(a & 127)
        for j in range(min(GROUP, n_bricks)):
            a = values[i * min(GROUP, n_bricks) + j, 3:4].astype(i32)
            edge_lefts.append(halves(spread(values[i * min(GROUP, n_bricks) + j, 1:2]), spread(a >> 7)))
            edge_lows.append(a & 127)
        return (
            totals[0] + one_hot_product(lefts, lows),
            totals[1] + one_hot_product(edge_lefts, edge_lows),
        )

    mine, edges = lax.fori_loop(
        0, n_bricks // min(GROUP, n_bricks), one, (jnp.zeros((3 * B, LZ), f32), jnp.zeros((6 * B, LZ), f32))
    )
    total = jnp.concatenate([joined(mine), joined(edges)], axis=0)
    for d in range(n_out):
        out[d] = total


def lookup(table, index):
    low, high = index & 127, index >> 7
    result = jnp.zeros((B, LZ), f32)
    for h in range(B):
        got = jnp.take_along_axis(spread(table[h : h + 1]), low, axis=1)
        result = jnp.where(high == h, got, result)
    return result


def pick(row, index):
    return jnp.take_along_axis(spread(row), index, axis=1)


def slab_total(parts, g, n_gx, part, size):
    total = parts[jnp.clip(g, 0, n_gx - 1), part : part + size]
    return jnp.where((g >= 0) & (g < n_gx), total, 0.0)


def guess(parts, g, n_gx):
    total = slab_total(parts, g, n_gx, 0, 2 * B)
    exists = (g >= 0) & (g < n_gx)
    rhs, diag = total[0:B], jnp.where(exists, total[B : 2 * B], 1.0)
    return rhs, diag, coarse_relax * rhs / diag


def expand(coarse, asg, labels, u, tables, first, last):
    near_side = lanes((B, LZ)) < 64

    def table(i, carry):
        b, ty = i // 3, lax.rem(i, 3)
        tables[b, ty] = lookup(coarse[b], asg[b, ty])
        return carry

    lax.fori_loop(0, 9, table, 0, unroll=3)

    def one(p, carry):
        b = p // B
        for ty in range(3):
            r = slice(ty * B, (ty + 1) * B)
            t = tables[b, ty]
            u[p + 1, r, 0:LZ] = pick(t[0:1], labels[p, r, 0:LZ])
            lab = labels[p, r, LZ:]
            u[p + 1, r, LZ:] = jnp.where(near_side, pick(t[1:2], lab), pick(t[2:3], lab))
        return carry

    lax.fori_loop(first, last + 1, one, 0, unroll=8)


def second_sums(n_gx, n_gy, n_col, parts, weights, labels, asg, dvals, paths,
                chunk, both, coarse, tables, ends, sums):
    gx = lax.axis_index("gx")
    row = rows((B, LZ))
    r = slice(B, 2 * B)
    for i in range(3):
        coarse[i] = guess(parts, gx + i - 1, n_gx)[2]
    expand(coarse, asg, labels, both.at[0], tables, 0, NP - 1)

    def after(k):
        @pl.when(k == 0)
        def _():
            first = both.at[1]
            zero = jnp.zeros(FULL, f32)
            first[1] = zero
            first[NP] = zero
            first[:, 0:1, :] = jnp.zeros((NP + 2, 1, 2 * LZ), f32)
            first[:, NP - 1 :, :] = jnp.zeros((NP + 2, 1, 2 * LZ), f32)
            ends[0] = first[B + 1, r, 0:LZ] * -paths[0]
            ends[1] = first[2 * B, r, 0:LZ] * -paths[1]
            for q in range(B):
                plane = first[B + 1 + q, r, 0:LZ]
                ends[2, q : q + 1, :] = plane[0:1] * -paths[2, q : q + 1, :]
                ends[3, q : q + 1, :] = plane[B - 1 : B] * -paths[3, q : q + 1, :]

    sweeps(both, weights, 0, 8, after=after, operator_at=4)
    tiles = [both[1, B + 1 + q, r, 0:LZ] * dvals[B + q] for q in range(B)]
    label_tiles = [labels[B + q, r, 0:LZ] for q in range(B)]
    beyond = [labels[2 * B, r, 0:LZ], labels[B - 1, r, 0:LZ]]
    for at in (2 * B, B - 1):
        edge = labels[B, at : at + 1, 0:LZ]
        edge = spread(edge)
        for q in range(1, B):
            edge = jnp.where(row == q, spread(labels[B + q, at : at + 1, 0:LZ]), edge)
        beyond.append(edge)
    groups = [(0, label_tiles, (tiles,))]
    groups += [((2 + i) * NSUB, [beyond[i]], ([ends[i]],)) for i in range(4)]
    sums[NSUB : 2 * NSUB, :] = jnp.zeros((NSUB, LZ), f32)
    label_sums(groups, sums)
    totals = lane_sums(sums[...])
    right, left = (spread(asg[b, 1, 0:1, :].astype(f32)) for b in (2, 0))
    sides = jnp.where(lanes((B, LZ)) < NSUB, right, pltpu.roll(left, NSUB, 1))
    tile = jnp.where(
        row < 2,
        jnp.where(row == 0, totals[:, 0:LZ], totals[:, LZ : 2 * LZ]),
        jnp.where(row == 2, totals[:, 2 * LZ :], sides),
    )[0:4]
    for d in range(n_gy * n_col):
        chunk[d] = tile


def last_sweeps(n_gx, n_gy, n_col, parts, images, weights, labels, asg,
                pressure, coarse_out, both, coarse, tables):
    gx, gy, col = (lax.axis_index(a) for a in ("gx", "gy", "col"))
    for i in range(3):
        g = gx + i - 1
        rhs, diag, start = guess(parts, g, n_gx)
        image = (
            slab_total(images, g, n_gx, 0, B)
            + slab_total(images, g - 1, n_gx, B, B)
            + slab_total(images, g + 1, n_gx, 2 * B, B)
        )
        second = start + coarse_relax * (rhs - image) / diag
        coarse[i] = jnp.where((g >= 0) & (g < n_gx), second, 0.0)
    share = B * LZ // (n_gy * n_col)
    per_row = LZ // share
    mine = gy * n_col + col
    row = coarse[1, pl.ds(mine // per_row, 1), :]
    turned = pltpu.roll(spread(row), lax.rem(LZ - lax.rem(mine, per_row) * share, LZ), 1)
    coarse_out[...] = turned[0:1, 0:share]
    expand(coarse, asg, labels, both.at[1], tables, 4, 19)
    sweeps(both, weights, 5, 8)
    for q in range(B):
        pressure[q] = both[1, B + 1 + q, B : 2 * B, 0:LZ]


def steps(count, by, wrap):
    return [
        (i, (i + by) % count) for i in range(count) if wrap or 0 <= i + by < count
    ]


def on_device(n_gx, n_gy, n_col, permeability, source, ownership, assignment, layer_flags):
    n_bricks = n_gy * n_col
    sizes = (n_gx, n_gy, n_col)
    vm = pltpu.VMEM
    fields = vm((2, NP + 2, *FULL), f32)
    plane = (B, B, LZ)

    def send(x, axis, by, wrap=False):
        return lax.ppermute(x, axis, steps(lax.axis_size(axis), by, wrap))

    mr, ml, base, flags = call(
        z_messages,
        [pinned(B // 2 + 1, B, LZ)] * 2 + [pinned(3 * B + 1, B, LZ), pinned(3, LZ)],
        5,
        scratch=[
            vm(plane, f32), vm(plane, f32), vm(plane, i32), vm((1, NSUB), i32),
            vm((n_col, LZ), i32), pltpu.SemaphoreType.DMA((5,)),
        ],
        space=pl.ANY,
        limit=WHOLE_VMEM,
    )(permeability, source, ownership, assignment.reshape(1, NSUB), layer_flags.reshape(n_col, LZ))
    mr, ml = send(mr, "col", -1), send(ml, "col", 1)
    mid, to_low, to_high = call(
        stack_up, [sds(STACK, B, LZ)] + [sds(X_MESSAGE, B, LZ)] * 2, 3
    )(base, mr, ml)
    low, high = send(to_high, "gx", 1), send(to_low, "gx", -1)
    up, down = call(y_messages, [sds(MESSAGE, B, LZ)] * 2, 3)(low, mid, high)
    below, above = send(up, "gy", 1, True), send(down, "gy", -1, True)
    middle = call(
        own_rows,
        [sds(NP, B, 2 * LZ), sds(NP, B, 2 * LZ, dtype=i32), sds(2 * B, B, 2 * LZ)],
        3,
        cost=pl.CostEstimate(flops=1000000, bytes_accessed=1000000, transcendentals=0),
    )(low, mid, high)

    weights, labels, chunk, dvals, paths, asg = call(
        functools.partial(first_sums, *sizes),
        [
            sds(6, NP, *FULL), sds(NP, *FULL, dtype=i32), sds(n_bricks, 2, LZ), sds(NP, B, LZ),
            sds(4, B, LZ), sds(3, 3, B, LZ, dtype=i32),
        ],
        9,
        scratch=[
            vm((NP + 2, *FULL), f32), vm((NP + 1, *FULL), f32), fields, vm((2, *FULL), f32),
            vm((2 * NSUB, LZ), f32),
        ],
    )(low, mid, high, below, above, flags, *middle)
    bricks = lax.all_to_all(chunk, ("gy", "col"), 0, 0, tiled=True)
    parts = call(
        functools.partial(first_coarse, n_bricks, n_gx), sds(n_gx, 2 * B, LZ), 1
    )(bricks)
    parts = lax.all_to_all(parts, "gx", 0, 0, tiled=True)
    tables = [vm((3, B, LZ), f32), vm((3, 3, B, LZ), f32)]
    chunk = call(
        functools.partial(second_sums, *sizes),
        sds(n_bricks, 4, LZ),
        6,
        scratch=[fields, *tables, vm((4, B, LZ), f32), vm((6 * NSUB, LZ), f32)],
    )(parts, weights, labels, asg, dvals, paths)
    images = lax.all_to_all(chunk, ("gy", "col"), 0, 0, tiled=True)
    images = call(
        functools.partial(second_coarse, n_gy, n_col, n_gx), sds(n_gx, 3 * B, LZ), 2
    )(images, bricks)
    images = lax.all_to_all(images, "gx", 0, 0, tiled=True)
    return call(
        functools.partial(last_sweeps, *sizes),
        [sds(*plane), sds(1, B * LZ // (n_gy * n_col))],
        5,
        scratch=[fields, *tables],
    )(parts, images, weights, labels, asg)


def solution(mesh):
    placed = (
        P("gx", "gy", "col"),
        P("gx", "gy", "col"),
        P("gx", "gy", "col"),
        P("gx", "gy", "col", None),
        P(),
    )
    sizes = mesh.shape
    return jax.shard_map(
        functools.partial(on_device, sizes["gx"], sizes["gy"], sizes["col"]),
        mesh=mesh,
        in_specs=placed,
        out_specs=(P("gx", "gy", "col"), P("gx", ("gy", "col"))),
        check_vma=False,
    )
```

```python
import functools

import jax
import jax.numpy as jnp
from jax import lax
from jax.experimental import pallas as pl
from jax.experimental.pallas import tpu as pltpu
from jax.sharding import PartitionSpec as P

f32 = jnp.float32
i32 = jnp.int32
bf16 = jnp.bfloat16
NSUB = 64
B = 8
LZ = 128
NP = 3 * B
W = 9
FULL = (NP, 2 * LZ)
FILL_UNROLL = 8
CHUNK = 12
fine_relax = 0.6666667
coarse_relax = 0.7
VMEM_LIMIT = 48 * 1024 * 1024
WHOLE_VMEM = 63 * 1024 * 1024

PERM, OWN, HZ, ASG, SRC = 0, 8, 16, 20, 21
STACK = 29
X_MESSAGE = 25

FOLDS = [(p, None, 0) for p in range(7, 17)]
FOLDS += [(6, 0, 1), (5, 1, 2), (4, 2, 3), (17, 23, 1), (18, 22, 2), (19, 21, 3), (3, 20, 4)]
FOLD_OF = {}
for _at, (_main, _other, _rows) in enumerate(FOLDS):
    FOLD_OF[_main] = (_at, 0)
    if _other is not None:
        FOLD_OF[_other] = (_at, _rows)
N_FOLD = len(FOLDS)
M_PERM, M_OWN, M_HZ, M_ASG, M_SRC = 0, N_FOLD, 2 * N_FOLD, 2 * N_FOLD + 12, 2 * N_FOLD + 13
SRC_FOLDS = [(8 + q, ((12 + q, 4, 4),)) for q in range(4)]
SRC_FOLDS += [(7, ((6, 2, 2), (5, 1, 3))), (16, ((17, 2, 2), (18, 1, 3)))]
SRC_OF = {}
for _at, (_main, _others) in enumerate(SRC_FOLDS):
    SRC_OF[_main] = (_at, 0)
    for _other, _rows, _top in _others:
        SRC_OF[_other] = (_at, _top)
MESSAGE = M_SRC + len(SRC_FOLDS)


def lanes(shape):
    return lax.broadcasted_iota(i32, shape, len(shape) - 1)


def rows(shape):
    return lax.broadcasted_iota(i32, shape, len(shape) - 2)


def sds(*shape, dtype=f32):
    return jax.ShapeDtypeStruct(shape, dtype)


def pinned(*shape):
    return pltpu.VMEM(shape, f32)


def call(kernel, outs, n_in, scratch=(), space=pltpu.VMEM, limit=VMEM_LIMIT, cost=None):
    single = not isinstance(outs, (list, tuple))
    vm = pl.BlockSpec(memory_space=pltpu.VMEM)
    return pl.pallas_call(
        kernel,
        out_shape=outs,
        in_specs=[pl.BlockSpec(memory_space=space)] * n_in,
        out_specs=vm if single else [vm] * len(outs),
        scratch_shapes=list(scratch),
        compiler_params=pltpu.CompilerParams(vmem_limit_bytes=limit),
        cost_estimate=cost,
    )


def spread(row):
    return jnp.broadcast_to(row, (B, LZ))


def asg_tile(asg):
    tile = jnp.concatenate([asg[...].astype(f32), jnp.zeros((1, LZ - NSUB), f32)], axis=1)
    return jnp.where(rows((B, LZ)) == 0, spread(tile), 0.0)


def z_messages(perm_in, src_in, own_in, asg_in, flags_in, mr, ml, base, flags_out,
               perm, src, own, asg, flags, sem):
    copies = [
        pltpu.make_async_copy(a, b, sem.at[i])
        for i, (a, b) in enumerate(
            ((perm_in, perm), (src_in, src), (own_in, own), (asg_in, asg), (flags_in, flags))
        )
    ]
    for copy in copies:
        copy.start()
    for copy in copies:
        copy.wait()
    lane = lanes((B, LZ))

    def first_cells(q):
        k, s, o = perm[q], src[q], own[q].astype(f32)
        return jnp.where(
            lane < 9, k, jnp.where(lane < 18, pltpu.roll(o, 9, 1), pltpu.roll(s, 18, 1))
        )

    def last_cells(q):
        k, s, o = perm[q], src[q], own[q].astype(f32)
        return jnp.where(
            lane >= 55,
            pltpu.roll(k, 64, 1),
            jnp.where(lane >= 46, pltpu.roll(o, 55, 1), pltpu.roll(s, 46, 1)),
        )

    for out, cells in ((mr, first_cells), (ml, last_cells)):
        for q in range(B // 2):
            out[q] = jnp.where(lane < 64, cells(q), pltpu.roll(cells(q + B // 2), 64, 1))
        out[B // 2] = asg_tile(asg)
    for q in range(B):
        base[q], base[B + q], base[2 * B + q] = perm[q], own[q].astype(f32), src[q]
    base[3 * B] = asg_tile(asg)
    col, n_col = lax.axis_index("col"), flags.shape[0]
    for i, at in enumerate((col - 1, col, col + 1)):
        at = jnp.clip(at, 0, n_col - 1)
        flags_out[pl.ds(i, 1), :] = flags[pl.ds(at, 1), :].astype(f32)


def source_at(b, q):
    return SRC + (q - 4 if b == 0 else q)


def stack_up(base, mr, ml, stack, to_low, to_high):
    lane = lanes((B, LZ))
    row = rows((B, LZ))
    for q in range(B):
        stack[PERM + q] = base[q]
        stack[OWN + q] = base[B + q]
        stack[SRC + q] = base[2 * B + q]
    for q in range(B // 2):
        stack[HZ + q] = jnp.where((lane & 63) < 32, mr[q], ml[q])
    at = B // 2
    stack[ASG] = jnp.where(
        row == 1, spread(mr[at, 0:1, :]), jnp.where(row == 2, spread(ml[at, 0:1, :]), base[3 * B])
    )
    for out, first in ((to_low, 0), (to_high, 4)):
        out[0:SRC] = stack[0:SRC]
        for q in range(4):
            out[SRC + q] = base[2 * B + first + q]


def y_messages(low, mid, high, up, down):
    stacks = (low, mid, high)
    row = rows((B, LZ))
    lane = lanes((B, LZ))

    def fold(main, other, n, top, upward):
        if upward:
            return jnp.where((row >= top - n) & (row < top), pltpu.roll(other, top, 0), main)
        return jnp.where(
            (row >= B - top) & (row < B - top + n), pltpu.roll(other, B - top, 0), main
        )

    for out, upward in ((up, True), (down, False)):
        for field, first in ((PERM, M_PERM), (OWN, M_OWN)):
            for at, (main, other, n) in enumerate(FOLDS):
                tile = stacks[main // B][field + main % B]
                if other is not None:
                    tile = fold(tile, stacks[other // B][field + other % B], n, n, upward)
                out[first + at] = tile
        for b in range(3):
            for q in range(B // 2):
                out[M_HZ + 4 * b + q] = stacks[b][HZ + q]
        for at, (main, others) in enumerate(SRC_FOLDS):
            tile = stacks[main // B][source_at(main // B, main % B)]
            for other, n, top in others:
                tile = fold(tile, stacks[other // B][source_at(other // B, other % B)], n, top, upward)
            out[M_SRC + at] = tile
        sides = jnp.where(lane < NSUB, low[ASG], pltpu.roll(high[ASG], NSUB, 1))
        out[M_ASG] = jnp.where(row < 3, sides, pltpu.roll(mid[ASG], 3, 0))


def line_asg(stacks, below, above, ty, b):
    if ty == 1:
        return stacks[b][ASG]
    tile = (below if ty == 0 else above)[M_ASG]
    return (tile, pltpu.roll(tile, 5, 0), pltpu.roll(tile, NSUB, 1))[b]


def around(u_ref, w_ref, p):
    u = u_ref[p + 1]
    return u, (
        (w_ref[0, p] * u_ref[p + 2] + w_ref[1, p] * u_ref[p])
        + (w_ref[2, p] * pltpu.roll(u, NP - 1, 0) + w_ref[3, p] * pltpu.roll(u, 1, 0))
        + (w_ref[4, p] * pltpu.roll(u, 2 * LZ - 1, 1) + w_ref[5, p] * pltpu.roll(u, 1, 1))
    )


def sweeps(both, w_ref, first, last, after=None, operator_at=-1):
    def one_sweep(k, carry):
        now = lax.rem(k, 2)
        src, dst = both.at[now], both.at[1 - now]
        count = NP - 2 * k
        keep = jnp.where(k == operator_at, 1.0, 1.0 - fine_relax)
        give = jnp.where(k == operator_at, -1.0 / fine_relax, 1.0)

        def chunk(i, carry):
            start = jnp.minimum(k + CHUNK * i, k + count - CHUNK)
            moved = []
            for j in range(CHUNK):
                u, near = around(src, w_ref, start + j)
                moved.append(keep * u + give * near)
            for j in range(CHUNK):
                dst[start + j + 1] = moved[j]
            return carry

        lax.fori_loop(0, (count + CHUNK - 1) // CHUNK, chunk, 0)
        if after is not None:
            after(k)
        return carry

    lax.fori_loop(first, last + 1, one_sweep, 0)


def label_sums(groups, sums):
    def one(s, carry):
        for first, labels, fields in groups:
            hits = [tile == s for tile in labels]
            for i, tiles in enumerate(fields):
                parts = [jnp.where(hit, tile, 0.0) for hit, tile in zip(hits, tiles)]
                while len(parts) > 1:
                    parts = [a + b for a, b in zip(parts[::2], parts[1::2])]
                sums[pl.ds(first + i * NSUB + s, 1), :] = jnp.sum(parts[0], axis=0, keepdims=True)
        return carry

    lax.fori_loop(0, NSUB, one, 0, unroll=8)


def three_parts(x):
    l1 = x.astype(bf16)
    rest = x - l1.astype(f32)
    l2 = rest.astype(bf16)
    return l1, l2, (rest - l2.astype(f32)).astype(bf16)


def lane_sums(sums):
    return lax.dot_general(
        jnp.ones((B, 3 * LZ), bf16), jnp.concatenate(three_parts(sums), axis=1),
        (((1,), (1,)), ((), ())), preferred_element_type=f32,
    )


def harmonic(a, b):
    return 2.0 * a * b / (a + b)


def row_product(tile):
    for by in (4, 2, 1):
        tile = tile * pltpu.roll(tile, by, 0)
    return tile


def positive(t):
    return jnp.where(t > 0.0, t, 1.0)


def near_and_far(tile, q):
    turned = pltpu.roll(tile, 64, 1)
    return jnp.where(q < 4, tile, turned), jnp.where(q < 4, turned, tile)


def halo_values(near, far):
    lane = lanes((B, LZ))
    near_side = lane < 64
    halo = (lane < W) | (lane >= LZ - W)
    source_halo = (lane < 4) | (lane >= LZ - 4)
    k = positive(jnp.where(halo, jnp.where(near_side, near, far), 1.0))
    own = jnp.where(near_side, pltpu.roll(near, LZ - 9, 1), pltpu.roll(near, 73, 1))
    src = jnp.where(near_side, pltpu.roll(near, LZ - 18, 1), pltpu.roll(near, 82, 1))
    return k, jnp.where(halo, own, 0.0).astype(i32), jnp.where(source_halo, src, 0.0)


def own_rows(low, mid, high, kmid, lmid, smid):
    for p in range(NP):
        stack, q = (low, mid, high)[p // B], p % B
        k, label, src = halo_values(*near_and_far(stack[HZ + q % 4], q))
        kmid[p, :, 0:LZ] = positive(stack[PERM + q])
        kmid[p, :, LZ:] = k
        lmid[p, :, 0:LZ] = stack[OWN + q].astype(i32)
        lmid[p, :, LZ:] = label
        if 4 <= p < 20:
            smid[p - 4, :, 0:LZ] = stack[source_at(p // B, q)]
            smid[p - 4, :, LZ:] = src


def first_sums(n_gx, n_gy, n_col, low, mid, high, below, above, flags, kmid, lmid, smid,
               weights, labels, chunk, dvals, paths, asg, kext, fx, both, masks, sums):
    gx, gy, col = (lax.axis_index(a) for a in ("gx", "gy", "col"))
    mids = (low, mid, high)
    lane = lanes((B, LZ))
    row = rows((B, LZ))
    def unfolded(ty, first, place):
        at, n = place
        tile = (below if ty == 0 else above)[first + at]
        return pltpu.roll(tile, (B - n if ty == 0 else n) % B, 0) if n else tile

    def beyond(ty, p):
        b, q = p // B, lax.rem(p, B)
        tile = (below if ty == 0 else above)[M_HZ + 4 * b + lax.rem(q, 4)]
        return halo_values(*near_and_far(tile, q))

    def fill(p, carry):
        kext[p + 1, B : 2 * B, :] = kmid[p]
        labels[p, B : 2 * B, :] = lmid[p]
        for ty in (0, 2):
            r = slice(ty * B, (ty + 1) * B)
            kext[p + 1, r, LZ:], labels[p, r, LZ:], _ = beyond(ty, p)
        return carry

    lax.fori_loop(0, NP, fill, 0, unroll=FILL_UNROLL)
    for p in range(NP):
        for ty in (0, 2):
            r = slice(ty * B, (ty + 1) * B)
            kext[p + 1, r, 0:LZ] = positive(unfolded(ty, M_PERM, FOLD_OF[p]))
            labels[p, r, 0:LZ] = unfolded(ty, M_OWN, FOLD_OF[p]).astype(i32)
    for b in range(3):
        for ty in range(3):
            asg[b, ty] = line_asg(mids, below, above, ty, b).astype(i32)
    kext[0] = jnp.ones(FULL, f32)
    kext[NP + 1] = jnp.ones(FULL, f32)

    flag_row = jnp.concatenate(
        [flags[1:2, :], jnp.where(lane[0:1] < 64, flags[2:3, :], flags[0:1, :])], axis=1
    )
    row_all, lane_all = rows(FULL), lanes(FULL)
    wrap_row = jnp.where(gy == 0, B - 1, jnp.where(gy == n_gy - 1, 2 * B - 1, -1))
    masks[0] = jnp.where(row_all == wrap_row, jnp.broadcast_to(flag_row, FULL), 1.0)
    closed = ((lane_all == LZ - 1) & (col == n_col - 1)) | ((lane_all == 2 * LZ - 1) & (col == 0))
    masks[1] = jnp.where(closed, 0.0, 1.0)

    def x_face(p, carry):
        fx[p] = harmonic(kext[p], kext[p + 1])
        return carry

    lax.fori_loop(0, NP + 1, x_face, 0, unroll=5)

    @pl.when(gx == 0)
    def _():
        fx[B] = kext[B + 1]

    @pl.when(gx == n_gx - 1)
    def _():
        fx[2 * B] = kext[2 * B]

    def terms(p, carry):
        b = p // B
        out = ((b == 0) & (gx == 0)) | ((b == 2) & (gx == n_gx - 1))
        k = kext[p + 1]
        fy_up = harmonic(k, pltpu.roll(k, NP - 1, 0)) * masks[0]
        fy_down = pltpu.roll(fy_up, 1, 0)
        fz_right = harmonic(k, pltpu.roll(k, 2 * LZ - 1, 1)) * masks[1]
        fz_left = pltpu.roll(fz_right, 1, 1)
        fx_up, fx_down = fx[p + 1], fx[p]
        diag = fx_up + fx_down + fy_up + fy_down + fz_right + fz_left
        scale = jnp.where(out, 0.0, fine_relax) / diag
        for i, face in enumerate((fx_up, fx_down, fy_up, fy_down, fz_right, fz_left)):
            weights[i, p] = face * scale
        both[0, p + 1] = scale
        dvals[p] = diag[B : 2 * B, 0:LZ]
        return carry

    lax.fori_loop(0, NP, terms, 0, unroll=8)


    def start(i, carry):
        p = i + B // 2
        over = both[0, p + 1] * (1.0 / fine_relax)
        both[1, p + 1, B : 2 * B, :] = smid[i] * over[B : 2 * B]
        for ty in (0, 2):
            r = slice(ty * B, (ty + 1) * B)
            both[1, p + 1, r, LZ:] = beyond(ty, p)[2] * over[r, LZ:]
        return carry

    lax.fori_loop(0, 2 * B, start, 0, unroll=8)
    for p in range(B // 2, NP - B // 2):
        for ty in (0, 2):
            r = slice(ty * B, (ty + 1) * B)
            if p in SRC_OF:
                over = both[0, p + 1, r, 0:LZ] * (1.0 / fine_relax)
                both[1, p + 1, r, 0:LZ] = unfolded(ty, M_SRC, SRC_OF[p]) * over
            else:
                both[1, p + 1, r, 0:LZ] = jnp.zeros((B, LZ), f32)

    r = slice(B, 2 * B)
    for q in range(B):
        p = B + q
        up, down = weights[2, p, r, 0:LZ], weights[3, p, r, 0:LZ]
        rise = row_product(jnp.where(row == 0, 1.0, down)) * up
        fall = row_product(jnp.where(row == B - 1, 1.0, up)) * down
        per = dvals[p] * (1.0 / fine_relax)
        paths[2, q : q + 1, :] = (rise * per)[B - 1 : B]
        paths[3, q : q + 1, :] = (fall * per)[0:1]
    rise, fall = fx[2 * B, B : 2 * B, 0:LZ], fx[B, B : 2 * B, 0:LZ]
    for p in range(B + 1, 2 * B):
        rise = rise * weights[1, p, B : 2 * B, 0:LZ]
        fall = fall * weights[0, p - 1, B : 2 * B, 0:LZ]
    paths[0] = rise
    paths[1] = fall

    sweeps(both, weights, 5, 8)
    tiles = [both[1, B + 1 + q, B : 2 * B, 0:LZ] * dvals[B + q] for q in range(B)]
    diag_tiles = [dvals[B + q] for q in range(B)]
    label_tiles = [labels[B + q, B : 2 * B, 0:LZ] for q in range(B)]
    label_sums([(0, label_tiles, (tiles, diag_tiles))], sums)
    totals = lane_sums(sums[...])

    own = spread(mid[ASG, 0:1, :])
    own = jnp.where(lane < NSUB, own, pltpu.roll(own, NSUB, 1))
    tile = jnp.where(row == 0, totals, own)[0:2]
    for d in range(n_gy * n_col):
        chunk[d] = tile


def one_hot_product(lefts, lows):
    left = jnp.concatenate(lefts, axis=1)
    wide = rows((LZ, LZ))
    right = jnp.concatenate(
        [
            jnp.where(jnp.broadcast_to(low, (LZ, LZ)) == wide, 1.0, 0.0).astype(bf16)
            for low in lows
        ],
        axis=1,
    )
    return lax.dot_general(
        jnp.concatenate(three_parts(left), axis=0), right, (((1,), (1,)), ((), ())),
        preferred_element_type=f32,
    )


def joined(total):
    n = total.shape[0] // 3
    return (total[2 * n :] + total[n : 2 * n]) + total[:n]


def halves(value, high):
    lane = lanes((B, LZ))
    scaled = jnp.where(high == rows((B, LZ)), value, 0.0)
    return jnp.concatenate(
        [jnp.where(lane < NSUB, scaled, 0.0), jnp.where(lane < NSUB, 0.0, scaled)], axis=0
    )


GROUP = 64


def first_coarse(n_bricks, values, out):
    def one(i, total):
        lefts, lows = [], []
        for j in range(min(GROUP, n_bricks)):
            value = values[i * min(GROUP, n_bricks) + j]
            a = value[1:2].astype(i32)
            lefts.append(halves(spread(value[0:1]), spread(a >> 7)))
            lows.append(a & 127)
        return total + one_hot_product(lefts, lows)

    total = lax.fori_loop(0, n_bricks // min(GROUP, n_bricks), one, jnp.zeros((6 * B, LZ), f32))
    out[...] = joined(total)


def second_coarse(n_gy, n_col, n_out, values, first, out):
    n_bricks = n_gy * n_col
    lane = lanes((B, LZ))
    near = lanes((1, LZ)) < NSUB

    def own(j):
        before = lax.rem(j + n_bricks - n_col, n_bricks)
        after = lax.rem(j + n_col, n_bricks)
        mine = spread(values[j, 0:1] + values[before, 2:3])
        return mine + pltpu.roll(spread(values[after, 2:3]), NSUB, 1)

    def one(i, totals):
        lefts, lows, edge_lefts, edge_lows = [], [], [], []
        for j in range(min(GROUP, n_bricks) // 2):
            at = i * min(GROUP, n_bricks) + 2 * j
            pair = jnp.where(lane < NSUB, own(at), pltpu.roll(own(at + 1), NSUB, 1))
            a = jnp.where(near, first[at, 1:2], first[at + 1, 1:2]).astype(i32)
            lefts.append(jnp.where(spread(a >> 7) == rows((B, LZ)), pair, 0.0))
            lows.append(a & 127)
        for j in range(min(GROUP, n_bricks)):
            a = values[i * min(GROUP, n_bricks) + j, 3:4].astype(i32)
            edge_lefts.append(halves(spread(values[i * min(GROUP, n_bricks) + j, 1:2]), spread(a >> 7)))
            edge_lows.append(a & 127)
        return (
            totals[0] + one_hot_product(lefts, lows),
            totals[1] + one_hot_product(edge_lefts, edge_lows),
        )

    mine, edges = lax.fori_loop(
        0, n_bricks // min(GROUP, n_bricks), one, (jnp.zeros((3 * B, LZ), f32), jnp.zeros((6 * B, LZ), f32))
    )
    total = jnp.concatenate([joined(mine), joined(edges)], axis=0)
    for d in range(n_out):
        out[d] = total


def lookup(table, index):
    low, high = index & 127, index >> 7
    result = jnp.zeros((B, LZ), f32)
    for h in range(B):
        got = jnp.take_along_axis(spread(table[h : h + 1]), low, axis=1)
        result = jnp.where(high == h, got, result)
    return result


def pick(row, index):
    return jnp.take_along_axis(spread(row), index, axis=1)


def slab_total(parts, g, n_gx, part, size):
    total = parts[jnp.clip(g, 0, n_gx - 1), part : part + size]
    return jnp.where((g >= 0) & (g < n_gx), total, 0.0)


def guess(total, exists):
    rhs, diag = total[0:B], jnp.where(exists, total[B : 2 * B], 1.0)
    return rhs, diag, jnp.where(exists, coarse_relax * rhs / diag, 0.0)


def expand(coarse, asg, labels, u, tables, first, last):
    near_side = lanes((B, LZ)) < 64

    def table(i, carry):
        b, ty = i // 3, lax.rem(i, 3)
        tables[b, ty] = lookup(coarse[b], asg[b, ty])
        return carry

    lax.fori_loop(0, 9, table, 0, unroll=3)

    def one(p, carry):
        b = p // B
        for ty in range(3):
            r = slice(ty * B, (ty + 1) * B)
            t = tables[b, ty]
            u[p + 1, r, 0:LZ] = pick(t[0:1], labels[p, r, 0:LZ])
            lab = labels[p, r, LZ:]
            u[p + 1, r, LZ:] = jnp.where(near_side, pick(t[1:2], lab), pick(t[2:3], lab))
        return carry

    lax.fori_loop(first, last + 1, one, 0, unroll=8)


def second_sums(n_gx, n_gy, n_col, below, here, above, weights, labels, asg, dvals, paths,
                chunk, both, coarse, tables, ends, sums):
    gx = lax.axis_index("gx")
    row = rows((B, LZ))
    r = slice(B, 2 * B)
    for i, total in enumerate((below, here, above)):
        g = gx + i - 1
        coarse[i] = guess(total, (g >= 0) & (g < n_gx))[2]
    expand(coarse, asg, labels, both.at[0], tables, 0, NP - 1)

    def after(k):
        @pl.when(k == 0)
        def _():
            first = both.at[1]
            zero = jnp.zeros(FULL, f32)
            first[1] = zero
            first[NP] = zero
            first[:, 0:1, :] = jnp.zeros((NP + 2, 1, 2 * LZ), f32)
            first[:, NP - 1 :, :] = jnp.zeros((NP + 2, 1, 2 * LZ), f32)
            ends[0] = first[B + 1, r, 0:LZ] * -paths[0]
            ends[1] = first[2 * B, r, 0:LZ] * -paths[1]
            for q in range(B):
                plane = first[B + 1 + q, r, 0:LZ]
                ends[2, q : q + 1, :] = plane[0:1] * -paths[2, q : q + 1, :]
                ends[3, q : q + 1, :] = plane[B - 1 : B] * -paths[3, q : q + 1, :]

    sweeps(both, weights, 0, 8, after=after, operator_at=4)
    tiles = [both[1, B + 1 + q, r, 0:LZ] * dvals[B + q] for q in range(B)]
    label_tiles = [labels[B + q, r, 0:LZ] for q in range(B)]
    beyond = [labels[2 * B, r, 0:LZ], labels[B - 1, r, 0:LZ]]
    for at in (2 * B, B - 1):
        edge = labels[B, at : at + 1, 0:LZ]
        edge = spread(edge)
        for q in range(1, B):
            edge = jnp.where(row == q, spread(labels[B + q, at : at + 1, 0:LZ]), edge)
        beyond.append(edge)
    groups = [(0, label_tiles, (tiles,))]
    groups += [((2 + i) * NSUB, [beyond[i]], ([ends[i]],)) for i in range(4)]
    sums[NSUB : 2 * NSUB, :] = jnp.zeros((NSUB, LZ), f32)
    label_sums(groups, sums)
    totals = lane_sums(sums[...])
    right, left = (spread(asg[b, 1, 0:1, :].astype(f32)) for b in (2, 0))
    sides = jnp.where(lanes((B, LZ)) < NSUB, right, pltpu.roll(left, NSUB, 1))
    tile = jnp.where(
        row < 2,
        jnp.where(row == 0, totals[:, 0:LZ], totals[:, LZ : 2 * LZ]),
        jnp.where(row == 2, totals[:, 2 * LZ :], sides),
    )[0:4]
    for d in range(n_gy * n_col):
        chunk[d] = tile


def last_sweeps(n_gx, n_gy, n_col, below, here, above, images, weights, labels, asg,
                pressure, coarse_out, both, coarse, tables):
    gx, gy, col = (lax.axis_index(a) for a in ("gx", "gy", "col"))
    for i, total in enumerate((below, here, above)):
        g = gx + i - 1
        exists = (g >= 0) & (g < n_gx)
        rhs, diag, start = guess(total, exists)
        image = (
            slab_total(images, g, n_gx, 0, B)
            + slab_total(images, g - 1, n_gx, B, B)
            + slab_total(images, g + 1, n_gx, 2 * B, B)
        )
        second = start + coarse_relax * (rhs - image) / diag
        coarse[i] = jnp.where(exists, second, 0.0)
    share = B * LZ // (n_gy * n_col)
    per_row = LZ // share
    mine = gy * n_col + col
    row = coarse[1, pl.ds(mine // per_row, 1), :]
    turned = pltpu.roll(spread(row), lax.rem(LZ - lax.rem(mine, per_row) * share, LZ), 1)
    coarse_out[...] = turned[0:1, 0:share]
    expand(coarse, asg, labels, both.at[1], tables, 4, 19)
    sweeps(both, weights, 5, 8)
    for q in range(B):
        pressure[q] = both[1, B + 1 + q, B : 2 * B, 0:LZ]


def steps(count, by, wrap):
    return [
        (i, (i + by) % count) for i in range(count) if wrap or 0 <= i + by < count
    ]


def on_device(n_gx, n_gy, n_col, permeability, source, ownership, assignment, layer_flags):
    n_bricks = n_gy * n_col
    sizes = (n_gx, n_gy, n_col)
    vm = pltpu.VMEM
    fields = vm((2, NP + 2, *FULL), f32)
    plane = (B, B, LZ)

    def send(x, axis, by, wrap=False):
        return lax.ppermute(x, axis, steps(lax.axis_size(axis), by, wrap))

    mr, ml, base, flags = call(
        z_messages,
        [pinned(B // 2 + 1, B, LZ)] * 2 + [pinned(3 * B + 1, B, LZ), pinned(3, LZ)],
        5,
        scratch=[
            vm(plane, f32), vm(plane, f32), vm(plane, i32), vm((1, NSUB), i32),
            vm((n_col, LZ), i32), pltpu.SemaphoreType.DMA((5,)),
        ],
        space=pl.ANY,
        limit=WHOLE_VMEM,
    )(permeability, source, ownership, assignment.reshape(1, NSUB), layer_flags.reshape(n_col, LZ))
    mr, ml = send(mr, "col", -1), send(ml, "col", 1)
    mid, to_low, to_high = call(
        stack_up, [sds(STACK, B, LZ)] + [sds(X_MESSAGE, B, LZ)] * 2, 3
    )(base, mr, ml)
    low, high = send(to_high, "gx", 1), send(to_low, "gx", -1)
    up, down = call(y_messages, [sds(MESSAGE, B, LZ)] * 2, 3)(low, mid, high)
    below, above = send(up, "gy", 1, True), send(down, "gy", -1, True)
    middle = call(
        own_rows,
        [sds(NP, B, 2 * LZ), sds(NP, B, 2 * LZ, dtype=i32), sds(2 * B, B, 2 * LZ)],
        3,
        cost=pl.CostEstimate(flops=1000000, bytes_accessed=1000000, transcendentals=0),
    )(low, mid, high)

    weights, labels, chunk, dvals, paths, asg = call(
        functools.partial(first_sums, *sizes),
        [
            sds(6, NP, *FULL), sds(NP, *FULL, dtype=i32), sds(n_bricks, 2, LZ), sds(NP, B, LZ),
            sds(4, B, LZ), sds(3, 3, B, LZ, dtype=i32),
        ],
        9,
        scratch=[
            vm((NP + 2, *FULL), f32), vm((NP + 1, *FULL), f32), fields, vm((2, *FULL), f32),
            vm((2 * NSUB, LZ), f32),
        ],
    )(low, mid, high, below, above, flags, *middle)
    bricks = lax.all_to_all(chunk, ("gy", "col"), 0, 0, tiled=True)
    here = call(functools.partial(first_coarse, n_bricks), sds(2 * B, LZ), 1)(bricks)
    parts = (send(here, "gx", 1), here, send(here, "gx", -1))
    tables = [vm((3, B, LZ), f32), vm((3, 3, B, LZ), f32)]
    chunk = call(
        functools.partial(second_sums, *sizes),
        sds(n_bricks, 4, LZ),
        8,
        scratch=[fields, *tables, vm((4, B, LZ), f32), vm((6 * NSUB, LZ), f32)],
    )(*parts, weights, labels, asg, dvals, paths)
    images = lax.all_to_all(chunk, ("gy", "col"), 0, 0, tiled=True)
    images = call(
        functools.partial(second_coarse, n_gy, n_col, n_gx), sds(n_gx, 3 * B, LZ), 2
    )(images, bricks)
    images = lax.all_to_all(images, "gx", 0, 0, tiled=True)
    return call(
        functools.partial(last_sweeps, *sizes),
        [sds(*plane), sds(1, B * LZ // (n_gy * n_col))],
        7,
        scratch=[fields, *tables],
    )(*parts, images, weights, labels, asg)


def solution(mesh):
    placed = (
        P("gx", "gy", "col"),
        P("gx", "gy", "col"),
        P("gx", "gy", "col"),
        P("gx", "gy", "col", None),
        P(),
    )
    sizes = mesh.shape
    return jax.shard_map(
        functools.partial(on_device, sizes["gx"], sizes["gy"], sizes["col"]),
        mesh=mesh,
        in_specs=placed,
        out_specs=(P("gx", "gy", "col"), P("gx", ("gy", "col"))),
        check_vma=False,
    )
```

```python
import functools

import jax
import jax.numpy as jnp
from jax import lax
from jax.experimental import pallas as pl
from jax.experimental.pallas import tpu as pltpu
from jax.sharding import PartitionSpec as P

f32 = jnp.float32
i32 = jnp.int32
bf16 = jnp.bfloat16
NSUB = 64
B = 8
LZ = 128
NP = 3 * B
W = 9
FULL = (NP, 2 * LZ)
FILL_UNROLL = 8
CHUNK = 12
fine_relax = 0.6666667
coarse_relax = 0.7
VMEM_LIMIT = 48 * 1024 * 1024
WHOLE_VMEM = 63 * 1024 * 1024

PERM, OWN, HZ, ASG, SRC = 0, 8, 16, 20, 21
STACK = 29
X_MESSAGE = 25

FOLDS = [(p, None, 0) for p in range(7, 17)]
FOLDS += [(6, 0, 1), (5, 1, 2), (4, 2, 3), (17, 23, 1), (18, 22, 2), (19, 21, 3), (3, 20, 4)]
FOLD_OF = {}
for _at, (_main, _other, _rows) in enumerate(FOLDS):
    FOLD_OF[_main] = (_at, 0)
    if _other is not None:
        FOLD_OF[_other] = (_at, _rows)
N_FOLD = len(FOLDS)
M_PERM, M_OWN, M_HZ, M_ASG, M_SRC = 0, N_FOLD, 2 * N_FOLD, 2 * N_FOLD + 12, 2 * N_FOLD + 13
SRC_FOLDS = [(8 + q, ((12 + q, 4, 4),)) for q in range(4)]
SRC_FOLDS += [(7, ((6, 2, 2), (5, 1, 3))), (16, ((17, 2, 2), (18, 1, 3)))]
SRC_OF = {}
for _at, (_main, _others) in enumerate(SRC_FOLDS):
    SRC_OF[_main] = (_at, 0)
    for _other, _rows, _top in _others:
        SRC_OF[_other] = (_at, _top)
MESSAGE = M_SRC + len(SRC_FOLDS)


def lanes(shape):
    return lax.broadcasted_iota(i32, shape, len(shape) - 1)


def rows(shape):
    return lax.broadcasted_iota(i32, shape, len(shape) - 2)


def sds(*shape, dtype=f32):
    return jax.ShapeDtypeStruct(shape, dtype)


def pinned(*shape):
    return pltpu.VMEM(shape, f32)


def call(kernel, outs, n_in, scratch=(), space=pltpu.VMEM, limit=VMEM_LIMIT, cost=None):
    single = not isinstance(outs, (list, tuple))
    vm = pl.BlockSpec(memory_space=pltpu.VMEM)
    return pl.pallas_call(
        kernel,
        out_shape=outs,
        in_specs=[pl.BlockSpec(memory_space=space)] * n_in,
        out_specs=vm if single else [vm] * len(outs),
        scratch_shapes=list(scratch),
        compiler_params=pltpu.CompilerParams(vmem_limit_bytes=limit),
        cost_estimate=cost,
    )


def spread(row):
    return jnp.broadcast_to(row, (B, LZ))


def asg_tile(asg):
    tile = jnp.concatenate([asg[...].astype(f32), jnp.zeros((1, LZ - NSUB), f32)], axis=1)
    return jnp.where(rows((B, LZ)) == 0, spread(tile), 0.0)


def z_messages(perm_in, src_in, own_in, asg_in, flags_in, mr, ml, base, flags_out,
               perm, src, own, asg, flags, sem):
    copies = [
        pltpu.make_async_copy(a, b, sem.at[i])
        for i, (a, b) in enumerate(
            ((perm_in, perm), (src_in, src), (own_in, own), (asg_in, asg), (flags_in, flags))
        )
    ]
    for copy in copies:
        copy.start()
    for copy in copies:
        copy.wait()
    lane = lanes((B, LZ))

    def first_cells(q):
        k, s, o = perm[q], src[q], own[q].astype(f32)
        return jnp.where(
            lane < 9, k, jnp.where(lane < 18, pltpu.roll(o, 9, 1), pltpu.roll(s, 18, 1))
        )

    def last_cells(q):
        k, s, o = perm[q], src[q], own[q].astype(f32)
        return jnp.where(
            lane >= 55,
            pltpu.roll(k, 64, 1),
            jnp.where(lane >= 46, pltpu.roll(o, 55, 1), pltpu.roll(s, 46, 1)),
        )

    for out, cells in ((mr, first_cells), (ml, last_cells)):
        for q in range(B // 2):
            out[q] = jnp.where(lane < 64, cells(q), pltpu.roll(cells(q + B // 2), 64, 1))
        out[B // 2] = asg_tile(asg)
    for q in range(B):
        base[q], base[B + q], base[2 * B + q] = perm[q], own[q].astype(f32), src[q]
    base[3 * B] = asg_tile(asg)
    col, n_col = lax.axis_index("col"), flags.shape[0]
    for i, at in enumerate((col - 1, col, col + 1)):
        at = jnp.clip(at, 0, n_col - 1)
        flags_out[pl.ds(i, 1), :] = flags[pl.ds(at, 1), :].astype(f32)


def source_at(b, q):
    return SRC + (q - 4 if b == 0 else q)


def stack_up(base, mr, ml, stack, to_low, to_high):
    lane = lanes((B, LZ))
    row = rows((B, LZ))
    for q in range(B):
        stack[PERM + q] = base[q]
        stack[OWN + q] = base[B + q]
        stack[SRC + q] = base[2 * B + q]
    for q in range(B // 2):
        stack[HZ + q] = jnp.where((lane & 63) < 32, mr[q], ml[q])
    at = B // 2
    stack[ASG] = jnp.where(
        row == 1, spread(mr[at, 0:1, :]), jnp.where(row == 2, spread(ml[at, 0:1, :]), base[3 * B])
    )
    for out, first in ((to_low, 0), (to_high, 4)):
        out[0:SRC] = stack[0:SRC]
        for q in range(4):
            out[SRC + q] = base[2 * B + first + q]


def y_messages(low, mid, high, up, down):
    stacks = (low, mid, high)
    row = rows((B, LZ))
    lane = lanes((B, LZ))

    def fold(main, other, n, top, upward):
        if upward:
            return jnp.where((row >= top - n) & (row < top), pltpu.roll(other, top, 0), main)
        return jnp.where(
            (row >= B - top) & (row < B - top + n), pltpu.roll(other, B - top, 0), main
        )

    for out, upward in ((up, True), (down, False)):
        for field, first in ((PERM, M_PERM), (OWN, M_OWN)):
            for at, (main, other, n) in enumerate(FOLDS):
                tile = stacks[main // B][field + main % B]
                if other is not None:
                    tile = fold(tile, stacks[other // B][field + other % B], n, n, upward)
                out[first + at] = tile
        for b in range(3):
            for q in range(B // 2):
                out[M_HZ + 4 * b + q] = stacks[b][HZ + q]
        for at, (main, others) in enumerate(SRC_FOLDS):
            tile = stacks[main // B][source_at(main // B, main % B)]
            for other, n, top in others:
                tile = fold(tile, stacks[other // B][source_at(other // B, other % B)], n, top, upward)
            out[M_SRC + at] = tile
        sides = jnp.where(lane < NSUB, low[ASG], pltpu.roll(high[ASG], NSUB, 1))
        out[M_ASG] = jnp.where(row < 3, sides, pltpu.roll(mid[ASG], 3, 0))


def line_asg(stacks, below, above, ty, b):
    if ty == 1:
        return stacks[b][ASG]
    tile = (below if ty == 0 else above)[M_ASG]
    return (tile, pltpu.roll(tile, 5, 0), pltpu.roll(tile, NSUB, 1))[b]


def around(u_ref, w_ref, p):
    u = u_ref[p + 1]
    return u, (
        (w_ref[0, p] * u_ref[p + 2] + w_ref[1, p] * u_ref[p])
        + (w_ref[2, p] * pltpu.roll(u, NP - 1, 0) + w_ref[3, p] * pltpu.roll(u, 1, 0))
        + (w_ref[4, p] * pltpu.roll(u, 2 * LZ - 1, 1) + w_ref[5, p] * pltpu.roll(u, 1, 1))
    )


def sweeps(both, w_ref, first, last, after=None, operator_at=-1):
    def one_sweep(k, carry):
        now = lax.rem(k, 2)
        src, dst = both.at[now], both.at[1 - now]
        count = NP - 2 * k
        keep = jnp.where(k == operator_at, 1.0, 1.0 - fine_relax)
        give = jnp.where(k == operator_at, -1.0 / fine_relax, 1.0)

        def chunk(i, carry):
            start = jnp.minimum(k + CHUNK * i, k + count - CHUNK)
            moved = []
            for j in range(CHUNK):
                u, near = around(src, w_ref, start + j)
                moved.append(keep * u + give * near)
            for j in range(CHUNK):
                dst[start + j + 1] = moved[j]
            return carry

        lax.fori_loop(0, (count + CHUNK - 1) // CHUNK, chunk, 0)
        if after is not None:
            after(k)
        return carry

    lax.fori_loop(first, last + 1, one_sweep, 0)


def own_tile(u_ref, w_ref, p):
    r, z = slice(B, 2 * B), slice(0, LZ)
    u, beyond = u_ref[p + 1, r, z], u_ref[p + 1, r, LZ:]
    lane = lanes((B, LZ))
    right = jnp.where(lane == LZ - 1, pltpu.roll(beyond, LZ - 1, 1), pltpu.roll(u, LZ - 1, 1))
    left = jnp.where(lane == 0, pltpu.roll(beyond, 1, 1), pltpu.roll(u, 1, 1))
    w = [w_ref[i, p, r, z] for i in range(6)]
    near = (
        (w[0] * u_ref[p + 2, r, z] + w[1] * u_ref[p, r, z])
        + (w[2] * u_ref[p + 1, B + 1 : 2 * B + 1, z] + w[3] * u_ref[p + 1, B - 1 : 2 * B - 1, z])
        + (w[4] * right + w[5] * left)
    )
    return (1.0 - fine_relax) * u + near


def label_sums(groups, sums):
    def one(s, carry):
        for first, labels, fields in groups:
            hits = [tile == s for tile in labels]
            for i, tiles in enumerate(fields):
                parts = [jnp.where(hit, tile, 0.0) for hit, tile in zip(hits, tiles)]
                while len(parts) > 1:
                    parts = [a + b for a, b in zip(parts[::2], parts[1::2])]
                sums[pl.ds(first + i * NSUB + s, 1), :] = jnp.sum(parts[0], axis=0, keepdims=True)
        return carry

    lax.fori_loop(0, NSUB, one, 0, unroll=8)


def three_parts(x):
    l1 = x.astype(bf16)
    rest = x - l1.astype(f32)
    l2 = rest.astype(bf16)
    return l1, l2, (rest - l2.astype(f32)).astype(bf16)


def lane_sums(sums):
    return lax.dot_general(
        jnp.ones((B, 3 * LZ), bf16), jnp.concatenate(three_parts(sums), axis=1),
        (((1,), (1,)), ((), ())), preferred_element_type=f32,
    )


def harmonic(a, b):
    return 2.0 * a * b / (a + b)


def row_product(tile):
    for by in (4, 2, 1):
        tile = tile * pltpu.roll(tile, by, 0)
    return tile


def positive(t):
    return jnp.where(t > 0.0, t, 1.0)


def near_and_far(tile, q):
    turned = pltpu.roll(tile, 64, 1)
    return jnp.where(q < 4, tile, turned), jnp.where(q < 4, turned, tile)


def halo_values(near, far):
    lane = lanes((B, LZ))
    near_side = lane < 64
    halo = (lane < W) | (lane >= LZ - W)
    source_halo = (lane < 4) | (lane >= LZ - 4)
    k = positive(jnp.where(halo, jnp.where(near_side, near, far), 1.0))
    own = jnp.where(near_side, pltpu.roll(near, LZ - 9, 1), pltpu.roll(near, 73, 1))
    src = jnp.where(near_side, pltpu.roll(near, LZ - 18, 1), pltpu.roll(near, 82, 1))
    return k, jnp.where(halo, own, 0.0).astype(i32), jnp.where(source_halo, src, 0.0)


def own_rows(low, mid, high, kmid, lmid, smid):
    for p in range(NP):
        stack, q = (low, mid, high)[p // B], p % B
        k, label, src = halo_values(*near_and_far(stack[HZ + q % 4], q))
        kmid[p, :, 0:LZ] = positive(stack[PERM + q])
        kmid[p, :, LZ:] = k
        lmid[p, :, 0:LZ] = stack[OWN + q].astype(i32)
        lmid[p, :, LZ:] = label
        if 4 <= p < 20:
            smid[p - 4, :, 0:LZ] = stack[source_at(p // B, q)]
            smid[p - 4, :, LZ:] = src


def first_sums(n_gx, n_gy, n_col, low, mid, high, below, above, flags, kmid, lmid, smid,
               weights, labels, chunk, dvals, paths, asg, kext, fx, both, masks, sums):
    gx, gy, col = (lax.axis_index(a) for a in ("gx", "gy", "col"))
    mids = (low, mid, high)
    lane = lanes((B, LZ))
    row = rows((B, LZ))
    def unfolded(ty, first, place):
        at, n = place
        tile = (below if ty == 0 else above)[first + at]
        return pltpu.roll(tile, (B - n if ty == 0 else n) % B, 0) if n else tile

    def beyond(ty, p):
        b, q = p // B, lax.rem(p, B)
        tile = (below if ty == 0 else above)[M_HZ + 4 * b + lax.rem(q, 4)]
        return halo_values(*near_and_far(tile, q))

    def fill(p, carry):
        kext[p + 1, B : 2 * B, :] = kmid[p]
        labels[p, B : 2 * B, :] = lmid[p]
        for ty in (0, 2):
            r = slice(ty * B, (ty + 1) * B)
            kext[p + 1, r, LZ:], labels[p, r, LZ:], _ = beyond(ty, p)
        return carry

    lax.fori_loop(0, NP, fill, 0, unroll=FILL_UNROLL)
    for p in range(NP):
        for ty in (0, 2):
            r = slice(ty * B, (ty + 1) * B)
            kext[p + 1, r, 0:LZ] = positive(unfolded(ty, M_PERM, FOLD_OF[p]))
            labels[p, r, 0:LZ] = unfolded(ty, M_OWN, FOLD_OF[p]).astype(i32)
    for b in range(3):
        for ty in range(3):
            asg[b, ty] = line_asg(mids, below, above, ty, b).astype(i32)
    kext[0] = jnp.ones(FULL, f32)
    kext[NP + 1] = jnp.ones(FULL, f32)

    flag_row = jnp.concatenate(
        [flags[1:2, :], jnp.where(lane[0:1] < 64, flags[2:3, :], flags[0:1, :])], axis=1
    )
    row_all, lane_all = rows(FULL), lanes(FULL)
    wrap_row = jnp.where(gy == 0, B - 1, jnp.where(gy == n_gy - 1, 2 * B - 1, -1))
    masks[0] = jnp.where(row_all == wrap_row, jnp.broadcast_to(flag_row, FULL), 1.0)
    closed = ((lane_all == LZ - 1) & (col == n_col - 1)) | ((lane_all == 2 * LZ - 1) & (col == 0))
    masks[1] = jnp.where(closed, 0.0, 1.0)

    def x_face(p, carry):
        fx[p] = harmonic(kext[p], kext[p + 1])
        return carry

    lax.fori_loop(0, NP + 1, x_face, 0, unroll=5)

    @pl.when(gx == 0)
    def _():
        fx[B] = kext[B + 1]

    @pl.when(gx == n_gx - 1)
    def _():
        fx[2 * B] = kext[2 * B]

    def terms(p, carry):
        b = p // B
        out = ((b == 0) & (gx == 0)) | ((b == 2) & (gx == n_gx - 1))
        k = kext[p + 1]
        fy_up = harmonic(k, pltpu.roll(k, NP - 1, 0)) * masks[0]
        fy_down = pltpu.roll(fy_up, 1, 0)
        fz_right = harmonic(k, pltpu.roll(k, 2 * LZ - 1, 1)) * masks[1]
        fz_left = pltpu.roll(fz_right, 1, 1)
        fx_up, fx_down = fx[p + 1], fx[p]
        diag = fx_up + fx_down + fy_up + fy_down + fz_right + fz_left
        scale = jnp.where(out, 0.0, fine_relax) / diag
        for i, face in enumerate((fx_up, fx_down, fy_up, fy_down, fz_right, fz_left)):
            weights[i, p] = face * scale
        both[0, p + 1] = scale
        dvals[p] = diag[B : 2 * B, 0:LZ]
        return carry

    lax.fori_loop(0, NP, terms, 0, unroll=8)


    def start(i, carry):
        p = i + B // 2
        over = both[0, p + 1] * (1.0 / fine_relax)
        both[1, p + 1, B : 2 * B, :] = smid[i] * over[B : 2 * B]
        for ty in (0, 2):
            r = slice(ty * B, (ty + 1) * B)
            both[1, p + 1, r, LZ:] = beyond(ty, p)[2] * over[r, LZ:]
        return carry

    lax.fori_loop(0, 2 * B, start, 0, unroll=8)
    for p in range(B // 2, NP - B // 2):
        for ty in (0, 2):
            r = slice(ty * B, (ty + 1) * B)
            if p in SRC_OF:
                over = both[0, p + 1, r, 0:LZ] * (1.0 / fine_relax)
                both[1, p + 1, r, 0:LZ] = unfolded(ty, M_SRC, SRC_OF[p]) * over
            else:
                both[1, p + 1, r, 0:LZ] = jnp.zeros((B, LZ), f32)

    r = slice(B, 2 * B)
    for q in range(B):
        p = B + q
        up, down = weights[2, p, r, 0:LZ], weights[3, p, r, 0:LZ]
        rise = row_product(jnp.where(row == 0, 1.0, down)) * up
        fall = row_product(jnp.where(row == B - 1, 1.0, up)) * down
        per = dvals[p] * (1.0 / fine_relax)
        paths[2, q : q + 1, :] = (rise * per)[B - 1 : B]
        paths[3, q : q + 1, :] = (fall * per)[0:1]
    rise, fall = fx[2 * B, B : 2 * B, 0:LZ], fx[B, B : 2 * B, 0:LZ]
    for p in range(B + 1, 2 * B):
        rise = rise * weights[1, p, B : 2 * B, 0:LZ]
        fall = fall * weights[0, p - 1, B : 2 * B, 0:LZ]
    paths[0] = rise
    paths[1] = fall

    sweeps(both, weights, 5, 7)
    tiles = [own_tile(both.at[0], weights, B + q) * dvals[B + q] for q in range(B)]
    diag_tiles = [dvals[B + q] for q in range(B)]
    label_tiles = [labels[B + q, B : 2 * B, 0:LZ] for q in range(B)]
    label_sums([(0, label_tiles, (tiles, diag_tiles))], sums)
    totals = lane_sums(sums[...])

    own = spread(mid[ASG, 0:1, :])
    own = jnp.where(lane < NSUB, own, pltpu.roll(own, NSUB, 1))
    tile = jnp.where(row == 0, totals, own)[0:2]
    for d in range(n_gy * n_col):
        chunk[d] = tile


def one_hot_product(lefts, lows):
    left = jnp.concatenate(lefts, axis=1)
    wide = rows((LZ, LZ))
    right = jnp.concatenate(
        [
            jnp.where(jnp.broadcast_to(low, (LZ, LZ)) == wide, 1.0, 0.0).astype(bf16)
            for low in lows
        ],
        axis=1,
    )
    return lax.dot_general(
        jnp.concatenate(three_parts(left), axis=0), right, (((1,), (1,)), ((), ())),
        preferred_element_type=f32,
    )


def joined(total):
    n = total.shape[0] // 3
    return (total[2 * n :] + total[n : 2 * n]) + total[:n]


def halves(value, high):
    lane = lanes((B, LZ))
    scaled = jnp.where(high == rows((B, LZ)), value, 0.0)
    return jnp.concatenate(
        [jnp.where(lane < NSUB, scaled, 0.0), jnp.where(lane < NSUB, 0.0, scaled)], axis=0
    )


GROUP = 64


def first_coarse(n_bricks, n_out, values, out):
    def one(i, total):
        lefts, lows = [], []
        for j in range(min(GROUP, n_bricks)):
            value = values[i * min(GROUP, n_bricks) + j]
            a = value[1:2].astype(i32)
            lefts.append(halves(spread(value[0:1]), spread(a >> 7)))
            lows.append(a & 127)
        return total + one_hot_product(lefts, lows)

    total = lax.fori_loop(0, n_bricks // min(GROUP, n_bricks), one, jnp.zeros((6 * B, LZ), f32))
    total = joined(total)
    for d in range(n_out):
        out[d] = total


def second_coarse(n_gy, n_col, n_out, values, first, out):
    n_bricks = n_gy * n_col
    lane = lanes((B, LZ))
    near = lanes((1, LZ)) < NSUB

    def own(j):
        before = lax.rem(j + n_bricks - n_col, n_bricks)
        after = lax.rem(j + n_col, n_bricks)
        mine = spread(values[j, 0:1] + values[before, 2:3])
        return mine + pltpu.roll(spread(values[after, 2:3]), NSUB, 1)

    def one(i, totals):
        lefts, lows, edge_lefts, edge_lows = [], [], [], []
        for j in range(min(GROUP, n_bricks) // 2):
            at = i * min(GROUP, n_bricks) + 2 * j
            pair = jnp.where(lane < NSUB, own(at), pltpu.roll(own(at + 1), NSUB, 1))
            a = jnp.where(near, first[at, 1:2], first[at + 1, 1:2]).astype(i32)
            lefts.append(jnp.where(spread(a >> 7) == rows((B, LZ)), pair, 0.0))
            lows.append(a & 127)
        for j in range(min(GROUP, n_bricks)):
            a = values[i * min(GROUP, n_bricks) + j, 3:4].astype(i32)
            edge_lefts.append(halves(spread(values[i * min(GROUP, n_bricks) + j, 1:2]), spread(a >> 7)))
            edge_lows.append(a & 127)
        return (
            totals[0] + one_hot_product(lefts, lows),
            totals[1] + one_hot_product(edge_lefts, edge_lows),
        )

    mine, edges = lax.fori_loop(
        0, n_bricks // min(GROUP, n_bricks), one, (jnp.zeros((3 * B, LZ), f32), jnp.zeros((6 * B, LZ), f32))
    )
    total = jnp.concatenate([joined(mine), joined(edges)], axis=0)
    for d in range(n_out):
        out[d] = total


def lookup(table, index):
    low, high = index & 127, index >> 7
    result = jnp.zeros((B, LZ), f32)
    for h in range(B):
        got = jnp.take_along_axis(spread(table[h : h + 1]), low, axis=1)
        result = jnp.where(high == h, got, result)
    return result


def pick(row, index):
    return jnp.take_along_axis(spread(row), index, axis=1)


def slab_total(parts, g, n_gx, part, size):
    total = parts[jnp.clip(g, 0, n_gx - 1), part : part + size]
    return jnp.where((g >= 0) & (g < n_gx), total, 0.0)


def guess(parts, g, n_gx):
    total = slab_total(parts, g, n_gx, 0, 2 * B)
    exists = (g >= 0) & (g < n_gx)
    rhs, diag = total[0:B], jnp.where(exists, total[B : 2 * B], 1.0)
    return rhs, diag, coarse_relax * rhs / diag


def expand(coarse, asg, labels, u, tables, first, last):
    near_side = lanes((B, LZ)) < 64

    def table(i, carry):
        b, ty = i // 3, lax.rem(i, 3)
        tables[b, ty] = lookup(coarse[b], asg[b, ty])
        return carry

    lax.fori_loop(0, 9, table, 0, unroll=3)

    def one(p, carry):
        b = p // B
        for ty in range(3):
            r = slice(ty * B, (ty + 1) * B)
            t = tables[b, ty]
            u[p + 1, r, 0:LZ] = pick(t[0:1], labels[p, r, 0:LZ])
            lab = labels[p, r, LZ:]
            u[p + 1, r, LZ:] = jnp.where(near_side, pick(t[1:2], lab), pick(t[2:3], lab))
        return carry

    lax.fori_loop(first, last + 1, one, 0, unroll=8)


def second_sums(n_gx, n_gy, n_col, parts, weights, labels, asg, dvals, paths,
                chunk, both, coarse, tables, ends, sums):
    gx = lax.axis_index("gx")
    row = rows((B, LZ))
    r = slice(B, 2 * B)
    for i in range(3):
        coarse[i] = guess(parts, gx + i - 1, n_gx)[2]
    expand(coarse, asg, labels, both.at[0], tables, 0, NP - 1)

    def after(k):
        @pl.when(k == 0)
        def _():
            first = both.at[1]
            zero = jnp.zeros(FULL, f32)
            first[1] = zero
            first[NP] = zero
            first[:, 0:1, :] = jnp.zeros((NP + 2, 1, 2 * LZ), f32)
            first[:, NP - 1 :, :] = jnp.zeros((NP + 2, 1, 2 * LZ), f32)
            ends[0] = first[B + 1, r, 0:LZ] * -paths[0]
            ends[1] = first[2 * B, r, 0:LZ] * -paths[1]
            for q in range(B):
                plane = first[B + 1 + q, r, 0:LZ]
                ends[2, q : q + 1, :] = plane[0:1] * -paths[2, q : q + 1, :]
                ends[3, q : q + 1, :] = plane[B - 1 : B] * -paths[3, q : q + 1, :]

    sweeps(both, weights, 0, 7, after=after, operator_at=4)
    tiles = [own_tile(both.at[0], weights, B + q) * dvals[B + q] for q in range(B)]
    label_tiles = [labels[B + q, r, 0:LZ] for q in range(B)]
    beyond = [labels[2 * B, r, 0:LZ], labels[B - 1, r, 0:LZ]]
    for at in (2 * B, B - 1):
        edge = labels[B, at : at + 1, 0:LZ]
        edge = spread(edge)
        for q in range(1, B):
            edge = jnp.where(row == q, spread(labels[B + q, at : at + 1, 0:LZ]), edge)
        beyond.append(edge)
    groups = [(0, label_tiles, (tiles,))]
    groups += [((2 + i) * NSUB, [beyond[i]], ([ends[i]],)) for i in range(4)]
    sums[NSUB : 2 * NSUB, :] = jnp.zeros((NSUB, LZ), f32)
    label_sums(groups, sums)
    totals = lane_sums(sums[...])
    right, left = (spread(asg[b, 1, 0:1, :].astype(f32)) for b in (2, 0))
    sides = jnp.where(lanes((B, LZ)) < NSUB, right, pltpu.roll(left, NSUB, 1))
    tile = jnp.where(
        row < 2,
        jnp.where(row == 0, totals[:, 0:LZ], totals[:, LZ : 2 * LZ]),
        jnp.where(row == 2, totals[:, 2 * LZ :], sides),
    )[0:4]
    for d in range(n_gy * n_col):
        chunk[d] = tile


def last_sweeps(n_gx, n_gy, n_col, parts, images, weights, labels, asg,
                pressure, coarse_out, both, coarse, tables):
    gx, gy, col = (lax.axis_index(a) for a in ("gx", "gy", "col"))
    for i in range(3):
        g = gx + i - 1
        rhs, diag, start = guess(parts, g, n_gx)
        image = (
            slab_total(images, g, n_gx, 0, B)
            + slab_total(images, g - 1, n_gx, B, B)
            + slab_total(images, g + 1, n_gx, 2 * B, B)
        )
        second = start + coarse_relax * (rhs - image) / diag
        coarse[i] = jnp.where((g >= 0) & (g < n_gx), second, 0.0)
    share = B * LZ // (n_gy * n_col)
    per_row = LZ // share
    mine = gy * n_col + col
    row = coarse[1, pl.ds(mine // per_row, 1), :]
    turned = pltpu.roll(spread(row), lax.rem(LZ - lax.rem(mine, per_row) * share, LZ), 1)
    coarse_out[...] = turned[0:1, 0:share]
    expand(coarse, asg, labels, both.at[1], tables, 4, 19)
    sweeps(both, weights, 5, 7)
    for q in range(B):
        pressure[q] = own_tile(both.at[0], weights, B + q)


def steps(count, by, wrap):
    return [
        (i, (i + by) % count) for i in range(count) if wrap or 0 <= i + by < count
    ]


def on_device(n_gx, n_gy, n_col, permeability, source, ownership, assignment, layer_flags):
    n_bricks = n_gy * n_col
    sizes = (n_gx, n_gy, n_col)
    vm = pltpu.VMEM
    fields = vm((2, NP + 2, *FULL), f32)
    plane = (B, B, LZ)

    def send(x, axis, by, wrap=False):
        return lax.ppermute(x, axis, steps(lax.axis_size(axis), by, wrap))

    mr, ml, base, flags = call(
        z_messages,
        [pinned(B // 2 + 1, B, LZ)] * 2 + [pinned(3 * B + 1, B, LZ), pinned(3, LZ)],
        5,
        scratch=[
            vm(plane, f32), vm(plane, f32), vm(plane, i32), vm((1, NSUB), i32),
            vm((n_col, LZ), i32), pltpu.SemaphoreType.DMA((5,)),
        ],
        space=pl.ANY,
        limit=WHOLE_VMEM,
    )(permeability, source, ownership, assignment.reshape(1, NSUB), layer_flags.reshape(n_col, LZ))
    mr, ml = send(mr, "col", -1), send(ml, "col", 1)
    mid, to_low, to_high = call(
        stack_up, [sds(STACK, B, LZ)] + [sds(X_MESSAGE, B, LZ)] * 2, 3
    )(base, mr, ml)
    low, high = send(to_high, "gx", 1), send(to_low, "gx", -1)
    up, down = call(y_messages, [sds(MESSAGE, B, LZ)] * 2, 3)(low, mid, high)
    below, above = send(up, "gy", 1, True), send(down, "gy", -1, True)
    middle = call(
        own_rows,
        [sds(NP, B, 2 * LZ), sds(NP, B, 2 * LZ, dtype=i32), sds(2 * B, B, 2 * LZ)],
        3,
        cost=pl.CostEstimate(flops=1000000, bytes_accessed=1000000, transcendentals=0),
    )(low, mid, high)

    weights, labels, chunk, dvals, paths, asg = call(
        functools.partial(first_sums, *sizes),
        [
            sds(6, NP, *FULL), sds(NP, *FULL, dtype=i32), sds(n_bricks, 2, LZ), sds(NP, B, LZ),
            sds(4, B, LZ), sds(3, 3, B, LZ, dtype=i32),
        ],
        9,
        scratch=[
            vm((NP + 2, *FULL), f32), vm((NP + 1, *FULL), f32), fields, vm((2, *FULL), f32),
            vm((2 * NSUB, LZ), f32),
        ],
    )(low, mid, high, below, above, flags, *middle)
    bricks = lax.all_to_all(chunk, ("gy", "col"), 0, 0, tiled=True)
    parts = call(
        functools.partial(first_coarse, n_bricks, n_gx), sds(n_gx, 2 * B, LZ), 1
    )(bricks)
    parts = lax.all_to_all(parts, "gx", 0, 0, tiled=True)
    tables = [vm((3, B, LZ), f32), vm((3, 3, B, LZ), f32)]
    chunk = call(
        functools.partial(second_sums, *sizes),
        sds(n_bricks, 4, LZ),
        6,
        scratch=[fields, *tables, vm((4, B, LZ), f32), vm((6 * NSUB, LZ), f32)],
    )(parts, weights, labels, asg, dvals, paths)
    images = lax.all_to_all(chunk, ("gy", "col"), 0, 0, tiled=True)
    images = call(
        functools.partial(second_coarse, n_gy, n_col, n_gx), sds(n_gx, 3 * B, LZ), 2
    )(images, bricks)
    images = lax.all_to_all(images, "gx", 0, 0, tiled=True)
    return call(
        functools.partial(last_sweeps, *sizes),
        [sds(*plane), sds(1, B * LZ // (n_gy * n_col))],
        5,
        scratch=[fields, *tables],
    )(parts, images, weights, labels, asg)


def solution(mesh):
    placed = (
        P("gx", "gy", "col"),
        P("gx", "gy", "col"),
        P("gx", "gy", "col"),
        P("gx", "gy", "col", None),
        P(),
    )
    sizes = mesh.shape
    return jax.shard_map(
        functools.partial(on_device, sizes["gx"], sizes["gy"], sizes["col"]),
        mesh=mesh,
        in_specs=placed,
        out_specs=(P("gx", "gy", "col"), P("gx", ("gy", "col"))),
        check_vma=False,
    )
```

```python
import functools

import jax
import jax.numpy as jnp
from jax import lax
from jax.experimental import pallas as pl
from jax.experimental.pallas import tpu as pltpu
from jax.sharding import PartitionSpec as P

f32 = jnp.float32
i32 = jnp.int32
bf16 = jnp.bfloat16
NSUB = 64
B = 8
LZ = 128
NP = 3 * B
W = 9
FULL = (NP, 2 * LZ)
CHUNK = 12
fine_relax = 0.6666667
coarse_relax = 0.7
VMEM_LIMIT = 48 * 1024 * 1024
WHOLE_VMEM = 63 * 1024 * 1024

PERM, OWN, HZ, ASG, SRC = 0, 8, 16, 20, 21
STACK = 29
X_MESSAGE = 25

FOLDS = [(p, None, 0) for p in range(7, 17)]
FOLDS += [(6, 0, 1), (5, 1, 2), (4, 2, 3), (17, 23, 1), (18, 22, 2), (19, 21, 3), (3, 20, 4)]
FOLD_OF = {}
for _at, (_main, _other, _rows) in enumerate(FOLDS):
    FOLD_OF[_main] = (_at, 0)
    if _other is not None:
        FOLD_OF[_other] = (_at, _rows)
N_FOLD = len(FOLDS)
M_PERM, M_OWN, M_HZ, M_ASG, M_SRC = 0, N_FOLD, 2 * N_FOLD, 2 * N_FOLD + 12, 2 * N_FOLD + 13
SRC_FOLDS = [(8 + q, ((12 + q, 4, 4),)) for q in range(4)]
SRC_FOLDS += [(7, ((6, 2, 2), (5, 1, 3))), (16, ((17, 2, 2), (18, 1, 3)))]
SRC_OF = {}
for _at, (_main, _others) in enumerate(SRC_FOLDS):
    SRC_OF[_main] = (_at, 0)
    for _other, _rows, _top in _others:
        SRC_OF[_other] = (_at, _top)
MESSAGE = M_SRC + len(SRC_FOLDS)


def lanes(shape):
    return lax.broadcasted_iota(i32, shape, len(shape) - 1)


def rows(shape):
    return lax.broadcasted_iota(i32, shape, len(shape) - 2)


def sds(*shape, dtype=f32):
    return jax.ShapeDtypeStruct(shape, dtype)


def pinned(*shape):
    return pltpu.VMEM(shape, f32)


def call(kernel, outs, n_in, scratch=(), space=pltpu.VMEM, limit=VMEM_LIMIT, cost=None):
    single = not isinstance(outs, (list, tuple))
    vm = pl.BlockSpec(memory_space=pltpu.VMEM)
    return pl.pallas_call(
        kernel,
        out_shape=outs,
        in_specs=[pl.BlockSpec(memory_space=space)] * n_in,
        out_specs=vm if single else [vm] * len(outs),
        scratch_shapes=list(scratch),
        compiler_params=pltpu.CompilerParams(vmem_limit_bytes=limit),
        cost_estimate=cost,
    )


def spread(row):
    return jnp.broadcast_to(row, (B, LZ))


def asg_tile(asg):
    tile = jnp.concatenate([asg[...].astype(f32), jnp.zeros((1, LZ - NSUB), f32)], axis=1)
    return jnp.where(rows((B, LZ)) == 0, spread(tile), 0.0)


def z_messages(perm_in, src_in, own_in, asg_in, flags_in, mr, ml, base, flags_out,
               perm, src, own, asg, flags, sem):
    copies = [
        pltpu.make_async_copy(a, b, sem.at[i])
        for i, (a, b) in enumerate(
            ((perm_in, perm), (src_in, src), (own_in, own), (asg_in, asg), (flags_in, flags))
        )
    ]
    for copy in copies:
        copy.start()
    for copy in copies:
        copy.wait()
    lane = lanes((B, LZ))

    def first_cells(q):
        k, s, o = perm[q], src[q], own[q].astype(f32)
        return jnp.where(
            lane < 9, k, jnp.where(lane < 18, pltpu.roll(o, 9, 1), pltpu.roll(s, 18, 1))
        )

    def last_cells(q):
        k, s, o = perm[q], src[q], own[q].astype(f32)
        return jnp.where(
            lane >= 55,
            pltpu.roll(k, 64, 1),
            jnp.where(lane >= 46, pltpu.roll(o, 55, 1), pltpu.roll(s, 46, 1)),
        )

    for out, cells in ((mr, first_cells), (ml, last_cells)):
        for q in range(B // 2):
            out[q] = jnp.where(lane < 64, cells(q), pltpu.roll(cells(q + B // 2), 64, 1))
        out[B // 2] = asg_tile(asg)
    for q in range(B):
        base[q], base[B + q], base[2 * B + q] = perm[q], own[q].astype(f32), src[q]
    base[3 * B] = asg_tile(asg)
    col, n_col = lax.axis_index("col"), flags.shape[0]
    for i, at in enumerate((col - 1, col, col + 1)):
        at = jnp.clip(at, 0, n_col - 1)
        flags_out[pl.ds(i, 1), :] = flags[pl.ds(at, 1), :].astype(f32)


def source_at(b, q):
    return SRC + (q - 4 if b == 0 else q)


def stack_up(base, mr, ml, stack, to_low, to_high):
    lane = lanes((B, LZ))
    row = rows((B, LZ))
    for q in range(B):
        stack[PERM + q] = base[q]
        stack[OWN + q] = base[B + q]
        stack[SRC + q] = base[2 * B + q]
    for q in range(B // 2):
        stack[HZ + q] = jnp.where((lane & 63) < 32, mr[q], ml[q])
    at = B // 2
    stack[ASG] = jnp.where(
        row == 1, spread(mr[at, 0:1, :]), jnp.where(row == 2, spread(ml[at, 0:1, :]), base[3 * B])
    )
    for out, first in ((to_low, 0), (to_high, 4)):
        out[0:SRC] = stack[0:SRC]
        for q in range(4):
            out[SRC + q] = base[2 * B + first + q]


def y_messages(low, mid, high, up, down):
    stacks = (low, mid, high)
    row = rows((B, LZ))
    lane = lanes((B, LZ))

    def fold(main, other, n, top, upward):
        if upward:
            return jnp.where((row >= top - n) & (row < top), pltpu.roll(other, top, 0), main)
        return jnp.where(
            (row >= B - top) & (row < B - top + n), pltpu.roll(other, B - top, 0), main
        )

    for out, upward in ((up, True), (down, False)):
        for field, first in ((PERM, M_PERM), (OWN, M_OWN)):
            for at, (main, other, n) in enumerate(FOLDS):
                tile = stacks[main // B][field + main % B]
                if other is not None:
                    tile = fold(tile, stacks[other // B][field + other % B], n, n, upward)
                out[first + at] = tile
        for b in range(3):
            for q in range(B // 2):
                out[M_HZ + 4 * b + q] = stacks[b][HZ + q]
        for at, (main, others) in enumerate(SRC_FOLDS):
            tile = stacks[main // B][source_at(main // B, main % B)]
            for other, n, top in others:
                tile = fold(tile, stacks[other // B][source_at(other // B, other % B)], n, top, upward)
            out[M_SRC + at] = tile
        sides = jnp.where(lane < NSUB, low[ASG], pltpu.roll(high[ASG], NSUB, 1))
        out[M_ASG] = jnp.where(row < 3, sides, pltpu.roll(mid[ASG], 3, 0))


def line_asg(stacks, below, above, ty, b):
    if ty == 1:
        return stacks[b][ASG]
    tile = (below if ty == 0 else above)[M_ASG]
    return (tile, pltpu.roll(tile, 5, 0), pltpu.roll(tile, NSUB, 1))[b]


def around(u_ref, w_ref, p):
    u = u_ref[p + 1]
    return u, (
        (w_ref[0, p] * u_ref[p + 2] + w_ref[1, p] * u_ref[p])
        + (w_ref[2, p] * pltpu.roll(u, NP - 1, 0) + w_ref[3, p] * pltpu.roll(u, 1, 0))
        + (w_ref[4, p] * pltpu.roll(u, 2 * LZ - 1, 1) + w_ref[5, p] * pltpu.roll(u, 1, 1))
    )


def sweeps(both, w_ref, first, last, after=None, operator_at=-1):
    def one_sweep(k, carry):
        now = lax.rem(k, 2)
        src, dst = both.at[now], both.at[1 - now]
        count = NP - 2 * k
        keep = jnp.where(k == operator_at, 1.0, 1.0 - fine_relax)
        give = jnp.where(k == operator_at, -1.0 / fine_relax, 1.0)

        def chunk(i, carry):
            start = jnp.minimum(k + CHUNK * i, k + count - CHUNK)
            moved = []
            for j in range(CHUNK):
                u, near = around(src, w_ref, start + j)
                moved.append(keep * u + give * near)
            for j in range(CHUNK):
                dst[start + j + 1] = moved[j]
            return carry

        lax.fori_loop(0, (count + CHUNK - 1) // CHUNK, chunk, 0)
        if after is not None:
            after(k)
        return carry

    lax.fori_loop(first, last + 1, one_sweep, 0)


def own_tile(u_ref, w_ref, p):
    r, z = slice(B, 2 * B), slice(0, LZ)
    u, beyond = u_ref[p + 1, r, z], u_ref[p + 1, r, LZ:]
    lane = lanes((B, LZ))
    right = jnp.where(lane == LZ - 1, pltpu.roll(beyond, LZ - 1, 1), pltpu.roll(u, LZ - 1, 1))
    left = jnp.where(lane == 0, pltpu.roll(beyond, 1, 1), pltpu.roll(u, 1, 1))
    w = [w_ref[i, p, r, z] for i in range(6)]
    near = (
        (w[0] * u_ref[p + 2, r, z] + w[1] * u_ref[p, r, z])
        + (w[2] * u_ref[p + 1, B + 1 : 2 * B + 1, z] + w[3] * u_ref[p + 1, B - 1 : 2 * B - 1, z])
        + (w[4] * right + w[5] * left)
    )
    return (1.0 - fine_relax) * u + near


def label_sums(groups, sums):
    def one(s, carry):
        for first, labels, fields in groups:
            hits = [tile == s for tile in labels]
            for i, tiles in enumerate(fields):
                parts = [jnp.where(hit, tile, 0.0) for hit, tile in zip(hits, tiles)]
                while len(parts) > 1:
                    parts = [a + b for a, b in zip(parts[::2], parts[1::2])]
                sums[pl.ds(first + i * NSUB + s, 1), :] = jnp.sum(parts[0], axis=0, keepdims=True)
        return carry

    lax.fori_loop(0, NSUB, one, 0, unroll=16)


def three_parts(x):
    l1 = x.astype(bf16)
    rest = x - l1.astype(f32)
    l2 = rest.astype(bf16)
    return l1, l2, (rest - l2.astype(f32)).astype(bf16)


def lane_sums(sums):
    return lax.dot_general(
        jnp.ones((B, 3 * LZ), bf16), jnp.concatenate(three_parts(sums), axis=1),
        (((1,), (1,)), ((), ())), preferred_element_type=f32,
    )


def harmonic(a, b):
    return 2.0 * a * b / (a + b)


def row_product(tile):
    for by in (4, 2, 1):
        tile = tile * pltpu.roll(tile, by, 0)
    return tile


def positive(t):
    return jnp.where(t > 0.0, t, 1.0)


def near_and_far(tile, q):
    turned = pltpu.roll(tile, 64, 1)
    return jnp.where(q < 4, tile, turned), jnp.where(q < 4, turned, tile)


def halo_values(near, far):
    lane = lanes((B, LZ))
    near_side = lane < 64
    halo = (lane < W) | (lane >= LZ - W)
    source_halo = (lane < 4) | (lane >= LZ - 4)
    k = positive(jnp.where(halo, jnp.where(near_side, near, far), 1.0))
    own = jnp.where(near_side, pltpu.roll(near, LZ - 9, 1), pltpu.roll(near, 73, 1))
    src = jnp.where(near_side, pltpu.roll(near, LZ - 18, 1), pltpu.roll(near, 82, 1))
    return k, jnp.where(halo, own, 0.0).astype(i32), jnp.where(source_halo, src, 0.0)


def own_rows(low, mid, high, kmid, lmid, smid):
    for p in range(NP):
        stack, q = (low, mid, high)[p // B], p % B
        k, label, src = halo_values(*near_and_far(stack[HZ + q % 4], q))
        kmid[p, :, 0:LZ] = positive(stack[PERM + q])
        kmid[p, :, LZ:] = k
        lmid[p, :, 0:LZ] = stack[OWN + q].astype(i32)
        lmid[p, :, LZ:] = label
        if 4 <= p < 20:
            smid[p - 4, :, 0:LZ] = stack[source_at(p // B, q)]
            smid[p - 4, :, LZ:] = src


def first_sums(n_gx, n_gy, n_col, low, mid, high, below, above, flags, kmid, lmid, smid,
               weights, labels, chunk, dvals, paths, asg, kext, fx, both, masks, sums):
    gx, gy, col = (lax.axis_index(a) for a in ("gx", "gy", "col"))
    mids = (low, mid, high)
    lane = lanes((B, LZ))
    row = rows((B, LZ))
    def unfolded(ty, first, place):
        at, n = place
        tile = (below if ty == 0 else above)[first + at]
        return pltpu.roll(tile, (B - n if ty == 0 else n) % B, 0) if n else tile

    def beyond(ty, p):
        b, q = p // B, lax.rem(p, B)
        tile = (below if ty == 0 else above)[M_HZ + 4 * b + lax.rem(q, 4)]
        return halo_values(*near_and_far(tile, q))

    def fill(p, carry):
        kext[p + 1, B : 2 * B, :] = kmid[p]
        labels[p, B : 2 * B, :] = lmid[p]
        for ty in (0, 2):
            r = slice(ty * B, (ty + 1) * B)
            kext[p + 1, r, LZ:], labels[p, r, LZ:], _ = beyond(ty, p)
        return carry

    lax.fori_loop(0, NP, fill, 0, unroll=12)
    for p in range(NP):
        for ty in (0, 2):
            r = slice(ty * B, (ty + 1) * B)
            kext[p + 1, r, 0:LZ] = positive(unfolded(ty, M_PERM, FOLD_OF[p]))
            labels[p, r, 0:LZ] = unfolded(ty, M_OWN, FOLD_OF[p]).astype(i32)
    for b in range(3):
        for ty in range(3):
            asg[b, ty] = line_asg(mids, below, above, ty, b).astype(i32)
    kext[0] = jnp.ones(FULL, f32)
    kext[NP + 1] = jnp.ones(FULL, f32)

    flag_row = jnp.concatenate(
        [flags[1:2, :], jnp.where(lane[0:1] < 64, flags[2:3, :], flags[0:1, :])], axis=1
    )
    row_all, lane_all = rows(FULL), lanes(FULL)
    wrap_row = jnp.where(gy == 0, B - 1, jnp.where(gy == n_gy - 1, 2 * B - 1, -1))
    masks[0] = jnp.where(row_all == wrap_row, jnp.broadcast_to(flag_row, FULL), 1.0)
    closed = ((lane_all == LZ - 1) & (col == n_col - 1)) | ((lane_all == 2 * LZ - 1) & (col == 0))
    masks[1] = jnp.where(closed, 0.0, 1.0)

    def terms(p, carry):
        b = p // B
        out = ((b == 0) & (gx == 0)) | ((b == 2) & (gx == n_gx - 1))
        k = kext[p + 1]
        fy_up = harmonic(k, pltpu.roll(k, NP - 1, 0)) * masks[0]
        fy_down = pltpu.roll(fy_up, 1, 0)
        fz_right = harmonic(k, pltpu.roll(k, 2 * LZ - 1, 1)) * masks[1]
        fz_left = pltpu.roll(fz_right, 1, 1)
        k_next = kext[p + 2]
        fx_up = jnp.where((p == B - 1) & (gx == 0), k_next, harmonic(k, k_next))
        fx_up = jnp.where((p == 2 * B - 1) & (gx == n_gx - 1), k, fx_up)
        fx_down = carry
        diag = fx_up + fx_down + fy_up + fy_down + fz_right + fz_left
        scale = jnp.where(out, 0.0, fine_relax) / diag
        for i, face in enumerate((fx_up, fx_down, fy_up, fy_down, fz_right, fz_left)):
            weights[i, p] = face * scale
        both[0, p + 1] = scale
        dvals[p] = diag[B : 2 * B, 0:LZ]
        fx[p + 1] = fx_up
        return fx_up

    lax.fori_loop(0, NP, terms, harmonic(kext[0], kext[1]), unroll=8)


    def start(i, carry):
        p = i + B // 2
        over = both[0, p + 1] * (1.0 / fine_relax)
        both[1, p + 1, B : 2 * B, :] = smid[i] * over[B : 2 * B]
        for ty in (0, 2):
            r = slice(ty * B, (ty + 1) * B)
            both[1, p + 1, r, LZ:] = beyond(ty, p)[2] * over[r, LZ:]
        return carry

    lax.fori_loop(0, 2 * B, start, 0, unroll=16)
    for p in range(B // 2, NP - B // 2):
        for ty in (0, 2):
            r = slice(ty * B, (ty + 1) * B)
            if p in SRC_OF:
                over = both[0, p + 1, r, 0:LZ] * (1.0 / fine_relax)
                both[1, p + 1, r, 0:LZ] = unfolded(ty, M_SRC, SRC_OF[p]) * over
            else:
                both[1, p + 1, r, 0:LZ] = jnp.zeros((B, LZ), f32)

    r = slice(B, 2 * B)
    for q in range(B):
        p = B + q
        up, down = weights[2, p, r, 0:LZ], weights[3, p, r, 0:LZ]
        rise = row_product(jnp.where(row == 0, 1.0, down)) * up
        fall = row_product(jnp.where(row == B - 1, 1.0, up)) * down
        per = dvals[p] * (1.0 / fine_relax)
        paths[2, q : q + 1, :] = (rise * per)[B - 1 : B]
        paths[3, q : q + 1, :] = (fall * per)[0:1]
    rise, fall = fx[2 * B, B : 2 * B, 0:LZ], fx[B, B : 2 * B, 0:LZ]
    for p in range(B + 1, 2 * B):
        rise = rise * weights[1, p, B : 2 * B, 0:LZ]
        fall = fall * weights[0, p - 1, B : 2 * B, 0:LZ]
    paths[0] = rise
    paths[1] = fall

    sweeps(both, weights, 5, 7)
    tiles = [own_tile(both.at[0], weights, B + q) * dvals[B + q] for q in range(B)]
    diag_tiles = [dvals[B + q] for q in range(B)]
    label_tiles = [labels[B + q, B : 2 * B, 0:LZ] for q in range(B)]
    label_sums([(0, label_tiles, (tiles, diag_tiles))], sums)
    totals = lane_sums(sums[...])

    own = spread(mid[ASG, 0:1, :])
    own = jnp.where(lane < NSUB, own, pltpu.roll(own, NSUB, 1))
    tile = jnp.where(row == 0, totals, own)[0:2]
    for d in range(n_gy * n_col):
        chunk[d] = tile


def one_hot_product(lefts, lows):
    left = jnp.concatenate(lefts, axis=1)
    wide = rows((LZ, LZ))
    right = jnp.concatenate(
        [
            jnp.where(jnp.broadcast_to(low, (LZ, LZ)) == wide, 1.0, 0.0).astype(bf16)
            for low in lows
        ],
        axis=1,
    )
    return lax.dot_general(
        jnp.concatenate(three_parts(left), axis=0), right, (((1,), (1,)), ((), ())),
        preferred_element_type=f32,
    )


def joined(total):
    n = total.shape[0] // 3
    return (total[2 * n :] + total[n : 2 * n]) + total[:n]


def halves(value, high):
    lane = lanes((B, LZ))
    scaled = jnp.where(high == rows((B, LZ)), value, 0.0)
    return jnp.concatenate(
        [jnp.where(lane < NSUB, scaled, 0.0), jnp.where(lane < NSUB, 0.0, scaled)], axis=0
    )


GROUP = 64


def first_coarse(n_bricks, n_out, values, out):
    def one(i, total):
        lefts, lows = [], []
        for j in range(min(GROUP, n_bricks)):
            value = values[i * min(GROUP, n_bricks) + j]
            a = value[1:2].astype(i32)
            lefts.append(halves(spread(value[0:1]), spread(a >> 7)))
            lows.append(a & 127)
        return total + one_hot_product(lefts, lows)

    total = lax.fori_loop(0, n_bricks // min(GROUP, n_bricks), one, jnp.zeros((6 * B, LZ), f32))
    total = joined(total)
    for d in range(n_out):
        out[d] = total


def second_coarse(n_gy, n_col, n_out, values, first, out):
    n_bricks = n_gy * n_col
    lane = lanes((B, LZ))
    near = lanes((1, LZ)) < NSUB

    def own(j):
        before = lax.rem(j + n_bricks - n_col, n_bricks)
        after = lax.rem(j + n_col, n_bricks)
        mine = spread(values[j, 0:1] + values[before, 2:3])
        return mine + pltpu.roll(spread(values[after, 2:3]), NSUB, 1)

    def one(i, totals):
        lefts, lows, edge_lefts, edge_lows = [], [], [], []
        for j in range(min(GROUP, n_bricks) // 2):
            at = i * min(GROUP, n_bricks) + 2 * j
            pair = jnp.where(lane < NSUB, own(at), pltpu.roll(own(at + 1), NSUB, 1))
            a = jnp.where(near, first[at, 1:2], first[at + 1, 1:2]).astype(i32)
            lefts.append(jnp.where(spread(a >> 7) == rows((B, LZ)), pair, 0.0))
            lows.append(a & 127)
        for j in range(min(GROUP, n_bricks)):
            a = values[i * min(GROUP, n_bricks) + j, 3:4].astype(i32)
            edge_lefts.append(halves(spread(values[i * min(GROUP, n_bricks) + j, 1:2]), spread(a >> 7)))
            edge_lows.append(a & 127)
        return (
            totals[0] + one_hot_product(lefts, lows),
            totals[1] + one_hot_product(edge_lefts, edge_lows),
        )

    mine, edges = lax.fori_loop(
        0, n_bricks // min(GROUP, n_bricks), one, (jnp.zeros((3 * B, LZ), f32), jnp.zeros((6 * B, LZ), f32))
    )
    total = jnp.concatenate([joined(mine), joined(edges)], axis=0)
    for d in range(n_out):
        out[d] = total


def lookup(table, index):
    low, high = index & 127, index >> 7
    result = jnp.zeros((B, LZ), f32)
    for h in range(B):
        got = jnp.take_along_axis(spread(table[h : h + 1]), low, axis=1)
        result = jnp.where(high == h, got, result)
    return result


def pick(row, index):
    return jnp.take_along_axis(spread(row), index, axis=1)


def slab_total(parts, g, n_gx, part, size):
    total = parts[jnp.clip(g, 0, n_gx - 1), part : part + size]
    return jnp.where((g >= 0) & (g < n_gx), total, 0.0)


def guess(parts, g, n_gx):
    total = slab_total(parts, g, n_gx, 0, 2 * B)
    exists = (g >= 0) & (g < n_gx)
    rhs, diag = total[0:B], jnp.where(exists, total[B : 2 * B], 1.0)
    return rhs, diag, coarse_relax * rhs / diag


def expand(coarse, asg, labels, u, tables, first, last):
    near_side = lanes((B, LZ)) < 64

    def table(i, carry):
        b, ty = i // 3, lax.rem(i, 3)
        tables[b, ty] = lookup(coarse[b], asg[b, ty])
        return carry

    lax.fori_loop(0, 9, table, 0, unroll=3)

    def one(p, carry):
        b = p // B
        for ty in range(3):
            r = slice(ty * B, (ty + 1) * B)
            t = tables[b, ty]
            u[p + 1, r, 0:LZ] = pick(t[0:1], labels[p, r, 0:LZ])
            lab = labels[p, r, LZ:]
            u[p + 1, r, LZ:] = jnp.where(near_side, pick(t[1:2], lab), pick(t[2:3], lab))
        return carry

    lax.fori_loop(first, last + 1, one, 0, unroll=8)


def second_sums(n_gx, n_gy, n_col, parts, weights, labels, asg, dvals, paths,
                chunk, both, coarse, tables, ends, sums):
    gx = lax.axis_index("gx")
    row = rows((B, LZ))
    r = slice(B, 2 * B)
    for i in range(3):
        coarse[i] = guess(parts, gx + i - 1, n_gx)[2]
    expand(coarse, asg, labels, both.at[0], tables, 0, NP - 1)

    def after(k):
        @pl.when(k == 0)
        def _():
            first = both.at[1]
            zero = jnp.zeros(FULL, f32)
            first[1] = zero
            first[NP] = zero
            first[:, 0:1, :] = jnp.zeros((NP + 2, 1, 2 * LZ), f32)
            first[:, NP - 1 :, :] = jnp.zeros((NP + 2, 1, 2 * LZ), f32)
            ends[0] = first[B + 1, r, 0:LZ] * -paths[0]
            ends[1] = first[2 * B, r, 0:LZ] * -paths[1]
            for q in range(B):
                plane = first[B + 1 + q, r, 0:LZ]
                ends[2, q : q + 1, :] = plane[0:1] * -paths[2, q : q + 1, :]
                ends[3, q : q + 1, :] = plane[B - 1 : B] * -paths[3, q : q + 1, :]

    sweeps(both, weights, 0, 7, after=after, operator_at=4)
    tiles = [own_tile(both.at[0], weights, B + q) * dvals[B + q] for q in range(B)]
    label_tiles = [labels[B + q, r, 0:LZ] for q in range(B)]
    beyond = [labels[2 * B, r, 0:LZ], labels[B - 1, r, 0:LZ]]
    for at in (2 * B, B - 1):
        edge = labels[B, at : at + 1, 0:LZ]
        edge = spread(edge)
        for q in range(1, B):
            edge = jnp.where(row == q, spread(labels[B + q, at : at + 1, 0:LZ]), edge)
        beyond.append(edge)
    groups = [(0, label_tiles, (tiles,))]
    groups += [((2 + i) * NSUB, [beyond[i]], ([ends[i]],)) for i in range(4)]
    sums[NSUB : 2 * NSUB, :] = jnp.zeros((NSUB, LZ), f32)
    label_sums(groups, sums)
    totals = lane_sums(sums[...])
    right, left = (spread(asg[b, 1, 0:1, :].astype(f32)) for b in (2, 0))
    sides = jnp.where(lanes((B, LZ)) < NSUB, right, pltpu.roll(left, NSUB, 1))
    tile = jnp.where(
        row < 2,
        jnp.where(row == 0, totals[:, 0:LZ], totals[:, LZ : 2 * LZ]),
        jnp.where(row == 2, totals[:, 2 * LZ :], sides),
    )[0:4]
    for d in range(n_gy * n_col):
        chunk[d] = tile


def last_sweeps(n_gx, n_gy, n_col, parts, images, weights, labels, asg,
                pressure, coarse_out, both, coarse, tables):
    gx, gy, col = (lax.axis_index(a) for a in ("gx", "gy", "col"))
    for i in range(3):
        g = gx + i - 1
        rhs, diag, start = guess(parts, g, n_gx)
        image = (
            slab_total(images, g, n_gx, 0, B)
            + slab_total(images, g - 1, n_gx, B, B)
            + slab_total(images, g + 1, n_gx, 2 * B, B)
        )
        second = start + coarse_relax * (rhs - image) / diag
        coarse[i] = jnp.where((g >= 0) & (g < n_gx), second, 0.0)
    share = B * LZ // (n_gy * n_col)
    per_row = LZ // share
    mine = gy * n_col + col
    row = coarse[1, pl.ds(mine // per_row, 1), :]
    turned = pltpu.roll(spread(row), lax.rem(LZ - lax.rem(mine, per_row) * share, LZ), 1)
    coarse_out[...] = turned[0:1, 0:share]
    expand(coarse, asg, labels, both.at[1], tables, 4, 19)
    sweeps(both, weights, 5, 7)
    for q in range(B):
        pressure[q] = own_tile(both.at[0], weights, B + q)


def steps(count, by, wrap):
    return [
        (i, (i + by) % count) for i in range(count) if wrap or 0 <= i + by < count
    ]


def on_device(n_gx, n_gy, n_col, permeability, source, ownership, assignment, layer_flags):
    n_bricks = n_gy * n_col
    sizes = (n_gx, n_gy, n_col)
    vm = pltpu.VMEM
    fields = vm((2, NP + 2, *FULL), f32)
    plane = (B, B, LZ)

    def send(x, axis, by, wrap=False):
        return lax.ppermute(x, axis, steps(lax.axis_size(axis), by, wrap))

    mr, ml, base, flags = call(
        z_messages,
        [pinned(B // 2 + 1, B, LZ)] * 2 + [pinned(3 * B + 1, B, LZ), pinned(3, LZ)],
        5,
        scratch=[
            vm(plane, f32), vm(plane, f32), vm(plane, i32), vm((1, NSUB), i32),
            vm((n_col, LZ), i32), pltpu.SemaphoreType.DMA((5,)),
        ],
        space=pl.ANY,
        limit=WHOLE_VMEM,
    )(permeability, source, ownership, assignment.reshape(1, NSUB), layer_flags.reshape(n_col, LZ))
    mr, ml = send(mr, "col", -1), send(ml, "col", 1)
    mid, to_low, to_high = call(
        stack_up, [sds(STACK, B, LZ)] + [sds(X_MESSAGE, B, LZ)] * 2, 3
    )(base, mr, ml)
    low, high = send(to_high, "gx", 1), send(to_low, "gx", -1)
    up, down = call(y_messages, [sds(MESSAGE, B, LZ)] * 2, 3)(low, mid, high)
    below, above = send(up, "gy", 1, True), send(down, "gy", -1, True)
    middle = call(
        own_rows,
        [sds(NP, B, 2 * LZ), sds(NP, B, 2 * LZ, dtype=i32), sds(2 * B, B, 2 * LZ)],
        3,
        cost=pl.CostEstimate(flops=1000000, bytes_accessed=1000000, transcendentals=0),
    )(low, mid, high)

    weights, labels, chunk, dvals, paths, asg = call(
        functools.partial(first_sums, *sizes),
        [
            sds(6, NP, *FULL), sds(NP, *FULL, dtype=i32), sds(n_bricks, 2, LZ), sds(NP, B, LZ),
            sds(4, B, LZ), sds(3, 3, B, LZ, dtype=i32),
        ],
        9,
        scratch=[
            vm((NP + 2, *FULL), f32), vm((NP + 1, *FULL), f32), fields, vm((2, *FULL), f32),
            vm((2 * NSUB, LZ), f32),
        ],
    )(low, mid, high, below, above, flags, *middle)
    bricks = lax.all_to_all(chunk, ("gy", "col"), 0, 0, tiled=True)
    parts = call(
        functools.partial(first_coarse, n_bricks, n_gx), sds(n_gx, 2 * B, LZ), 1
    )(bricks)
    parts = lax.all_to_all(parts, "gx", 0, 0, tiled=True)
    tables = [vm((3, B, LZ), f32), vm((3, 3, B, LZ), f32)]
    chunk = call(
        functools.partial(second_sums, *sizes),
        sds(n_bricks, 4, LZ),
        6,
        scratch=[fields, *tables, vm((4, B, LZ), f32), vm((6 * NSUB, LZ), f32)],
    )(parts, weights, labels, asg, dvals, paths)
    images = lax.all_to_all(chunk, ("gy", "col"), 0, 0, tiled=True)
    images = call(
        functools.partial(second_coarse, n_gy, n_col, n_gx), sds(n_gx, 3 * B, LZ), 2
    )(images, bricks)
    images = lax.all_to_all(images, "gx", 0, 0, tiled=True)
    return call(
        functools.partial(last_sweeps, *sizes),
        [sds(*plane), sds(1, B * LZ // (n_gy * n_col))],
        5,
        scratch=[fields, *tables],
    )(parts, images, weights, labels, asg)


def solution(mesh):
    placed = (
        P("gx", "gy", "col"),
        P("gx", "gy", "col"),
        P("gx", "gy", "col"),
        P("gx", "gy", "col", None),
        P(),
    )
    sizes = mesh.shape
    return jax.shard_map(
        functools.partial(on_device, sizes["gx"], sizes["gy"], sizes["col"]),
        mesh=mesh,
        in_specs=placed,
        out_specs=(P("gx", "gy", "col"), P("gx", ("gy", "col"))),
        check_vma=False,
    )
```

```python
import functools

import jax
import jax.numpy as jnp
from jax import lax
from jax.experimental import pallas as pl
from jax.experimental.pallas import tpu as pltpu
from jax.sharding import PartitionSpec as P

f32 = jnp.float32
i32 = jnp.int32
bf16 = jnp.bfloat16
NSUB = 64
B = 8
LZ = 128
NP = 3 * B
W = 9
FULL = (NP, 2 * LZ)
CHUNK = 12
fine_relax = 0.6666667
coarse_relax = 0.7
VMEM_LIMIT = 48 * 1024 * 1024
WHOLE_VMEM = 63 * 1024 * 1024

PERM, OWN, HZ, ASG, SRC = 0, 8, 16, 20, 21
STACK = 29
X_MESSAGE = 25

FOLDS = [(p, None, 0) for p in range(7, 17)]
FOLDS += [(6, 0, 1), (5, 1, 2), (4, 2, 3), (17, 23, 1), (18, 22, 2), (19, 21, 3), (3, 20, 4)]
FOLD_OF = {}
for _at, (_main, _other, _rows) in enumerate(FOLDS):
    FOLD_OF[_main] = (_at, 0)
    if _other is not None:
        FOLD_OF[_other] = (_at, _rows)
N_FOLD = len(FOLDS)
M_PERM, M_OWN, M_HZ, M_ASG, M_SRC = 0, N_FOLD, 2 * N_FOLD, 2 * N_FOLD + 12, 2 * N_FOLD + 13
SRC_FOLDS = [(8 + q, ((12 + q, 4, 4),)) for q in range(4)]
SRC_FOLDS += [(7, ((6, 2, 2), (5, 1, 3))), (16, ((17, 2, 2), (18, 1, 3)))]
SRC_OF = {}
for _at, (_main, _others) in enumerate(SRC_FOLDS):
    SRC_OF[_main] = (_at, 0)
    for _other, _rows, _top in _others:
        SRC_OF[_other] = (_at, _top)
MESSAGE = M_SRC + len(SRC_FOLDS)


def lanes(shape):
    return lax.broadcasted_iota(i32, shape, len(shape) - 1)


def rows(shape):
    return lax.broadcasted_iota(i32, shape, len(shape) - 2)


def sds(*shape, dtype=f32):
    return jax.ShapeDtypeStruct(shape, dtype)


def pinned(*shape):
    return pltpu.VMEM(shape, f32)


def call(kernel, outs, n_in, scratch=(), space=pltpu.VMEM, limit=VMEM_LIMIT, cost=None):
    single = not isinstance(outs, (list, tuple))
    vm = pl.BlockSpec(memory_space=pltpu.VMEM)
    return pl.pallas_call(
        kernel,
        out_shape=outs,
        in_specs=[pl.BlockSpec(memory_space=space)] * n_in,
        out_specs=vm if single else [vm] * len(outs),
        scratch_shapes=list(scratch),
        compiler_params=pltpu.CompilerParams(vmem_limit_bytes=limit),
        cost_estimate=cost,
    )


def spread(row):
    return jnp.broadcast_to(row, (B, LZ))


def asg_tile(asg):
    tile = jnp.concatenate([asg[...].astype(f32), jnp.zeros((1, LZ - NSUB), f32)], axis=1)
    return jnp.where(rows((B, LZ)) == 0, spread(tile), 0.0)


def z_messages(perm_in, src_in, own_in, asg_in, flags_in, mr, ml, base, flags_out,
               perm, src, own, asg, flags, sem):
    copies = [
        pltpu.make_async_copy(a, b, sem.at[i])
        for i, (a, b) in enumerate(
            ((perm_in, perm), (src_in, src), (own_in, own), (asg_in, asg), (flags_in, flags))
        )
    ]
    for copy in copies:
        copy.start()
    for copy in copies:
        copy.wait()
    lane = lanes((B, LZ))

    def first_cells(q):
        k, s, o = perm[q], src[q], own[q].astype(f32)
        return jnp.where(
            lane < 9, k, jnp.where(lane < 18, pltpu.roll(o, 9, 1), pltpu.roll(s, 18, 1))
        )

    def last_cells(q):
        k, s, o = perm[q], src[q], own[q].astype(f32)
        return jnp.where(
            lane >= 55,
            pltpu.roll(k, 64, 1),
            jnp.where(lane >= 46, pltpu.roll(o, 55, 1), pltpu.roll(s, 46, 1)),
        )

    for out, cells in ((mr, first_cells), (ml, last_cells)):
        for q in range(B // 2):
            out[q] = jnp.where(lane < 64, cells(q), pltpu.roll(cells(q + B // 2), 64, 1))
        out[B // 2] = asg_tile(asg)
    for q in range(B):
        base[q], base[B + q], base[2 * B + q] = perm[q], own[q].astype(f32), src[q]
    base[3 * B] = asg_tile(asg)
    col, n_col = lax.axis_index("col"), flags.shape[0]
    for i, at in enumerate((col - 1, col, col + 1)):
        at = jnp.clip(at, 0, n_col - 1)
        flags_out[pl.ds(i, 1), :] = flags[pl.ds(at, 1), :].astype(f32)


def source_at(b, q):
    return SRC + (q - 4 if b == 0 else q)


def stack_up(base, mr, ml, stack, to_low, to_high):
    lane = lanes((B, LZ))
    row = rows((B, LZ))
    for q in range(B):
        stack[PERM + q] = base[q]
        stack[OWN + q] = base[B + q]
        stack[SRC + q] = base[2 * B + q]
    for q in range(B // 2):
        stack[HZ + q] = jnp.where((lane & 63) < 32, mr[q], ml[q])
    at = B // 2
    stack[ASG] = jnp.where(
        row == 1, spread(mr[at, 0:1, :]), jnp.where(row == 2, spread(ml[at, 0:1, :]), base[3 * B])
    )
    for out, first in ((to_low, 0), (to_high, 4)):
        out[0:SRC] = stack[0:SRC]
        for q in range(4):
            out[SRC + q] = base[2 * B + first + q]


def y_messages(low, mid, high, up, down):
    stacks = (low, mid, high)
    row = rows((B, LZ))
    lane = lanes((B, LZ))

    def fold(main, other, n, top, upward):
        if upward:
            return jnp.where((row >= top - n) & (row < top), pltpu.roll(other, top, 0), main)
        return jnp.where(
            (row >= B - top) & (row < B - top + n), pltpu.roll(other, B - top, 0), main
        )

    for out, upward in ((up, True), (down, False)):
        for field, first in ((PERM, M_PERM), (OWN, M_OWN)):
            for at, (main, other, n) in enumerate(FOLDS):
                tile = stacks[main // B][field + main % B]
                if other is not None:
                    tile = fold(tile, stacks[other // B][field + other % B], n, n, upward)
                out[first + at] = tile
        for b in range(3):
            for q in range(B // 2):
                out[M_HZ + 4 * b + q] = stacks[b][HZ + q]
        for at, (main, others) in enumerate(SRC_FOLDS):
            tile = stacks[main // B][source_at(main // B, main % B)]
            for other, n, top in others:
                tile = fold(tile, stacks[other // B][source_at(other // B, other % B)], n, top, upward)
            out[M_SRC + at] = tile
        sides = jnp.where(lane < NSUB, low[ASG], pltpu.roll(high[ASG], NSUB, 1))
        out[M_ASG] = jnp.where(row < 3, sides, pltpu.roll(mid[ASG], 3, 0))


def line_asg(stacks, below, above, ty, b):
    if ty == 1:
        return stacks[b][ASG]
    tile = (below if ty == 0 else above)[M_ASG]
    return (tile, pltpu.roll(tile, 5, 0), pltpu.roll(tile, NSUB, 1))[b]


def around(u_ref, w_ref, p):
    u = u_ref[p + 1]
    return u, (
        (w_ref[0, p] * u_ref[p + 2] + w_ref[1, p] * u_ref[p])
        + (w_ref[2, p] * pltpu.roll(u, NP - 1, 0) + w_ref[3, p] * pltpu.roll(u, 1, 0))
        + (w_ref[4, p] * pltpu.roll(u, 2 * LZ - 1, 1) + w_ref[5, p] * pltpu.roll(u, 1, 1))
    )


def sweeps(both, w_ref, first, last, after=None, operator_at=-1):
    def one_sweep(k, carry):
        now = lax.rem(k, 2)
        src, dst = both.at[now], both.at[1 - now]
        count = NP - 2 * k
        keep = jnp.where(k == operator_at, 1.0, 1.0 - fine_relax)
        give = jnp.where(k == operator_at, -1.0 / fine_relax, 1.0)

        def chunk(i, carry):
            start = jnp.minimum(k + CHUNK * i, k + count - CHUNK)
            moved = []
            for j in range(CHUNK):
                u, near = around(src, w_ref, start + j)
                moved.append(keep * u + give * near)
            for j in range(CHUNK):
                dst[start + j + 1] = moved[j]
            return carry

        lax.fori_loop(0, (count + CHUNK - 1) // CHUNK, chunk, 0)
        if after is not None:
            after(k)
        return carry

    lax.fori_loop(first, last + 1, one_sweep, 0)


def own_tile(u_ref, w_ref, p):
    r, z = slice(B, 2 * B), slice(0, LZ)
    u, beyond = u_ref[p + 1, r, z], u_ref[p + 1, r, LZ:]
    lane = lanes((B, LZ))
    right = jnp.where(lane == LZ - 1, pltpu.roll(beyond, LZ - 1, 1), pltpu.roll(u, LZ - 1, 1))
    left = jnp.where(lane == 0, pltpu.roll(beyond, 1, 1), pltpu.roll(u, 1, 1))
    w = [w_ref[i, p, r, z] for i in range(6)]
    near = (
        (w[0] * u_ref[p + 2, r, z] + w[1] * u_ref[p, r, z])
        + (w[2] * u_ref[p + 1, B + 1 : 2 * B + 1, z] + w[3] * u_ref[p + 1, B - 1 : 2 * B - 1, z])
        + (w[4] * right + w[5] * left)
    )
    return (1.0 - fine_relax) * u + near


def label_sums(groups, sums):
    def one(s, carry):
        for first, labels, fields in groups:
            hits = [tile == s for tile in labels]
            for i, tiles in enumerate(fields):
                parts = [jnp.where(hit, tile, 0.0) for hit, tile in zip(hits, tiles)]
                while len(parts) > 1:
                    parts = [a + b for a, b in zip(parts[::2], parts[1::2])]
                sums[pl.ds(first + i * NSUB + s, 1), :] = jnp.sum(parts[0], axis=0, keepdims=True)
        return carry

    lax.fori_loop(0, NSUB, one, 0, unroll=16)


def three_parts(x):
    high = x.astype(bf16).astype(f32)
    rest = x - high
    middle = rest.astype(bf16).astype(f32)
    return high, middle, rest - middle


def lane_sums(sums):
    parts = jnp.concatenate(three_parts(sums), axis=1).astype(bf16)
    total = lax.dot_general(
        jnp.ones((2 * B, 3 * LZ), bf16), parts,
        (((1,), (1,)), ((), ())), preferred_element_type=f32,
    )
    return total[0:B]


def harmonic(a, b):
    return 2.0 * a * b / (a + b)


def row_product(tile):
    for by in (4, 2, 1):
        tile = tile * pltpu.roll(tile, by, 0)
    return tile


def positive(t):
    return jnp.where(t > 0.0, t, 1.0)


def near_and_far(tile, q):
    turned = pltpu.roll(tile, 64, 1)
    return jnp.where(q < 4, tile, turned), jnp.where(q < 4, turned, tile)


def halo_values(near, far):
    lane = lanes((B, LZ))
    near_side = lane < 64
    halo = (lane < W) | (lane >= LZ - W)
    source_halo = (lane < 4) | (lane >= LZ - 4)
    k = positive(jnp.where(halo, jnp.where(near_side, near, far), 1.0))
    own = jnp.where(near_side, pltpu.roll(near, LZ - 9, 1), pltpu.roll(near, 73, 1))
    src = jnp.where(near_side, pltpu.roll(near, LZ - 18, 1), pltpu.roll(near, 82, 1))
    return k, jnp.where(halo, own, 0.0).astype(i32), jnp.where(source_halo, src, 0.0)


def own_rows(low, mid, high, kmid, lmid, smid):
    for p in range(NP):
        stack, q = (low, mid, high)[p // B], p % B
        k, label, src = halo_values(*near_and_far(stack[HZ + q % 4], q))
        kmid[p, :, 0:LZ] = positive(stack[PERM + q])
        kmid[p, :, LZ:] = k
        lmid[p, :, 0:LZ] = stack[OWN + q].astype(i32)
        lmid[p, :, LZ:] = label
        if 4 <= p < 20:
            smid[p - 4, :, 0:LZ] = stack[source_at(p // B, q)]
            smid[p - 4, :, LZ:] = src


def first_sums(n_gx, n_gy, n_col, low, mid, high, below, above, flags, kmid, lmid, smid,
               weights, labels, chunk, dvals, paths, asg, kext, fx, both, masks, sums):
    gx, gy, col = (lax.axis_index(a) for a in ("gx", "gy", "col"))
    mids = (low, mid, high)
    lane = lanes((B, LZ))
    row = rows((B, LZ))
    def unfolded(ty, first, place):
        at, n = place
        tile = (below if ty == 0 else above)[first + at]
        return pltpu.roll(tile, (B - n if ty == 0 else n) % B, 0) if n else tile

    def beyond(ty, p):
        b, q = p // B, lax.rem(p, B)
        tile = (below if ty == 0 else above)[M_HZ + 4 * b + lax.rem(q, 4)]
        return halo_values(*near_and_far(tile, q))

    def fill(p, carry):
        kext[p + 1, B : 2 * B, :] = kmid[p]
        labels[p, B : 2 * B, :] = lmid[p]
        for ty in (0, 2):
            r = slice(ty * B, (ty + 1) * B)
            kext[p + 1, r, LZ:], labels[p, r, LZ:], _ = beyond(ty, p)
        return carry

    lax.fori_loop(0, NP, fill, 0, unroll=12)
    for p in range(NP):
        for ty in (0, 2):
            r = slice(ty * B, (ty + 1) * B)
            kext[p + 1, r, 0:LZ] = positive(unfolded(ty, M_PERM, FOLD_OF[p]))
            labels[p, r, 0:LZ] = unfolded(ty, M_OWN, FOLD_OF[p]).astype(i32)
    for b in range(3):
        for ty in range(3):
            asg[b, ty] = line_asg(mids, below, above, ty, b).astype(i32)
    kext[0] = jnp.ones(FULL, f32)
    kext[NP + 1] = jnp.ones(FULL, f32)

    flag_row = jnp.concatenate(
        [flags[1:2, :], jnp.where(lane[0:1] < 64, flags[2:3, :], flags[0:1, :])], axis=1
    )
    row_all, lane_all = rows(FULL), lanes(FULL)
    wrap_row = jnp.where(gy == 0, B - 1, jnp.where(gy == n_gy - 1, 2 * B - 1, -1))
    masks[0] = jnp.where(row_all == wrap_row, jnp.broadcast_to(flag_row, FULL), 1.0)
    closed = ((lane_all == LZ - 1) & (col == n_col - 1)) | ((lane_all == 2 * LZ - 1) & (col == 0))
    masks[1] = jnp.where(closed, 0.0, 1.0)

    def terms(p, carry):
        b = p // B
        out = ((b == 0) & (gx == 0)) | ((b == 2) & (gx == n_gx - 1))
        k = kext[p + 1]
        fy_up = harmonic(k, pltpu.roll(k, NP - 1, 0)) * masks[0]
        fy_down = pltpu.roll(fy_up, 1, 0)
        fz_right = harmonic(k, pltpu.roll(k, 2 * LZ - 1, 1)) * masks[1]
        fz_left = pltpu.roll(fz_right, 1, 1)
        k_next = kext[p + 2]
        fx_up = jnp.where((p == B - 1) & (gx == 0), k_next, harmonic(k, k_next))
        fx_up = jnp.where((p == 2 * B - 1) & (gx == n_gx - 1), k, fx_up)
        fx_down = carry
        diag = fx_up + fx_down + fy_up + fy_down + fz_right + fz_left
        scale = jnp.where(out, 0.0, fine_relax) / diag
        for i, face in enumerate((fx_up, fx_down, fy_up, fy_down, fz_right, fz_left)):
            weights[i, p] = face * scale
        both[0, p + 1] = scale
        dvals[p] = diag[B : 2 * B, 0:LZ]
        fx[p + 1] = fx_up
        return fx_up

    lax.fori_loop(0, NP, terms, harmonic(kext[0], kext[1]), unroll=8)


    def start(i, carry):
        p = i + B // 2
        over = both[0, p + 1] * (1.0 / fine_relax)
        both[1, p + 1, B : 2 * B, :] = smid[i] * over[B : 2 * B]
        for ty in (0, 2):
            r = slice(ty * B, (ty + 1) * B)
            both[1, p + 1, r, LZ:] = beyond(ty, p)[2] * over[r, LZ:]
        return carry

    lax.fori_loop(0, 2 * B, start, 0, unroll=16)
    for p in range(B // 2, NP - B // 2):
        for ty in (0, 2):
            r = slice(ty * B, (ty + 1) * B)
            if p in SRC_OF:
                over = both[0, p + 1, r, 0:LZ] * (1.0 / fine_relax)
                both[1, p + 1, r, 0:LZ] = unfolded(ty, M_SRC, SRC_OF[p]) * over
            else:
                both[1, p + 1, r, 0:LZ] = jnp.zeros((B, LZ), f32)

    r = slice(B, 2 * B)
    for q in range(B):
        p = B + q
        up, down = weights[2, p, r, 0:LZ], weights[3, p, r, 0:LZ]
        rise = row_product(jnp.where(row == 0, 1.0, down)) * up
        fall = row_product(jnp.where(row == B - 1, 1.0, up)) * down
        per = dvals[p] * (1.0 / fine_relax)
        paths[2, q : q + 1, :] = (rise * per)[B - 1 : B]
        paths[3, q : q + 1, :] = (fall * per)[0:1]
    rise, fall = fx[2 * B, B : 2 * B, 0:LZ], fx[B, B : 2 * B, 0:LZ]
    for p in range(B + 1, 2 * B):
        rise = rise * weights[1, p, B : 2 * B, 0:LZ]
        fall = fall * weights[0, p - 1, B : 2 * B, 0:LZ]
    paths[0] = rise
    paths[1] = fall

    sweeps(both, weights, 5, 7)
    tiles = [own_tile(both.at[0], weights, B + q) * dvals[B + q] for q in range(B)]
    diag_tiles = [dvals[B + q] for q in range(B)]
    label_tiles = [labels[B + q, B : 2 * B, 0:LZ] for q in range(B)]
    label_sums([(0, label_tiles, (tiles, diag_tiles))], sums)
    totals = lane_sums(sums[...])

    own = spread(mid[ASG, 0:1, :])
    own = jnp.where(lane < NSUB, own, pltpu.roll(own, NSUB, 1))
    tile = jnp.where(row == 0, totals, own)[0:2]
    for d in range(n_gy * n_col):
        chunk[d] = tile


def one_hot_product(lefts, lows):
    left = jnp.concatenate(lefts, axis=1)
    wide = rows((LZ, LZ))
    right = jnp.concatenate(
        [
            jnp.where(jnp.broadcast_to(low, (LZ, LZ)) == wide, 1.0, 0.0).astype(bf16)
            for low in lows
        ],
        axis=1,
    )
    parts = three_parts(left)
    if left.shape[0] % (2 * B):
        parts += (jnp.zeros_like(left),)
    return lax.dot_general(
        jnp.concatenate(parts, axis=0).astype(bf16), right, (((1,), (1,)), ((), ())),
        preferred_element_type=f32,
    )


def joined(total, n):
    return (total[2 * n : 3 * n] + total[n : 2 * n]) + total[:n]


def halves(value, high):
    lane = lanes((B, LZ))
    scaled = jnp.where(high == rows((B, LZ)), value, 0.0)
    return jnp.concatenate(
        [jnp.where(lane < NSUB, scaled, 0.0), jnp.where(lane < NSUB, 0.0, scaled)], axis=0
    )


GROUP = 64


def first_coarse(n_bricks, n_out, values, out):
    def one(i, total):
        lefts, lows = [], []
        for j in range(min(GROUP, n_bricks)):
            value = values[i * min(GROUP, n_bricks) + j]
            a = value[1:2].astype(i32)
            lefts.append(halves(spread(value[0:1]), spread(a >> 7)))
            lows.append(a & 127)
        return total + one_hot_product(lefts, lows)

    total = lax.fori_loop(0, n_bricks // min(GROUP, n_bricks), one, jnp.zeros((6 * B, LZ), f32))
    total = joined(total, 2 * B)
    for d in range(n_out):
        out[d] = total


def second_coarse(n_gy, n_col, n_out, values, first, out):
    n_bricks = n_gy * n_col
    lane = lanes((B, LZ))
    near = lanes((1, LZ)) < NSUB

    def own(j):
        before = lax.rem(j + n_bricks - n_col, n_bricks)
        after = lax.rem(j + n_col, n_bricks)
        mine = spread(values[j, 0:1] + values[before, 2:3])
        return mine + pltpu.roll(spread(values[after, 2:3]), NSUB, 1)

    def one(i, totals):
        lefts, lows, edge_lefts, edge_lows = [], [], [], []
        for j in range(min(GROUP, n_bricks) // 2):
            at = i * min(GROUP, n_bricks) + 2 * j
            pair = jnp.where(lane < NSUB, own(at), pltpu.roll(own(at + 1), NSUB, 1))
            a = jnp.where(near, first[at, 1:2], first[at + 1, 1:2]).astype(i32)
            lefts.append(jnp.where(spread(a >> 7) == rows((B, LZ)), pair, 0.0))
            lows.append(a & 127)
        for j in range(min(GROUP, n_bricks)):
            a = values[i * min(GROUP, n_bricks) + j, 3:4].astype(i32)
            edge_lefts.append(halves(spread(values[i * min(GROUP, n_bricks) + j, 1:2]), spread(a >> 7)))
            edge_lows.append(a & 127)
        return (
            totals[0] + one_hot_product(lefts, lows),
            totals[1] + one_hot_product(edge_lefts, edge_lows),
        )

    mine, edges = lax.fori_loop(
        0, n_bricks // min(GROUP, n_bricks), one, (jnp.zeros((4 * B, LZ), f32), jnp.zeros((6 * B, LZ), f32))
    )
    total = jnp.concatenate([joined(mine, B), joined(edges, 2 * B)], axis=0)
    for d in range(n_out):
        out[d] = total


def lookup(table, index):
    low, high = index & 127, index >> 7
    result = jnp.zeros((B, LZ), f32)
    for h in range(B):
        got = jnp.take_along_axis(spread(table[h : h + 1]), low, axis=1)
        result = jnp.where(high == h, got, result)
    return result


def pick(row, index):
    return jnp.take_along_axis(spread(row), index, axis=1)


def slab_total(parts, g, n_gx, part, size):
    total = parts[jnp.clip(g, 0, n_gx - 1), part : part + size]
    return jnp.where((g >= 0) & (g < n_gx), total, 0.0)


def guess(parts, g, n_gx):
    total = slab_total(parts, g, n_gx, 0, 2 * B)
    exists = (g >= 0) & (g < n_gx)
    rhs, diag = total[0:B], jnp.where(exists, total[B : 2 * B], 1.0)
    return rhs, diag, coarse_relax * rhs / diag


def expand(coarse, asg, labels, u, tables, first, last):
    near_side = lanes((B, LZ)) < 64

    def table(i, carry):
        b, ty = i // 3, lax.rem(i, 3)
        tables[b, ty] = lookup(coarse[b], asg[b, ty])
        return carry

    lax.fori_loop(0, 9, table, 0, unroll=3)

    def one(p, carry):
        b = p // B
        for ty in range(3):
            r = slice(ty * B, (ty + 1) * B)
            t = tables[b, ty]
            u[p + 1, r, 0:LZ] = pick(t[0:1], labels[p, r, 0:LZ])
            lab = labels[p, r, LZ:]
            u[p + 1, r, LZ:] = jnp.where(near_side, pick(t[1:2], lab), pick(t[2:3], lab))
        return carry

    lax.fori_loop(first, last + 1, one, 0, unroll=8)


def second_sums(n_gx, n_gy, n_col, parts, weights, labels, asg, dvals, paths,
                chunk, both, coarse, tables, ends, sums):
    gx = lax.axis_index("gx")
    row = rows((B, LZ))
    r = slice(B, 2 * B)
    for i in range(3):
        coarse[i] = guess(parts, gx + i - 1, n_gx)[2]
    expand(coarse, asg, labels, both.at[0], tables, 0, NP - 1)

    def after(k):
        @pl.when(k == 0)
        def _():
            first = both.at[1]
            zero = jnp.zeros(FULL, f32)
            first[1] = zero
            first[NP] = zero
            first[:, 0:1, :] = jnp.zeros((NP + 2, 1, 2 * LZ), f32)
            first[:, NP - 1 :, :] = jnp.zeros((NP + 2, 1, 2 * LZ), f32)
            ends[0] = first[B + 1, r, 0:LZ] * -paths[0]
            ends[1] = first[2 * B, r, 0:LZ] * -paths[1]
            for q in range(B):
                plane = first[B + 1 + q, r, 0:LZ]
                ends[2, q : q + 1, :] = plane[0:1] * -paths[2, q : q + 1, :]
                ends[3, q : q + 1, :] = plane[B - 1 : B] * -paths[3, q : q + 1, :]

    sweeps(both, weights, 0, 7, after=after, operator_at=4)
    tiles = [own_tile(both.at[0], weights, B + q) * dvals[B + q] for q in range(B)]
    label_tiles = [labels[B + q, r, 0:LZ] for q in range(B)]
    beyond = [labels[2 * B, r, 0:LZ], labels[B - 1, r, 0:LZ]]
    for at in (2 * B, B - 1):
        edge = labels[B, at : at + 1, 0:LZ]
        edge = spread(edge)
        for q in range(1, B):
            edge = jnp.where(row == q, spread(labels[B + q, at : at + 1, 0:LZ]), edge)
        beyond.append(edge)
    groups = [(0, label_tiles, (tiles,))]
    groups += [((2 + i) * NSUB, [beyond[i]], ([ends[i]],)) for i in range(4)]
    sums[NSUB : 2 * NSUB, :] = jnp.zeros((NSUB, LZ), f32)
    label_sums(groups, sums)
    totals = lane_sums(sums[...])
    right, left = (spread(asg[b, 1, 0:1, :].astype(f32)) for b in (2, 0))
    sides = jnp.where(lanes((B, LZ)) < NSUB, right, pltpu.roll(left, NSUB, 1))
    tile = jnp.where(
        row < 2,
        jnp.where(row == 0, totals[:, 0:LZ], totals[:, LZ : 2 * LZ]),
        jnp.where(row == 2, totals[:, 2 * LZ :], sides),
    )[0:4]
    for d in range(n_gy * n_col):
        chunk[d] = tile


def last_sweeps(n_gx, n_gy, n_col, parts, images, weights, labels, asg,
                pressure, coarse_out, both, coarse, tables):
    gx, gy, col = (lax.axis_index(a) for a in ("gx", "gy", "col"))
    for i in range(3):
        g = gx + i - 1
        rhs, diag, start = guess(parts, g, n_gx)
        image = (
            slab_total(images, g, n_gx, 0, B)
            + slab_total(images, g - 1, n_gx, B, B)
            + slab_total(images, g + 1, n_gx, 2 * B, B)
        )
        second = start + coarse_relax * (rhs - image) / diag
        coarse[i] = jnp.where((g >= 0) & (g < n_gx), second, 0.0)
    share = B * LZ // (n_gy * n_col)
    per_row = LZ // share
    mine = gy * n_col + col
    row = coarse[1, pl.ds(mine // per_row, 1), :]
    turned = pltpu.roll(spread(row), lax.rem(LZ - lax.rem(mine, per_row) * share, LZ), 1)
    coarse_out[...] = turned[0:1, 0:share]
    expand(coarse, asg, labels, both.at[1], tables, 4, 19)
    sweeps(both, weights, 5, 7)
    for q in range(B):
        pressure[q] = own_tile(both.at[0], weights, B + q)


def steps(count, by, wrap):
    return [
        (i, (i + by) % count) for i in range(count) if wrap or 0 <= i + by < count
    ]


def on_device(n_gx, n_gy, n_col, permeability, source, ownership, assignment, layer_flags):
    n_bricks = n_gy * n_col
    sizes = (n_gx, n_gy, n_col)
    vm = pltpu.VMEM
    fields = vm((2, NP + 2, *FULL), f32)
    plane = (B, B, LZ)

    def send(x, axis, by, wrap=False):
        return lax.ppermute(x, axis, steps(lax.axis_size(axis), by, wrap))

    mr, ml, base, flags = call(
        z_messages,
        [pinned(B // 2 + 1, B, LZ)] * 2 + [pinned(3 * B + 1, B, LZ), pinned(3, LZ)],
        5,
        scratch=[
            vm(plane, f32), vm(plane, f32), vm(plane, i32), vm((1, NSUB), i32),
            vm((n_col, LZ), i32), pltpu.SemaphoreType.DMA((5,)),
        ],
        space=pl.ANY,
        limit=WHOLE_VMEM,
    )(permeability, source, ownership, assignment.reshape(1, NSUB), layer_flags.reshape(n_col, LZ))
    mr, ml = send(mr, "col", -1), send(ml, "col", 1)
    mid, to_low, to_high = call(
        stack_up, [sds(STACK, B, LZ)] + [sds(X_MESSAGE, B, LZ)] * 2, 3
    )(base, mr, ml)
    low, high = send(to_high, "gx", 1), send(to_low, "gx", -1)
    up, down = call(y_messages, [sds(MESSAGE, B, LZ)] * 2, 3)(low, mid, high)
    below, above = send(up, "gy", 1, True), send(down, "gy", -1, True)
    middle = call(
        own_rows,
        [sds(NP, B, 2 * LZ), sds(NP, B, 2 * LZ, dtype=i32), sds(2 * B, B, 2 * LZ)],
        3,
        cost=pl.CostEstimate(flops=1000000, bytes_accessed=1000000, transcendentals=0),
    )(low, mid, high)

    weights, labels, chunk, dvals, paths, asg = call(
        functools.partial(first_sums, *sizes),
        [
            sds(6, NP, *FULL), sds(NP, *FULL, dtype=i32), sds(n_bricks, 2, LZ), sds(NP, B, LZ),
            sds(4, B, LZ), sds(3, 3, B, LZ, dtype=i32),
        ],
        9,
        scratch=[
            vm((NP + 2, *FULL), f32), vm((NP + 1, *FULL), f32), fields, vm((2, *FULL), f32),
            vm((2 * NSUB, LZ), f32),
        ],
    )(low, mid, high, below, above, flags, *middle)
    bricks = lax.all_to_all(chunk, ("gy", "col"), 0, 0, tiled=True)
    parts = call(
        functools.partial(first_coarse, n_bricks, n_gx), sds(n_gx, 2 * B, LZ), 1
    )(bricks)
    parts = lax.all_to_all(parts, "gx", 0, 0, tiled=True)
    tables = [vm((3, B, LZ), f32), vm((3, 3, B, LZ), f32)]
    chunk = call(
        functools.partial(second_sums, *sizes),
        sds(n_bricks, 4, LZ),
        6,
        scratch=[fields, *tables, vm((4, B, LZ), f32), vm((6 * NSUB, LZ), f32)],
    )(parts, weights, labels, asg, dvals, paths)
    images = lax.all_to_all(chunk, ("gy", "col"), 0, 0, tiled=True)
    images = call(
        functools.partial(second_coarse, n_gy, n_col, n_gx), sds(n_gx, 3 * B, LZ), 2
    )(images, bricks)
    images = lax.all_to_all(images, "gx", 0, 0, tiled=True)
    return call(
        functools.partial(last_sweeps, *sizes),
        [sds(*plane), sds(1, B * LZ // (n_gy * n_col))],
        5,
        scratch=[fields, *tables],
    )(parts, images, weights, labels, asg)


def solution(mesh):
    placed = (
        P("gx", "gy", "col"),
        P("gx", "gy", "col"),
        P("gx", "gy", "col"),
        P("gx", "gy", "col", None),
        P(),
    )
    sizes = mesh.shape
    return jax.shard_map(
        functools.partial(on_device, sizes["gx"], sizes["gy"], sizes["col"]),
        mesh=mesh,
        in_specs=placed,
        out_specs=(P("gx", "gy", "col"), P("gx", ("gy", "col"))),
        check_vma=False,
    )
```

```python
import functools

import jax
import jax.numpy as jnp
from jax import lax
from jax.experimental import pallas as pl
from jax.experimental.pallas import tpu as pltpu
from jax.sharding import PartitionSpec as P

f32 = jnp.float32
i32 = jnp.int32
bf16 = jnp.bfloat16
NSUB = 64
B = 8
LZ = 128
NP = 3 * B
W = 9
FULL = (NP, 2 * LZ)
CHUNK = 12
fine_relax = 0.6666667
coarse_relax = 0.7
VMEM_LIMIT = 48 * 1024 * 1024
WHOLE_VMEM = 63 * 1024 * 1024

PERM, OWN, HZ, ASG, SRC = 0, 8, 16, 20, 21
STACK = 29
X_MESSAGE = 25

FOLDS = [(p, None, 0) for p in range(7, 17)]
FOLDS += [(6, 0, 1), (5, 1, 2), (4, 2, 3), (17, 23, 1), (18, 22, 2), (19, 21, 3), (3, 20, 4)]
FOLD_OF = {}
for _at, (_main, _other, _rows) in enumerate(FOLDS):
    FOLD_OF[_main] = (_at, 0)
    if _other is not None:
        FOLD_OF[_other] = (_at, _rows)
N_FOLD = len(FOLDS)
M_PERM, M_OWN, M_HZ, M_ASG, M_SRC = 0, N_FOLD, 2 * N_FOLD, 2 * N_FOLD + 12, 2 * N_FOLD + 13
SRC_FOLDS = [(8 + q, ((12 + q, 4, 4),)) for q in range(4)]
SRC_FOLDS += [(7, ((6, 2, 2), (5, 1, 3))), (16, ((17, 2, 2), (18, 1, 3)))]
SRC_OF = {}
for _at, (_main, _others) in enumerate(SRC_FOLDS):
    SRC_OF[_main] = (_at, 0)
    for _other, _rows, _top in _others:
        SRC_OF[_other] = (_at, _top)
MESSAGE = M_SRC + len(SRC_FOLDS)


def lanes(shape):
    return lax.broadcasted_iota(i32, shape, len(shape) - 1)


def rows(shape):
    return lax.broadcasted_iota(i32, shape, len(shape) - 2)


def sds(*shape, dtype=f32):
    return jax.ShapeDtypeStruct(shape, dtype)


def pinned(*shape):
    return pltpu.VMEM(shape, f32)


def call(kernel, outs, n_in, scratch=(), space=pltpu.VMEM, limit=VMEM_LIMIT, cost=None):
    single = not isinstance(outs, (list, tuple))
    vm = pl.BlockSpec(memory_space=pltpu.VMEM)
    return pl.pallas_call(
        kernel,
        out_shape=outs,
        in_specs=[pl.BlockSpec(memory_space=space)] * n_in,
        out_specs=vm if single else [vm] * len(outs),
        scratch_shapes=list(scratch),
        compiler_params=pltpu.CompilerParams(vmem_limit_bytes=limit),
        cost_estimate=cost,
    )


def spread(row):
    return jnp.broadcast_to(row, (B, LZ))


def asg_tile(asg):
    tile = jnp.concatenate([asg[...].astype(f32), jnp.zeros((1, LZ - NSUB), f32)], axis=1)
    return jnp.where(rows((B, LZ)) == 0, spread(tile), 0.0)


def z_messages(perm_in, src_in, own_in, asg_in, flags_in, mr, ml, base, flags_out,
               perm, src, own, asg, flags, sem):
    copies = [
        pltpu.make_async_copy(a, b, sem.at[i])
        for i, (a, b) in enumerate(
            ((perm_in, perm), (src_in, src), (own_in, own), (asg_in, asg), (flags_in, flags))
        )
    ]
    for copy in copies:
        copy.start()
    for copy in copies:
        copy.wait()
    lane = lanes((B, LZ))

    def first_cells(q):
        k, s, o = perm[q], src[q], own[q].astype(f32)
        return jnp.where(
            lane < 9, k, jnp.where(lane < 18, pltpu.roll(o, 9, 1), pltpu.roll(s, 18, 1))
        )

    def last_cells(q):
        k, s, o = perm[q], src[q], own[q].astype(f32)
        return jnp.where(
            lane >= 55,
            pltpu.roll(k, 64, 1),
            jnp.where(lane >= 46, pltpu.roll(o, 55, 1), pltpu.roll(s, 46, 1)),
        )

    for out, cells in ((mr, first_cells), (ml, last_cells)):
        for q in range(B // 2):
            out[q] = jnp.where(lane < 64, cells(q), pltpu.roll(cells(q + B // 2), 64, 1))
        out[B // 2] = asg_tile(asg)
    for q in range(B):
        base[q], base[B + q], base[2 * B + q] = perm[q], own[q].astype(f32), src[q]
    base[3 * B] = asg_tile(asg)
    col, n_col = lax.axis_index("col"), flags.shape[0]
    for i, at in enumerate((col - 1, col, col + 1)):
        at = jnp.clip(at, 0, n_col - 1)
        flags_out[pl.ds(i, 1), :] = flags[pl.ds(at, 1), :].astype(f32)


def source_at(b, q):
    return SRC + (q - 4 if b == 0 else q)


def stack_up(base, mr, ml, stack, to_low, to_high):
    lane = lanes((B, LZ))
    row = rows((B, LZ))
    for q in range(B):
        stack[PERM + q] = base[q]
        stack[OWN + q] = base[B + q]
        stack[SRC + q] = base[2 * B + q]
    for q in range(B // 2):
        stack[HZ + q] = jnp.where((lane & 63) < 32, mr[q], ml[q])
    at = B // 2
    stack[ASG] = jnp.where(
        row == 1, spread(mr[at, 0:1, :]), jnp.where(row == 2, spread(ml[at, 0:1, :]), base[3 * B])
    )
    for out, first in ((to_low, 0), (to_high, 4)):
        out[0:SRC] = stack[0:SRC]
        for q in range(4):
            out[SRC + q] = base[2 * B + first + q]


def y_messages(low, mid, high, up, down):
    stacks = (low, mid, high)
    row = rows((B, LZ))
    lane = lanes((B, LZ))

    def fold(main, other, n, top, upward):
        if upward:
            return jnp.where((row >= top - n) & (row < top), pltpu.roll(other, top, 0), main)
        return jnp.where(
            (row >= B - top) & (row < B - top + n), pltpu.roll(other, B - top, 0), main
        )

    for out, upward in ((up, True), (down, False)):
        for field, first in ((PERM, M_PERM), (OWN, M_OWN)):
            for at, (main, other, n) in enumerate(FOLDS):
                tile = stacks[main // B][field + main % B]
                if other is not None:
                    tile = fold(tile, stacks[other // B][field + other % B], n, n, upward)
                out[first + at] = tile
        for b in range(3):
            for q in range(B // 2):
                out[M_HZ + 4 * b + q] = stacks[b][HZ + q]
        for at, (main, others) in enumerate(SRC_FOLDS):
            tile = stacks[main // B][source_at(main // B, main % B)]
            for other, n, top in others:
                tile = fold(tile, stacks[other // B][source_at(other // B, other % B)], n, top, upward)
            out[M_SRC + at] = tile
        sides = jnp.where(lane < NSUB, low[ASG], pltpu.roll(high[ASG], NSUB, 1))
        out[M_ASG] = jnp.where(row < 3, sides, pltpu.roll(mid[ASG], 3, 0))


def line_asg(stacks, below, above, ty, b):
    if ty == 1:
        return stacks[b][ASG]
    tile = (below if ty == 0 else above)[M_ASG]
    return (tile, pltpu.roll(tile, 5, 0), pltpu.roll(tile, NSUB, 1))[b]


def around(u_ref, w_ref, p):
    u = u_ref[p + 1]
    return u, (
        (w_ref[0, p] * u_ref[p + 2] + w_ref[1, p] * u_ref[p])
        + (w_ref[2, p] * pltpu.roll(u, NP - 1, 0) + w_ref[3, p] * pltpu.roll(u, 1, 0))
        + (w_ref[4, p] * pltpu.roll(u, 2 * LZ - 1, 1) + w_ref[5, p] * pltpu.roll(u, 1, 1))
    )


def sweeps(both, w_ref, first, last, after=None, operator_at=-1, size=CHUNK):
    def one_sweep(k, carry):
        now = lax.rem(k, 2)
        src, dst = both.at[now], both.at[1 - now]
        count = NP - 2 * k
        keep = jnp.where(k == operator_at, 1.0, 1.0 - fine_relax)
        give = jnp.where(k == operator_at, -1.0 / fine_relax, 1.0)

        def chunk(i, carry):
            start = jnp.minimum(k + size * i, k + count - size)
            moved = []
            for j in range(size):
                u, near = around(src, w_ref, start + j)
                moved.append(keep * u + give * near)
            for j in range(size):
                dst[start + j + 1] = moved[j]
            return carry

        lax.fori_loop(0, (count + size - 1) // size, chunk, 0)
        if after is not None:
            after(k)
        return carry

    lax.fori_loop(first, last + 1, one_sweep, 0)


def own_tile(u_ref, w_ref, p):
    r, z = slice(B, 2 * B), slice(0, LZ)
    u, beyond = u_ref[p + 1, r, z], u_ref[p + 1, r, LZ:]
    lane = lanes((B, LZ))
    right = jnp.where(lane == LZ - 1, pltpu.roll(beyond, LZ - 1, 1), pltpu.roll(u, LZ - 1, 1))
    left = jnp.where(lane == 0, pltpu.roll(beyond, 1, 1), pltpu.roll(u, 1, 1))
    w = [w_ref[i, p, r, z] for i in range(6)]
    near = (
        (w[0] * u_ref[p + 2, r, z] + w[1] * u_ref[p, r, z])
        + (w[2] * u_ref[p + 1, B + 1 : 2 * B + 1, z] + w[3] * u_ref[p + 1, B - 1 : 2 * B - 1, z])
        + (w[4] * right + w[5] * left)
    )
    return (1.0 - fine_relax) * u + near


def label_sums(groups, sums):
    def one(s, carry):
        for first, labels, fields in groups:
            hits = [tile == s for tile in labels]
            for i, tiles in enumerate(fields):
                parts = [jnp.where(hit, tile, 0.0) for hit, tile in zip(hits, tiles)]
                while len(parts) > 1:
                    parts = [a + b for a, b in zip(parts[::2], parts[1::2])]
                sums[pl.ds(first + i * NSUB + s, 1), :] = jnp.sum(parts[0], axis=0, keepdims=True)
        return carry

    lax.fori_loop(0, NSUB, one, 0, unroll=16)


def three_parts(x):
    high = x.astype(bf16).astype(f32)
    rest = x - high
    middle = rest.astype(bf16).astype(f32)
    return high, middle, rest - middle


def lane_sums(sums):
    parts = jnp.concatenate(three_parts(sums), axis=1).astype(bf16)
    total = lax.dot_general(
        jnp.ones((2 * B, 3 * LZ), bf16), parts,
        (((1,), (1,)), ((), ())), preferred_element_type=f32,
    )
    return total[0:B]


def harmonic(a, b):
    return 2.0 * a * b / (a + b)


def row_product(tile):
    for by in (4, 2, 1):
        tile = tile * pltpu.roll(tile, by, 0)
    return tile


def positive(t):
    return jnp.where(t > 0.0, t, 1.0)


def near_and_far(tile, q):
    turned = pltpu.roll(tile, 64, 1)
    return jnp.where(q < 4, tile, turned), jnp.where(q < 4, turned, tile)


def halo_values(near, far):
    lane = lanes((B, LZ))
    near_side = lane < 64
    halo = (lane < W) | (lane >= LZ - W)
    source_halo = (lane < 4) | (lane >= LZ - 4)
    k = positive(jnp.where(halo, jnp.where(near_side, near, far), 1.0))
    own = jnp.where(near_side, pltpu.roll(near, LZ - 9, 1), pltpu.roll(near, 73, 1))
    src = jnp.where(near_side, pltpu.roll(near, LZ - 18, 1), pltpu.roll(near, 82, 1))
    return k, jnp.where(halo, own, 0.0).astype(i32), jnp.where(source_halo, src, 0.0)


def own_rows(low, mid, high, kmid, lmid, smid):
    for p in range(NP):
        stack, q = (low, mid, high)[p // B], p % B
        k, label, src = halo_values(*near_and_far(stack[HZ + q % 4], q))
        kmid[p, :, 0:LZ] = positive(stack[PERM + q])
        kmid[p, :, LZ:] = k
        lmid[p, :, 0:LZ] = stack[OWN + q].astype(i32)
        lmid[p, :, LZ:] = label
        if 4 <= p < 20:
            smid[p - 4, :, 0:LZ] = stack[source_at(p // B, q)]
            smid[p - 4, :, LZ:] = src


def first_sums(n_gx, n_gy, n_col, low, mid, high, below, above, flags, kmid, lmid, smid,
               weights, labels, chunk, dvals, paths, asg, kext, fx, both, masks, sums):
    gx, gy, col = (lax.axis_index(a) for a in ("gx", "gy", "col"))
    mids = (low, mid, high)
    lane = lanes((B, LZ))
    row = rows((B, LZ))
    def unfolded(ty, first, place):
        at, n = place
        tile = (below if ty == 0 else above)[first + at]
        return pltpu.roll(tile, (B - n if ty == 0 else n) % B, 0) if n else tile

    def beyond(ty, p):
        b, q = p // B, lax.rem(p, B)
        tile = (below if ty == 0 else above)[M_HZ + 4 * b + lax.rem(q, 4)]
        return halo_values(*near_and_far(tile, q))

    def fill(p, carry):
        kext[p + 1, B : 2 * B, :] = kmid[p]
        labels[p, B : 2 * B, :] = lmid[p]
        for ty in (0, 2):
            r = slice(ty * B, (ty + 1) * B)
            kext[p + 1, r, LZ:], labels[p, r, LZ:], _ = beyond(ty, p)
        return carry

    lax.fori_loop(0, NP, fill, 0, unroll=12)
    for p in range(NP):
        for ty in (0, 2):
            r = slice(ty * B, (ty + 1) * B)
            kext[p + 1, r, 0:LZ] = positive(unfolded(ty, M_PERM, FOLD_OF[p]))
            labels[p, r, 0:LZ] = unfolded(ty, M_OWN, FOLD_OF[p]).astype(i32)
    for b in range(3):
        for ty in range(3):
            asg[b, ty] = line_asg(mids, below, above, ty, b).astype(i32)
    kext[0] = jnp.ones(FULL, f32)
    kext[NP + 1] = jnp.ones(FULL, f32)

    flag_row = jnp.concatenate(
        [flags[1:2, :], jnp.where(lane[0:1] < 64, flags[2:3, :], flags[0:1, :])], axis=1
    )
    row_all, lane_all = rows(FULL), lanes(FULL)
    wrap_row = jnp.where(gy == 0, B - 1, jnp.where(gy == n_gy - 1, 2 * B - 1, -1))
    masks[0] = jnp.where(row_all == wrap_row, jnp.broadcast_to(flag_row, FULL), 1.0)
    closed = ((lane_all == LZ - 1) & (col == n_col - 1)) | ((lane_all == 2 * LZ - 1) & (col == 0))
    masks[1] = jnp.where(closed, 0.0, 1.0)

    def terms(p, carry):
        b = p // B
        out = ((b == 0) & (gx == 0)) | ((b == 2) & (gx == n_gx - 1))
        k = kext[p + 1]
        fy_up = harmonic(k, pltpu.roll(k, NP - 1, 0)) * masks[0]
        fy_down = pltpu.roll(fy_up, 1, 0)
        fz_right = harmonic(k, pltpu.roll(k, 2 * LZ - 1, 1)) * masks[1]
        fz_left = pltpu.roll(fz_right, 1, 1)
        k_next = kext[p + 2]
        fx_up = jnp.where((p == B - 1) & (gx == 0), k_next, harmonic(k, k_next))
        fx_up = jnp.where((p == 2 * B - 1) & (gx == n_gx - 1), k, fx_up)
        fx_down = carry
        diag = fx_up + fx_down + fy_up + fy_down + fz_right + fz_left
        scale = jnp.where(out, 0.0, fine_relax) / diag
        for i, face in enumerate((fx_up, fx_down, fy_up, fy_down, fz_right, fz_left)):
            weights[i, p] = face * scale
        both[0, p + 1] = scale
        dvals[p] = diag[B : 2 * B, 0:LZ]
        fx[p + 1] = fx_up
        return fx_up

    lax.fori_loop(0, NP, terms, harmonic(kext[0], kext[1]), unroll=8)


    def start(i, carry):
        p = i + B // 2
        over = both[0, p + 1] * (1.0 / fine_relax)
        both[1, p + 1, B : 2 * B, :] = smid[i] * over[B : 2 * B]
        for ty in (0, 2):
            r = slice(ty * B, (ty + 1) * B)
            both[1, p + 1, r, LZ:] = beyond(ty, p)[2] * over[r, LZ:]
        return carry

    lax.fori_loop(0, 2 * B, start, 0, unroll=16)
    for p in range(B // 2, NP - B // 2):
        for ty in (0, 2):
            r = slice(ty * B, (ty + 1) * B)
            if p in SRC_OF:
                over = both[0, p + 1, r, 0:LZ] * (1.0 / fine_relax)
                both[1, p + 1, r, 0:LZ] = unfolded(ty, M_SRC, SRC_OF[p]) * over
            else:
                both[1, p + 1, r, 0:LZ] = jnp.zeros((B, LZ), f32)

    r = slice(B, 2 * B)
    for q in range(B):
        p = B + q
        up, down = weights[2, p, r, 0:LZ], weights[3, p, r, 0:LZ]
        rise = row_product(jnp.where(row == 0, 1.0, down)) * up
        fall = row_product(jnp.where(row == B - 1, 1.0, up)) * down
        per = dvals[p] * (1.0 / fine_relax)
        paths[2, q : q + 1, :] = (rise * per)[B - 1 : B]
        paths[3, q : q + 1, :] = (fall * per)[0:1]
    rise, fall = fx[2 * B, B : 2 * B, 0:LZ], fx[B, B : 2 * B, 0:LZ]
    for p in range(B + 1, 2 * B):
        rise = rise * weights[1, p, B : 2 * B, 0:LZ]
        fall = fall * weights[0, p - 1, B : 2 * B, 0:LZ]
    paths[0] = rise
    paths[1] = fall

    sweeps(both, weights, 5, 7, size=NP - 10)
    tiles = [own_tile(both.at[0], weights, B + q) * dvals[B + q] for q in range(B)]
    diag_tiles = [dvals[B + q] for q in range(B)]
    label_tiles = [labels[B + q, B : 2 * B, 0:LZ] for q in range(B)]
    label_sums([(0, label_tiles, (tiles, diag_tiles))], sums)
    totals = lane_sums(sums[...])

    own = spread(mid[ASG, 0:1, :])
    own = jnp.where(lane < NSUB, own, pltpu.roll(own, NSUB, 1))
    tile = jnp.where(row == 0, totals, own)[0:2]
    for d in range(n_gy * n_col):
        chunk[d] = tile


def one_hot_product(lefts, lows):
    left = jnp.concatenate(lefts, axis=1)
    wide = rows((LZ, LZ))
    right = jnp.concatenate(
        [
            jnp.where(jnp.broadcast_to(low, (LZ, LZ)) == wide, 1.0, 0.0).astype(bf16)
            for low in lows
        ],
        axis=1,
    )
    parts = three_parts(left)
    if left.shape[0] % (2 * B):
        parts += (jnp.zeros_like(left),)
    return lax.dot_general(
        jnp.concatenate(parts, axis=0).astype(bf16), right, (((1,), (1,)), ((), ())),
        preferred_element_type=f32,
    )


def joined(total, n):
    return (total[2 * n : 3 * n] + total[n : 2 * n]) + total[:n]


def halves(value, high):
    lane = lanes((B, LZ))
    scaled = jnp.where(high == rows((B, LZ)), value, 0.0)
    return jnp.concatenate(
        [jnp.where(lane < NSUB, scaled, 0.0), jnp.where(lane < NSUB, 0.0, scaled)], axis=0
    )


GROUP = 64


def first_coarse(n_bricks, n_out, values, out):
    def one(i, total):
        lefts, lows = [], []
        for j in range(min(GROUP, n_bricks)):
            value = values[i * min(GROUP, n_bricks) + j]
            a = value[1:2].astype(i32)
            lefts.append(halves(spread(value[0:1]), spread(a >> 7)))
            lows.append(a & 127)
        return total + one_hot_product(lefts, lows)

    total = lax.fori_loop(0, n_bricks // min(GROUP, n_bricks), one, jnp.zeros((6 * B, LZ), f32))
    total = joined(total, 2 * B)
    for d in range(n_out):
        out[d] = total


def second_coarse(n_gy, n_col, n_out, values, first, out):
    n_bricks = n_gy * n_col
    lane = lanes((B, LZ))
    near = lanes((1, LZ)) < NSUB

    def own(j):
        before = lax.rem(j + n_bricks - n_col, n_bricks)
        after = lax.rem(j + n_col, n_bricks)
        mine = spread(values[j, 0:1] + values[before, 2:3])
        return mine + pltpu.roll(spread(values[after, 2:3]), NSUB, 1)

    def one(i, totals):
        lefts, lows, edge_lefts, edge_lows = [], [], [], []
        for j in range(min(GROUP, n_bricks) // 2):
            at = i * min(GROUP, n_bricks) + 2 * j
            pair = jnp.where(lane < NSUB, own(at), pltpu.roll(own(at + 1), NSUB, 1))
            a = jnp.where(near, first[at, 1:2], first[at + 1, 1:2]).astype(i32)
            lefts.append(jnp.where(spread(a >> 7) == rows((B, LZ)), pair, 0.0))
            lows.append(a & 127)
        for j in range(min(GROUP, n_bricks)):
            a = values[i * min(GROUP, n_bricks) + j, 3:4].astype(i32)
            edge_lefts.append(halves(spread(values[i * min(GROUP, n_bricks) + j, 1:2]), spread(a >> 7)))
            edge_lows.append(a & 127)
        return (
            totals[0] + one_hot_product(lefts, lows),
            totals[1] + one_hot_product(edge_lefts, edge_lows),
        )

    mine, edges = lax.fori_loop(
        0, n_bricks // min(GROUP, n_bricks), one, (jnp.zeros((4 * B, LZ), f32), jnp.zeros((6 * B, LZ), f32))
    )
    total = jnp.concatenate([joined(mine, B), joined(edges, 2 * B)], axis=0)
    for d in range(n_out):
        out[d] = total


def lookup(table, index):
    low, high = index & 127, index >> 7
    result = jnp.zeros((B, LZ), f32)
    for h in range(B):
        got = jnp.take_along_axis(spread(table[h : h + 1]), low, axis=1)
        result = jnp.where(high == h, got, result)
    return result


def pick(row, index):
    return jnp.take_along_axis(spread(row), index, axis=1)


def slab_total(parts, g, n_gx, part, size):
    total = parts[jnp.clip(g, 0, n_gx - 1), part : part + size]
    return jnp.where((g >= 0) & (g < n_gx), total, 0.0)


def guess(parts, g, n_gx):
    total = slab_total(parts, g, n_gx, 0, 2 * B)
    exists = (g >= 0) & (g < n_gx)
    rhs, diag = total[0:B], jnp.where(exists, total[B : 2 * B], 1.0)
    return rhs, diag, coarse_relax * rhs / diag


def expand(coarse, asg, labels, u, tables, first, last):
    near_side = lanes((B, LZ)) < 64

    def table(i, carry):
        b, ty = i // 3, lax.rem(i, 3)
        tables[b, ty] = lookup(coarse[b], asg[b, ty])
        return carry

    lax.fori_loop(0, 9, table, 0, unroll=3)

    def one(p, carry):
        b = p // B
        for ty in range(3):
            r = slice(ty * B, (ty + 1) * B)
            t = tables[b, ty]
            u[p + 1, r, 0:LZ] = pick(t[0:1], labels[p, r, 0:LZ])
            lab = labels[p, r, LZ:]
            u[p + 1, r, LZ:] = jnp.where(near_side, pick(t[1:2], lab), pick(t[2:3], lab))
        return carry

    lax.fori_loop(first, last + 1, one, 0, unroll=8)


def second_sums(n_gx, n_gy, n_col, parts, weights, labels, asg, dvals, paths,
                chunk, both, coarse, tables, ends, sums):
    gx = lax.axis_index("gx")
    row = rows((B, LZ))
    r = slice(B, 2 * B)
    for i in range(3):
        coarse[i] = guess(parts, gx + i - 1, n_gx)[2]
    expand(coarse, asg, labels, both.at[0], tables, 0, NP - 1)

    def after(k):
        @pl.when(k == 0)
        def _():
            first = both.at[1]
            zero = jnp.zeros(FULL, f32)
            first[1] = zero
            first[NP] = zero
            first[:, 0:1, :] = jnp.zeros((NP + 2, 1, 2 * LZ), f32)
            first[:, NP - 1 :, :] = jnp.zeros((NP + 2, 1, 2 * LZ), f32)
            ends[0] = first[B + 1, r, 0:LZ] * -paths[0]
            ends[1] = first[2 * B, r, 0:LZ] * -paths[1]
            for q in range(B):
                plane = first[B + 1 + q, r, 0:LZ]
                ends[2, q : q + 1, :] = plane[0:1] * -paths[2, q : q + 1, :]
                ends[3, q : q + 1, :] = plane[B - 1 : B] * -paths[3, q : q + 1, :]

    sweeps(both, weights, 0, 7, after=after, operator_at=4)
    tiles = [own_tile(both.at[0], weights, B + q) * dvals[B + q] for q in range(B)]
    label_tiles = [labels[B + q, r, 0:LZ] for q in range(B)]
    beyond = [labels[2 * B, r, 0:LZ], labels[B - 1, r, 0:LZ]]
    for at in (2 * B, B - 1):
        edge = labels[B, at : at + 1, 0:LZ]
        edge = spread(edge)
        for q in range(1, B):
            edge = jnp.where(row == q, spread(labels[B + q, at : at + 1, 0:LZ]), edge)
        beyond.append(edge)
    groups = [(0, label_tiles, (tiles,))]
    groups += [((2 + i) * NSUB, [beyond[i]], ([ends[i]],)) for i in range(4)]
    sums[NSUB : 2 * NSUB, :] = jnp.zeros((NSUB, LZ), f32)
    label_sums(groups, sums)
    totals = lane_sums(sums[...])
    right, left = (spread(asg[b, 1, 0:1, :].astype(f32)) for b in (2, 0))
    sides = jnp.where(lanes((B, LZ)) < NSUB, right, pltpu.roll(left, NSUB, 1))
    tile = jnp.where(
        row < 2,
        jnp.where(row == 0, totals[:, 0:LZ], totals[:, LZ : 2 * LZ]),
        jnp.where(row == 2, totals[:, 2 * LZ :], sides),
    )[0:4]
    for d in range(n_gy * n_col):
        chunk[d] = tile


def last_sweeps(n_gx, n_gy, n_col, parts, images, weights, labels, asg,
                pressure, coarse_out, both, coarse, tables):
    gx, gy, col = (lax.axis_index(a) for a in ("gx", "gy", "col"))
    for i in range(3):
        g = gx + i - 1
        rhs, diag, start = guess(parts, g, n_gx)
        image = (
            slab_total(images, g, n_gx, 0, B)
            + slab_total(images, g - 1, n_gx, B, B)
            + slab_total(images, g + 1, n_gx, 2 * B, B)
        )
        second = start + coarse_relax * (rhs - image) / diag
        coarse[i] = jnp.where((g >= 0) & (g < n_gx), second, 0.0)
    share = B * LZ // (n_gy * n_col)
    per_row = LZ // share
    mine = gy * n_col + col
    row = coarse[1, pl.ds(mine // per_row, 1), :]
    turned = pltpu.roll(spread(row), lax.rem(LZ - lax.rem(mine, per_row) * share, LZ), 1)
    coarse_out[...] = turned[0:1, 0:share]
    expand(coarse, asg, labels, both.at[1], tables, 4, 19)
    sweeps(both, weights, 5, 7, size=NP - 10)
    for q in range(B):
        pressure[q] = own_tile(both.at[0], weights, B + q)


def steps(count, by, wrap):
    return [
        (i, (i + by) % count) for i in range(count) if wrap or 0 <= i + by < count
    ]


def on_device(n_gx, n_gy, n_col, permeability, source, ownership, assignment, layer_flags):
    n_bricks = n_gy * n_col
    sizes = (n_gx, n_gy, n_col)
    vm = pltpu.VMEM
    fields = vm((2, NP + 2, *FULL), f32)
    plane = (B, B, LZ)

    def send(x, axis, by, wrap=False):
        return lax.ppermute(x, axis, steps(lax.axis_size(axis), by, wrap))

    mr, ml, base, flags = call(
        z_messages,
        [pinned(B // 2 + 1, B, LZ)] * 2 + [pinned(3 * B + 1, B, LZ), pinned(3, LZ)],
        5,
        scratch=[
            vm(plane, f32), vm(plane, f32), vm(plane, i32), vm((1, NSUB), i32),
            vm((n_col, LZ), i32), pltpu.SemaphoreType.DMA((5,)),
        ],
        space=pl.ANY,
        limit=WHOLE_VMEM,
    )(permeability, source, ownership, assignment.reshape(1, NSUB), layer_flags.reshape(n_col, LZ))
    mr, ml = send(mr, "col", -1), send(ml, "col", 1)
    mid, to_low, to_high = call(
        stack_up, [sds(STACK, B, LZ)] + [sds(X_MESSAGE, B, LZ)] * 2, 3
    )(base, mr, ml)
    low, high = send(to_high, "gx", 1), send(to_low, "gx", -1)
    up, down = call(y_messages, [sds(MESSAGE, B, LZ)] * 2, 3)(low, mid, high)
    below, above = send(up, "gy", 1, True), send(down, "gy", -1, True)
    middle = call(
        own_rows,
        [sds(NP, B, 2 * LZ), sds(NP, B, 2 * LZ, dtype=i32), sds(2 * B, B, 2 * LZ)],
        3,
        cost=pl.CostEstimate(flops=1000000, bytes_accessed=1000000, transcendentals=0),
    )(low, mid, high)

    weights, labels, chunk, dvals, paths, asg = call(
        functools.partial(first_sums, *sizes),
        [
            sds(6, NP, *FULL), sds(NP, *FULL, dtype=i32), sds(n_bricks, 2, LZ), sds(NP, B, LZ),
            sds(4, B, LZ), sds(3, 3, B, LZ, dtype=i32),
        ],
        9,
        scratch=[
            vm((NP + 2, *FULL), f32), vm((NP + 1, *FULL), f32), fields, vm((2, *FULL), f32),
            vm((2 * NSUB, LZ), f32),
        ],
    )(low, mid, high, below, above, flags, *middle)
    bricks = lax.all_to_all(chunk, ("gy", "col"), 0, 0, tiled=True)
    parts = call(
        functools.partial(first_coarse, n_bricks, n_gx), sds(n_gx, 2 * B, LZ), 1
    )(bricks)
    parts = lax.all_to_all(parts, "gx", 0, 0, tiled=True)
    tables = [vm((3, B, LZ), f32), vm((3, 3, B, LZ), f32)]
    chunk = call(
        functools.partial(second_sums, *sizes),
        sds(n_bricks, 4, LZ),
        6,
        scratch=[fields, *tables, vm((4, B, LZ), f32), vm((6 * NSUB, LZ), f32)],
    )(parts, weights, labels, asg, dvals, paths)
    images = lax.all_to_all(chunk, ("gy", "col"), 0, 0, tiled=True)
    images = call(
        functools.partial(second_coarse, n_gy, n_col, n_gx), sds(n_gx, 3 * B, LZ), 2
    )(images, bricks)
    images = lax.all_to_all(images, "gx", 0, 0, tiled=True)
    return call(
        functools.partial(last_sweeps, *sizes),
        [sds(*plane), sds(1, B * LZ // (n_gy * n_col))],
        5,
        scratch=[fields, *tables],
    )(parts, images, weights, labels, asg)


def solution(mesh):
    placed = (
        P("gx", "gy", "col"),
        P("gx", "gy", "col"),
        P("gx", "gy", "col"),
        P("gx", "gy", "col", None),
        P(),
    )
    sizes = mesh.shape
    return jax.shard_map(
        functools.partial(on_device, sizes["gx"], sizes["gy"], sizes["col"]),
        mesh=mesh,
        in_specs=placed,
        out_specs=(P("gx", "gy", "col"), P("gx", ("gy", "col"))),
        check_vma=False,
    )
```

```python
import functools

import jax
import jax.numpy as jnp
from jax import lax
from jax.experimental import pallas as pl
from jax.experimental.pallas import tpu as pltpu
from jax.sharding import PartitionSpec as P

f32 = jnp.float32
i32 = jnp.int32
bf16 = jnp.bfloat16
NSUB = 64
B = 8
LZ = 128
NP = 3 * B
W = 9
FULL = (NP, 2 * LZ)
CHUNK = 12
fine_relax = 0.6666667
coarse_relax = 0.7
VMEM_LIMIT = 48 * 1024 * 1024
WHOLE_VMEM = 63 * 1024 * 1024

PERM, OWN, HZ, ASG, SRC = 0, 8, 16, 20, 21
STACK = 29
X_MESSAGE = 25

FOLDS = [(p, None, 0) for p in range(7, 17)]
FOLDS += [(6, 0, 1), (5, 1, 2), (4, 2, 3), (17, 23, 1), (18, 22, 2), (19, 21, 3), (3, 20, 4)]
FOLD_OF = {}
for _at, (_main, _other, _rows) in enumerate(FOLDS):
    FOLD_OF[_main] = (_at, 0)
    if _other is not None:
        FOLD_OF[_other] = (_at, _rows)
N_FOLD = len(FOLDS)
M_PERM, M_OWN, M_HZ, M_ASG, M_SRC = 0, N_FOLD, 2 * N_FOLD, 2 * N_FOLD + 12, 2 * N_FOLD + 13
SRC_FOLDS = [(8 + q, ((12 + q, 4, 4),)) for q in range(4)]
SRC_FOLDS += [(7, ((6, 2, 2), (5, 1, 3))), (16, ((17, 2, 2), (18, 1, 3)))]
SRC_OF = {}
for _at, (_main, _others) in enumerate(SRC_FOLDS):
    SRC_OF[_main] = (_at, 0)
    for _other, _rows, _top in _others:
        SRC_OF[_other] = (_at, _top)
MESSAGE = M_SRC + len(SRC_FOLDS)


def lanes(shape):
    return lax.broadcasted_iota(i32, shape, len(shape) - 1)


def rows(shape):
    return lax.broadcasted_iota(i32, shape, len(shape) - 2)


def sds(*shape, dtype=f32):
    return jax.ShapeDtypeStruct(shape, dtype)


def pinned(*shape):
    return pltpu.VMEM(shape, f32)


def call(kernel, outs, n_in, scratch=(), space=pltpu.VMEM, limit=VMEM_LIMIT, cost=None):
    single = not isinstance(outs, (list, tuple))
    vm = pl.BlockSpec(memory_space=pltpu.VMEM)
    return pl.pallas_call(
        kernel,
        out_shape=outs,
        in_specs=[pl.BlockSpec(memory_space=space)] * n_in,
        out_specs=vm if single else [vm] * len(outs),
        scratch_shapes=list(scratch),
        compiler_params=pltpu.CompilerParams(vmem_limit_bytes=limit),
        cost_estimate=cost,
    )


def spread(row):
    return jnp.broadcast_to(row, (B, LZ))


def asg_tile(asg):
    tile = jnp.concatenate([asg[...].astype(f32), jnp.zeros((1, LZ - NSUB), f32)], axis=1)
    return jnp.where(rows((B, LZ)) == 0, spread(tile), 0.0)


def z_messages(perm_in, src_in, own_in, asg_in, flags_in, mr, ml, base, flags_out,
               perm, src, own, asg, flags, sem):
    copies = [
        pltpu.make_async_copy(a, b, sem.at[i])
        for i, (a, b) in enumerate(
            ((perm_in, perm), (src_in, src), (own_in, own), (asg_in, asg), (flags_in, flags))
        )
    ]
    for copy in copies:
        copy.start()
    for copy in copies:
        copy.wait()
    lane = lanes((B, LZ))

    def first_cells(q):
        k, s, o = perm[q], src[q], own[q].astype(f32)
        return jnp.where(
            lane < 9, k, jnp.where(lane < 18, pltpu.roll(o, 9, 1), pltpu.roll(s, 18, 1))
        )

    def last_cells(q):
        k, s, o = perm[q], src[q], own[q].astype(f32)
        return jnp.where(
            lane >= 55,
            pltpu.roll(k, 64, 1),
            jnp.where(lane >= 46, pltpu.roll(o, 55, 1), pltpu.roll(s, 46, 1)),
        )

    for out, cells in ((mr, first_cells), (ml, last_cells)):
        for q in range(B // 2):
            out[q] = jnp.where(lane < 64, cells(q), pltpu.roll(cells(q + B // 2), 64, 1))
        out[B // 2] = asg_tile(asg)
    for q in range(B):
        base[q], base[B + q], base[2 * B + q] = perm[q], own[q].astype(f32), src[q]
    base[3 * B] = asg_tile(asg)
    col, n_col = lax.axis_index("col"), flags.shape[0]
    for i, at in enumerate((col - 1, col, col + 1)):
        at = jnp.clip(at, 0, n_col - 1)
        flags_out[pl.ds(i, 1), :] = flags[pl.ds(at, 1), :].astype(f32)


def source_at(b, q):
    return SRC + (q - 4 if b == 0 else q)


def stack_up(base, mr, ml, stack, to_low, to_high):
    lane = lanes((B, LZ))
    row = rows((B, LZ))
    for q in range(B):
        stack[PERM + q] = base[q]
        stack[OWN + q] = base[B + q]
        stack[SRC + q] = base[2 * B + q]
    for q in range(B // 2):
        stack[HZ + q] = jnp.where((lane & 63) < 32, mr[q], ml[q])
    at = B // 2
    stack[ASG] = jnp.where(
        row == 1, spread(mr[at, 0:1, :]), jnp.where(row == 2, spread(ml[at, 0:1, :]), base[3 * B])
    )
    for out, first in ((to_low, 0), (to_high, 4)):
        out[0:SRC] = stack[0:SRC]
        for q in range(4):
            out[SRC + q] = base[2 * B + first + q]


def y_messages(low, mid, high, up, down):
    stacks = (low, mid, high)
    row = rows((B, LZ))
    lane = lanes((B, LZ))

    def fold(main, other, n, top, upward):
        if upward:
            return jnp.where((row >= top - n) & (row < top), pltpu.roll(other, top, 0), main)
        return jnp.where(
            (row >= B - top) & (row < B - top + n), pltpu.roll(other, B - top, 0), main
        )

    for out, upward in ((up, True), (down, False)):
        for field, first in ((PERM, M_PERM), (OWN, M_OWN)):
            for at, (main, other, n) in enumerate(FOLDS):
                tile = stacks[main // B][field + main % B]
                if other is not None:
                    tile = fold(tile, stacks[other // B][field + other % B], n, n, upward)
                out[first + at] = tile
        for b in range(3):
            for q in range(B // 2):
                out[M_HZ + 4 * b + q] = stacks[b][HZ + q]
        for at, (main, others) in enumerate(SRC_FOLDS):
            tile = stacks[main // B][source_at(main // B, main % B)]
            for other, n, top in others:
                tile = fold(tile, stacks[other // B][source_at(other // B, other % B)], n, top, upward)
            out[M_SRC + at] = tile
        sides = jnp.where(lane < NSUB, low[ASG], pltpu.roll(high[ASG], NSUB, 1))
        out[M_ASG] = jnp.where(row < 3, sides, pltpu.roll(mid[ASG], 3, 0))


def line_asg(stacks, below, above, ty, b):
    if ty == 1:
        return stacks[b][ASG]
    tile = (below if ty == 0 else above)[M_ASG]
    return (tile, pltpu.roll(tile, 5, 0), pltpu.roll(tile, NSUB, 1))[b]


def around(u_ref, w_ref, p):
    u = u_ref[p + 1]
    return u, (
        (w_ref[0, p] * u_ref[p + 2] + w_ref[1, p] * u_ref[p])
        + (w_ref[2, p] * pltpu.roll(u, NP - 1, 0) + w_ref[3, p] * pltpu.roll(u, 1, 0))
        + (w_ref[4, p] * pltpu.roll(u, 2 * LZ - 1, 1) + w_ref[5, p] * pltpu.roll(u, 1, 1))
    )


def sweeps(both, w_ref, first, last, after=None, operator_at=-1, size=CHUNK):
    def one_sweep(k, carry):
        now = lax.rem(k, 2)
        src, dst = both.at[now], both.at[1 - now]
        count = NP - 2 * k
        keep = jnp.where(k == operator_at, 1.0, 1.0 - fine_relax)
        give = jnp.where(k == operator_at, -1.0 / fine_relax, 1.0)

        def chunk(i, carry):
            start = jnp.minimum(k + size * i, k + count - size)
            moved = []
            for j in range(size):
                u, near = around(src, w_ref, start + j)
                moved.append(keep * u + give * near)
            for j in range(size):
                dst[start + j + 1] = moved[j]
            return carry

        lax.fori_loop(0, (count + size - 1) // size, chunk, 0)
        if after is not None:
            after(k)
        return carry

    lax.fori_loop(first, last + 1, one_sweep, 0)


def own_tile(u_ref, w_ref, p):
    r, z = slice(B, 2 * B), slice(0, LZ)
    u, beyond = u_ref[p + 1, r, z], u_ref[p + 1, r, LZ:]
    lane = lanes((B, LZ))
    right = jnp.where(lane == LZ - 1, pltpu.roll(beyond, LZ - 1, 1), pltpu.roll(u, LZ - 1, 1))
    left = jnp.where(lane == 0, pltpu.roll(beyond, 1, 1), pltpu.roll(u, 1, 1))
    w = [w_ref[i, p, r, z] for i in range(6)]
    near = (
        (w[0] * u_ref[p + 2, r, z] + w[1] * u_ref[p, r, z])
        + (w[2] * u_ref[p + 1, B + 1 : 2 * B + 1, z] + w[3] * u_ref[p + 1, B - 1 : 2 * B - 1, z])
        + (w[4] * right + w[5] * left)
    )
    return (1.0 - fine_relax) * u + near


def label_sums(groups, sums):
    def one(s, carry):
        for first, labels, fields in groups:
            hits = [tile == s for tile in labels]
            for i, tiles in enumerate(fields):
                parts = [jnp.where(hit, tile, 0.0) for hit, tile in zip(hits, tiles)]
                while len(parts) > 1:
                    parts = [a + b for a, b in zip(parts[::2], parts[1::2])]
                sums[pl.ds(first + i * NSUB + s, 1), :] = jnp.sum(parts[0], axis=0, keepdims=True)
        return carry

    lax.fori_loop(0, NSUB, one, 0, unroll=16)


def three_parts(x):
    high = x.astype(bf16).astype(f32)
    rest = x - high
    middle = rest.astype(bf16).astype(f32)
    return high, middle, rest - middle


def lane_sums(sums):
    parts = jnp.concatenate(three_parts(sums), axis=1).astype(bf16)
    total = lax.dot_general(
        jnp.ones((2 * B, 3 * LZ), bf16), parts,
        (((1,), (1,)), ((), ())), preferred_element_type=f32,
    )
    return total[0:B]


def harmonic(a, b):
    return 2.0 * a * b / (a + b)


def row_product(tile):
    for by in (4, 2, 1):
        tile = tile * pltpu.roll(tile, by, 0)
    return tile


def positive(t):
    return jnp.where(t > 0.0, t, 1.0)


def near_and_far(tile, q):
    turned = pltpu.roll(tile, 64, 1)
    return jnp.where(q < 4, tile, turned), jnp.where(q < 4, turned, tile)


def halo_values(near, far):
    lane = lanes((B, LZ))
    near_side = lane < 64
    halo = (lane < W) | (lane >= LZ - W)
    source_halo = (lane < 4) | (lane >= LZ - 4)
    k = positive(jnp.where(halo, jnp.where(near_side, near, far), 1.0))
    own = jnp.where(near_side, pltpu.roll(near, LZ - 9, 1), pltpu.roll(near, 73, 1))
    src = jnp.where(near_side, pltpu.roll(near, LZ - 18, 1), pltpu.roll(near, 82, 1))
    return k, jnp.where(halo, own, 0.0).astype(i32), jnp.where(source_halo, src, 0.0)


def own_rows(low, mid, high, kmid, lmid, smid):
    for p in range(NP):
        stack, q = (low, mid, high)[p // B], p % B
        k, label, src = halo_values(*near_and_far(stack[HZ + q % 4], q))
        kmid[p, :, 0:LZ] = positive(stack[PERM + q])
        kmid[p, :, LZ:] = k
        lmid[p, :, 0:LZ] = stack[OWN + q].astype(i32)
        lmid[p, :, LZ:] = label
        if 4 <= p < 20:
            smid[p - 4, :, 0:LZ] = stack[source_at(p // B, q)]
            smid[p - 4, :, LZ:] = src


def first_sums(n_gx, n_gy, n_col, low, mid, high, below, above, flags, kmid, lmid, smid,
               weights, labels, chunk, dvals, paths, asg, kext, fx, both, masks, sums):
    gx, gy, col = (lax.axis_index(a) for a in ("gx", "gy", "col"))
    mids = (low, mid, high)
    lane = lanes((B, LZ))
    row = rows((B, LZ))
    def unfolded(ty, first, place):
        at, n = place
        tile = (below if ty == 0 else above)[first + at]
        return pltpu.roll(tile, (B - n if ty == 0 else n) % B, 0) if n else tile

    def beyond(ty, p):
        b, q = p // B, lax.rem(p, B)
        tile = (below if ty == 0 else above)[M_HZ + 4 * b + lax.rem(q, 4)]
        return halo_values(*near_and_far(tile, q))

    def fill(p, carry):
        kext[p + 1, B : 2 * B, :] = kmid[p]
        labels[p, B : 2 * B, :] = lmid[p]
        for ty in (0, 2):
            r = slice(ty * B, (ty + 1) * B)
            kext[p + 1, r, LZ:], labels[p, r, LZ:], _ = beyond(ty, p)
        return carry

    lax.fori_loop(0, NP, fill, 0, unroll=12)
    for p in range(NP):
        for ty in (0, 2):
            r = slice(ty * B, (ty + 1) * B)
            kext[p + 1, r, 0:LZ] = positive(unfolded(ty, M_PERM, FOLD_OF[p]))
            labels[p, r, 0:LZ] = unfolded(ty, M_OWN, FOLD_OF[p]).astype(i32)
    for b in range(3):
        for ty in range(3):
            asg[b, ty] = line_asg(mids, below, above, ty, b).astype(i32)
    kext[0] = jnp.ones(FULL, f32)
    kext[NP + 1] = jnp.ones(FULL, f32)

    flag_row = jnp.concatenate(
        [flags[1:2, :], jnp.where(lane[0:1] < 64, flags[2:3, :], flags[0:1, :])], axis=1
    )
    row_all, lane_all = rows(FULL), lanes(FULL)
    wrap_row = jnp.where(gy == 0, B - 1, jnp.where(gy == n_gy - 1, 2 * B - 1, -1))
    masks[0] = jnp.where(row_all == wrap_row, jnp.broadcast_to(flag_row, FULL), 1.0)
    closed = ((lane_all == LZ - 1) & (col == n_col - 1)) | ((lane_all == 2 * LZ - 1) & (col == 0))
    masks[1] = jnp.where(closed, 0.0, 1.0)

    def terms(p, carry):
        b = p // B
        out = ((b == 0) & (gx == 0)) | ((b == 2) & (gx == n_gx - 1))
        k = kext[p + 1]
        fy_up = harmonic(k, pltpu.roll(k, NP - 1, 0)) * masks[0]
        fy_down = pltpu.roll(fy_up, 1, 0)
        fz_right = harmonic(k, pltpu.roll(k, 2 * LZ - 1, 1)) * masks[1]
        fz_left = pltpu.roll(fz_right, 1, 1)
        k_next = kext[p + 2]
        fx_up = jnp.where((p == B - 1) & (gx == 0), k_next, harmonic(k, k_next))
        fx_up = jnp.where((p == 2 * B - 1) & (gx == n_gx - 1), k, fx_up)
        fx_down = carry
        diag = fx_up + fx_down + fy_up + fy_down + fz_right + fz_left
        scale = jnp.where(out, 0.0, fine_relax) / diag
        for i, face in enumerate((fx_up, fx_down, fy_up, fy_down, fz_right, fz_left)):
            weights[i, p] = face * scale
        both[0, p + 1] = scale
        dvals[p] = diag[B : 2 * B, 0:LZ]
        fx[p + 1] = fx_up
        return fx_up

    lax.fori_loop(0, NP, terms, harmonic(kext[0], kext[1]), unroll=8)


    def start(i, carry):
        p = i + B // 2
        over = both[0, p + 1] * (1.0 / fine_relax)
        both[1, p + 1, B : 2 * B, :] = smid[i] * over[B : 2 * B]
        for ty in (0, 2):
            r = slice(ty * B, (ty + 1) * B)
            both[1, p + 1, r, LZ:] = beyond(ty, p)[2] * over[r, LZ:]
        return carry

    lax.fori_loop(0, 2 * B, start, 0, unroll=16)
    for p in range(B // 2, NP - B // 2):
        for ty in (0, 2):
            r = slice(ty * B, (ty + 1) * B)
            if p in SRC_OF:
                over = both[0, p + 1, r, 0:LZ] * (1.0 / fine_relax)
                both[1, p + 1, r, 0:LZ] = unfolded(ty, M_SRC, SRC_OF[p]) * over
            else:
                both[1, p + 1, r, 0:LZ] = jnp.zeros((B, LZ), f32)

    r = slice(B, 2 * B)
    for q in range(B):
        p = B + q
        up, down = weights[2, p, r, 0:LZ], weights[3, p, r, 0:LZ]
        rise = row_product(jnp.where(row == 0, 1.0, down)) * up
        fall = row_product(jnp.where(row == B - 1, 1.0, up)) * down
        per = dvals[p] * (1.0 / fine_relax)
        paths[2, q : q + 1, :] = (rise * per)[B - 1 : B]
        paths[3, q : q + 1, :] = (fall * per)[0:1]
    rise, fall = fx[2 * B, B : 2 * B, 0:LZ], fx[B, B : 2 * B, 0:LZ]
    for p in range(B + 1, 2 * B):
        rise = rise * weights[1, p, B : 2 * B, 0:LZ]
        fall = fall * weights[0, p - 1, B : 2 * B, 0:LZ]
    paths[0] = rise
    paths[1] = fall

    sweeps(both, weights, 5, 7, size=NP - 10)
    tiles = [own_tile(both.at[0], weights, B + q) * dvals[B + q] for q in range(B)]
    diag_tiles = [dvals[B + q] for q in range(B)]
    label_tiles = [labels[B + q, B : 2 * B, 0:LZ] for q in range(B)]
    label_sums([(0, label_tiles, (tiles, diag_tiles))], sums)
    totals = lane_sums(sums[...])

    own = spread(mid[ASG, 0:1, :])
    own = jnp.where(lane < NSUB, own, pltpu.roll(own, NSUB, 1))
    tile = jnp.where(row == 0, totals, own)[0:2]
    for d in range(n_gy * n_col):
        chunk[d] = tile


def one_hot_product(lefts, lows):
    left = jnp.concatenate(lefts, axis=1)
    wide = rows((LZ, LZ))
    right = jnp.concatenate(
        [
            jnp.where(jnp.broadcast_to(low, (LZ, LZ)) == wide, 1.0, 0.0).astype(bf16)
            for low in lows
        ],
        axis=1,
    )
    parts = three_parts(left)
    if left.shape[0] % (2 * B):
        parts += (jnp.zeros_like(left),)
    return lax.dot_general(
        jnp.concatenate(parts, axis=0).astype(bf16), right, (((1,), (1,)), ((), ())),
        preferred_element_type=f32,
    )


def joined(total, n):
    return (total[2 * n : 3 * n] + total[n : 2 * n]) + total[:n]


def halves(value, high):
    lane = lanes((B, LZ))
    scaled = jnp.where(high == rows((B, LZ)), value, 0.0)
    return jnp.concatenate(
        [jnp.where(lane < NSUB, scaled, 0.0), jnp.where(lane < NSUB, 0.0, scaled)], axis=0
    )


GROUP = 64


def first_coarse(n_bricks, n_out, values, out):
    def one(i, total):
        lefts, lows = [], []
        for j in range(min(GROUP, n_bricks)):
            value = values[i * min(GROUP, n_bricks) + j]
            a = value[1:2].astype(i32)
            lefts.append(halves(spread(value[0:1]), spread(a >> 7)))
            lows.append(a & 127)
        return total + one_hot_product(lefts, lows)

    total = lax.fori_loop(0, n_bricks // min(GROUP, n_bricks), one, jnp.zeros((6 * B, LZ), f32))
    total = joined(total, 2 * B)
    for d in range(n_out):
        out[d] = total


def second_coarse(n_gy, n_col, n_out, values, first, out):
    n_bricks = n_gy * n_col
    lane = lanes((B, LZ))
    near = lanes((1, LZ)) < NSUB

    def own(j):
        before = lax.rem(j + n_bricks - n_col, n_bricks)
        after = lax.rem(j + n_col, n_bricks)
        mine = spread(values[j, 0:1] + values[before, 2:3])
        return mine + pltpu.roll(spread(values[after, 2:3]), NSUB, 1)

    def one(i, totals):
        lefts, lows, edge_lefts, edge_lows = [], [], [], []
        for j in range(min(GROUP, n_bricks) // 2):
            at = i * min(GROUP, n_bricks) + 2 * j
            pair = jnp.where(lane < NSUB, own(at), pltpu.roll(own(at + 1), NSUB, 1))
            a = jnp.where(near, first[at, 1:2], first[at + 1, 1:2]).astype(i32)
            lefts.append(jnp.where(spread(a >> 7) == rows((B, LZ)), pair, 0.0))
            lows.append(a & 127)
        for j in range(min(GROUP, n_bricks)):
            a = values[i * min(GROUP, n_bricks) + j, 3:4].astype(i32)
            edge_lefts.append(halves(spread(values[i * min(GROUP, n_bricks) + j, 1:2]), spread(a >> 7)))
            edge_lows.append(a & 127)
        return (
            totals[0] + one_hot_product(lefts, lows),
            totals[1] + one_hot_product(edge_lefts, edge_lows),
        )

    mine, edges = lax.fori_loop(
        0, n_bricks // min(GROUP, n_bricks), one, (jnp.zeros((4 * B, LZ), f32), jnp.zeros((6 * B, LZ), f32))
    )
    total = jnp.concatenate([joined(mine, B), joined(edges, 2 * B)], axis=0)
    for d in range(n_out):
        out[d] = total


def lookup(table, index):
    low, high = index & 127, index >> 7
    result = jnp.zeros((B, LZ), f32)
    for h in range(B):
        got = jnp.take_along_axis(spread(table[h : h + 1]), low, axis=1)
        result = jnp.where(high == h, got, result)
    return result


def pick(row, index):
    return jnp.take_along_axis(spread(row), index, axis=1)


def slab_total(parts, g, n_gx, part, size):
    total = parts[jnp.clip(g, 0, n_gx - 1), part : part + size]
    return jnp.where((g >= 0) & (g < n_gx), total, 0.0)


def guess(parts, g, n_gx):
    total = slab_total(parts, g, n_gx, 0, 2 * B)
    exists = (g >= 0) & (g < n_gx)
    rhs, diag = total[0:B], jnp.where(exists, total[B : 2 * B], 1.0)
    return rhs, diag, coarse_relax * rhs / diag


def expand(coarse, asg, labels, u, tables, first, last):
    near_side = lanes((B, LZ)) < 64

    def table(i, carry):
        b, ty = i // 3, lax.rem(i, 3)
        tables[b, ty] = lookup(coarse[b], asg[b, ty])
        return carry

    lax.fori_loop(0, 9, table, 0, unroll=3)

    def one(p, carry):
        b = p // B
        for ty in range(3):
            r = slice(ty * B, (ty + 1) * B)
            t = tables[b, ty]
            u[p + 1, r, 0:LZ] = pick(t[0:1], labels[p, r, 0:LZ])
            lab = labels[p, r, LZ:]
            u[p + 1, r, LZ:] = jnp.where(near_side, pick(t[1:2], lab), pick(t[2:3], lab))
        return carry

    lax.fori_loop(first, last + 1, one, 0, unroll=8)


def second_sums(n_gx, n_gy, n_col, parts, weights, labels, asg, dvals, paths,
                chunk, both, coarse, tables, ends, sums):
    gx = lax.axis_index("gx")
    row = rows((B, LZ))
    r = slice(B, 2 * B)
    for i in range(3):
        coarse[i] = guess(parts, gx + i - 1, n_gx)[2]
    expand(coarse, asg, labels, both.at[0], tables, 0, NP - 1)

    def after(k):
        @pl.when(k == 0)
        def _():
            first = both.at[1]
            zero = jnp.zeros(FULL, f32)
            first[1] = zero
            first[NP] = zero
            first[:, 0:1, :] = jnp.zeros((NP + 2, 1, 2 * LZ), f32)
            first[:, NP - 1 :, :] = jnp.zeros((NP + 2, 1, 2 * LZ), f32)
            ends[0] = first[B + 1, r, 0:LZ] * -paths[0]
            ends[1] = first[2 * B, r, 0:LZ] * -paths[1]
            for q in range(B):
                plane = first[B + 1 + q, r, 0:LZ]
                ends[2, q : q + 1, :] = plane[0:1] * -paths[2, q : q + 1, :]
                ends[3, q : q + 1, :] = plane[B - 1 : B] * -paths[3, q : q + 1, :]

    sweeps(both, weights, 0, 4, after=after, operator_at=4)
    sweeps(both, weights, 5, 7, size=NP - 10)
    tiles = [own_tile(both.at[0], weights, B + q) * dvals[B + q] for q in range(B)]
    label_tiles = [labels[B + q, r, 0:LZ] for q in range(B)]
    beyond = [labels[2 * B, r, 0:LZ], labels[B - 1, r, 0:LZ]]
    for at in (2 * B, B - 1):
        edge = labels[B, at : at + 1, 0:LZ]
        edge = spread(edge)
        for q in range(1, B):
            edge = jnp.where(row == q, spread(labels[B + q, at : at + 1, 0:LZ]), edge)
        beyond.append(edge)
    groups = [(0, label_tiles, (tiles,))]
    groups += [((2 + i) * NSUB, [beyond[i]], ([ends[i]],)) for i in range(4)]
    sums[NSUB : 2 * NSUB, :] = jnp.zeros((NSUB, LZ), f32)
    label_sums(groups, sums)
    totals = lane_sums(sums[...])
    right, left = (spread(asg[b, 1, 0:1, :].astype(f32)) for b in (2, 0))
    sides = jnp.where(lanes((B, LZ)) < NSUB, right, pltpu.roll(left, NSUB, 1))
    tile = jnp.where(
        row < 2,
        jnp.where(row == 0, totals[:, 0:LZ], totals[:, LZ : 2 * LZ]),
        jnp.where(row == 2, totals[:, 2 * LZ :], sides),
    )[0:4]
    for d in range(n_gy * n_col):
        chunk[d] = tile


def last_sweeps(n_gx, n_gy, n_col, parts, images, weights, labels, asg,
                pressure, coarse_out, both, coarse, tables):
    gx, gy, col = (lax.axis_index(a) for a in ("gx", "gy", "col"))
    for i in range(3):
        g = gx + i - 1
        rhs, diag, start = guess(parts, g, n_gx)
        image = (
            slab_total(images, g, n_gx, 0, B)
            + slab_total(images, g - 1, n_gx, B, B)
            + slab_total(images, g + 1, n_gx, 2 * B, B)
        )
        second = start + coarse_relax * (rhs - image) / diag
        coarse[i] = jnp.where((g >= 0) & (g < n_gx), second, 0.0)
    share = B * LZ // (n_gy * n_col)
    per_row = LZ // share
    mine = gy * n_col + col
    row = coarse[1, pl.ds(mine // per_row, 1), :]
    turned = pltpu.roll(spread(row), lax.rem(LZ - lax.rem(mine, per_row) * share, LZ), 1)
    coarse_out[...] = turned[0:1, 0:share]
    expand(coarse, asg, labels, both.at[1], tables, 4, 19)
    sweeps(both, weights, 5, 7, size=NP - 10)
    for q in range(B):
        pressure[q] = own_tile(both.at[0], weights, B + q)


def steps(count, by, wrap):
    return [
        (i, (i + by) % count) for i in range(count) if wrap or 0 <= i + by < count
    ]


def on_device(n_gx, n_gy, n_col, permeability, source, ownership, assignment, layer_flags):
    n_bricks = n_gy * n_col
    sizes = (n_gx, n_gy, n_col)
    vm = pltpu.VMEM
    fields = vm((2, NP + 2, *FULL), f32)
    plane = (B, B, LZ)

    def send(x, axis, by, wrap=False):
        return lax.ppermute(x, axis, steps(lax.axis_size(axis), by, wrap))

    mr, ml, base, flags = call(
        z_messages,
        [pinned(B // 2 + 1, B, LZ)] * 2 + [pinned(3 * B + 1, B, LZ), pinned(3, LZ)],
        5,
        scratch=[
            vm(plane, f32), vm(plane, f32), vm(plane, i32), vm((1, NSUB), i32),
            vm((n_col, LZ), i32), pltpu.SemaphoreType.DMA((5,)),
        ],
        space=pl.ANY,
        limit=WHOLE_VMEM,
    )(permeability, source, ownership, assignment.reshape(1, NSUB), layer_flags.reshape(n_col, LZ))
    mr, ml = send(mr, "col", -1), send(ml, "col", 1)
    mid, to_low, to_high = call(
        stack_up, [sds(STACK, B, LZ)] + [sds(X_MESSAGE, B, LZ)] * 2, 3
    )(base, mr, ml)
    low, high = send(to_high, "gx", 1), send(to_low, "gx", -1)
    up, down = call(y_messages, [sds(MESSAGE, B, LZ)] * 2, 3)(low, mid, high)
    below, above = send(up, "gy", 1, True), send(down, "gy", -1, True)
    middle = call(
        own_rows,
        [sds(NP, B, 2 * LZ), sds(NP, B, 2 * LZ, dtype=i32), sds(2 * B, B, 2 * LZ)],
        3,
        cost=pl.CostEstimate(flops=1000000, bytes_accessed=1000000, transcendentals=0),
    )(low, mid, high)

    weights, labels, chunk, dvals, paths, asg = call(
        functools.partial(first_sums, *sizes),
        [
            sds(6, NP, *FULL), sds(NP, *FULL, dtype=i32), sds(n_bricks, 2, LZ), sds(NP, B, LZ),
            sds(4, B, LZ), sds(3, 3, B, LZ, dtype=i32),
        ],
        9,
        scratch=[
            vm((NP + 2, *FULL), f32), vm((NP + 1, *FULL), f32), fields, vm((2, *FULL), f32),
            vm((2 * NSUB, LZ), f32),
        ],
    )(low, mid, high, below, above, flags, *middle)
    bricks = lax.all_to_all(chunk, ("gy", "col"), 0, 0, tiled=True)
    parts = call(
        functools.partial(first_coarse, n_bricks, n_gx), sds(n_gx, 2 * B, LZ), 1
    )(bricks)
    parts = lax.all_to_all(parts, "gx", 0, 0, tiled=True)
    tables = [vm((3, B, LZ), f32), vm((3, 3, B, LZ), f32)]
    chunk = call(
        functools.partial(second_sums, *sizes),
        sds(n_bricks, 4, LZ),
        6,
        scratch=[fields, *tables, vm((4, B, LZ), f32), vm((6 * NSUB, LZ), f32)],
    )(parts, weights, labels, asg, dvals, paths)
    images = lax.all_to_all(chunk, ("gy", "col"), 0, 0, tiled=True)
    images = call(
        functools.partial(second_coarse, n_gy, n_col, n_gx), sds(n_gx, 3 * B, LZ), 2
    )(images, bricks)
    images = lax.all_to_all(images, "gx", 0, 0, tiled=True)
    return call(
        functools.partial(last_sweeps, *sizes),
        [sds(*plane), sds(1, B * LZ // (n_gy * n_col))],
        5,
        scratch=[fields, *tables],
    )(parts, images, weights, labels, asg)


def solution(mesh):
    placed = (
        P("gx", "gy", "col"),
        P("gx", "gy", "col"),
        P("gx", "gy", "col"),
        P("gx", "gy", "col", None),
        P(),
    )
    sizes = mesh.shape
    return jax.shard_map(
        functools.partial(on_device, sizes["gx"], sizes["gy"], sizes["col"]),
        mesh=mesh,
        in_specs=placed,
        out_specs=(P("gx", "gy", "col"), P("gx", ("gy", "col"))),
        check_vma=False,
    )
```
